32 devices in a mesh: groups: 2 (over y), seq: 4 (over z), mp: 4 (over x, core).
Axes of the slice: x: 2, y: 2, z: 4, core: 2. Of those that a mesh axis runs over, the one named last changes fastest.
Arguments:
- nucleotide_features: bfloat16 [3072, 1536], P(('groups', 'seq')), parts along dimension 0, may hold values from -36 to 36
- location_table: bfloat16 [1536, 1536], P('seq'), may hold values from -6 to 6
- premix_rescaler: float32 [1536], replicated, may hold values from 0.5 to 1.5
- probe_lookup_matrices: bfloat16 [2, 1536, 1024], P(None, None, 'mp'), may hold values from -0.15625 to 0.15625
- payload_projector: bfloat16 [1536, 1536], P(None, 'mp'), may hold values from -0.15625 to 0.15625
- logit_sharpness: float32 [8], P('mp'), may hold values from 8 to 32
- mixing_projector: bfloat16 [1536, 1536], P('mp'), may hold values from -0.15625 to 0.15625
- premlp_rescaler: float32 [1536], replicated, may hold values from 0.5 to 1.5
- widening_matrix: bfloat16 [1536, 3072], P(None, 'mp'), may hold values from -0.15625 to 0.15625
- narrowing_matrix: bfloat16 [3072, 1536], P('mp'), may hold values from -0.109375 to 0.109375
Outputs:
- averaged: float32 [3072, 1536], P(('groups', 'seq'), 'mp'), parts along dimension 0
The draws below stay inside these ranges and needn't reach their ends.
There are 2 independent parts, one for each index of `groups`. The reference program is written for one: setup_inputs(seed, part) draws one part's arguments, and reference() takes and returns one part's arrays. A program takes and returns all parts, laid end to end along the dimension named above; an argument that names none is the same for every part. Nothing has to cross between parts.
All inputs are finite; a program needn't handle non-finite values.
Results may differ from the reference program's by a relative error of at most 0.0033.
Values may be sent and summed in bfloat16 or wider, within the bound.
No kernel may reach another device: no remote copies, remote signals or barrier semaphores. Data moves between devices by JAX's collectives and lax.ppermute only.
A program may use at most 128 MiB of HBM per device.

```python
import math
import jax
import jax.numpy as jnp
from jax import lax

D = 1536
NUM_SUBSPACES = 8
QK = 128
VD = 192
FF = 3072
SEQ_LEN = 1536


def draw_nucleotide_features(key, part):
    key_rows, key_cols, key_base = jax.random.split(key, 3)
    row_scale = jnp.exp(jax.random.uniform(key_rows, (SEQ_LEN, 1), jnp.float32, math.log(0.3), math.log(3.0)))
    col_scale = jnp.exp(jax.random.uniform(key_cols, (1, D), jnp.float32, math.log(0.3), math.log(3.0)))
    payload_vectors = jnp.clip(jax.random.normal(key_base, (SEQ_LEN, D), jnp.float32), -4.0, 4.0)
    return (payload_vectors * row_scale * col_scale).astype(jnp.bfloat16)


def levels(key, dims, pieces, low, largest):
    gain, own = 1.0, jax.random.fold_in(key, 6)
    for dim, blocks in pieces:
        heights = jnp.exp(jax.random.uniform(jax.random.fold_in(own, dim), (blocks,), jnp.float32, low / len(pieces), largest / len(pieces)))
        gain = gain * jnp.repeat(heights, dims[dim] // blocks).reshape([-1 if axis == dim else 1 for axis in range(len(dims))])
    return gain


def gaussian(rng, extent, spread, most, cuts=(), kind=jnp.bfloat16):
    level = levels(rng, extent, cuts, -0.22, 0.18) if cuts else 1.0
    result = jax.random.normal(rng, extent, jnp.float32) * spread * level
    return jnp.minimum(jnp.maximum(result, -most), most).astype(kind)


def setup_inputs(seed: int = 0, part: int = 0) -> dict:
    arg_keys = jax.random.split(jax.random.key(seed), 11)
    part_keys = jax.random.split(jax.random.fold_in(arg_keys[10], part), 11)
    nucleotide_features = draw_nucleotide_features(jax.random.fold_in(jax.random.fold_in(arg_keys[10], part), 71), part)
    location_table = gaussian(arg_keys[1], (SEQ_LEN, D), 1.0, 6.0, ((0, 4),))
    premix_rescaler = jnp.clip(1.0 + 0.1 * jax.random.normal(arg_keys[2], (D,), jnp.float32), 0.5, 1.5)
    probe_lookup_matrices = gaussian(arg_keys[3], (2, D, NUM_SUBSPACES * QK), D ** -0.5, 0.15625, ((2, 4),))
    payload_projector = gaussian(arg_keys[4], (D, NUM_SUBSPACES * VD), D ** -0.5, 0.15625, ((1, 4),))
    logit_sharpness = jnp.clip(jnp.exp(math.log(32.0) - 1.3862944 * jax.random.uniform(arg_keys[5], (NUM_SUBSPACES,), jnp.float32) ** levels(arg_keys[5], (NUM_SUBSPACES,), ((0, 4),), -0.2, 0.2)), 8.0, 32.0)
    mixing_projector = gaussian(arg_keys[6], (NUM_SUBSPACES * VD, D), (NUM_SUBSPACES * VD) ** -0.5, 0.15625, ((0, 4),))
    premlp_rescaler = jnp.clip(1.0 + 0.1 * jax.random.normal(arg_keys[7], (D,), jnp.float32), 0.5, 1.5)
    widening_matrix = gaussian(arg_keys[8], (D, FF), D ** -0.5, 0.15625, ((1, 4),))
    narrowing_matrix = gaussian(arg_keys[9], (FF, D), FF ** -0.5, 0.109375, ((0, 4),))
    return {"nucleotide_features": nucleotide_features, "location_table": location_table, "premix_rescaler": premix_rescaler, "probe_lookup_matrices": probe_lookup_matrices, "payload_projector": payload_projector, "logit_sharpness": logit_sharpness, "mixing_projector": mixing_projector, "premlp_rescaler": premlp_rescaler, "widening_matrix": widening_matrix, "narrowing_matrix": narrowing_matrix}


epsilon = 1e-06

def normalize(payload_vectors):
    return payload_vectors * lax.rsqrt(lax.optimization_barrier(jnp.mean(payload_vectors * payload_vectors, axis=-1, keepdims=True)) + epsilon)

def twin_helix_transformer(running_sum_hidden, premix_rescaler, probe_lookup_matrices, payload_projector, logit_sharpness, mixing_projector, premlp_rescaler, widening_matrix, narrowing_matrix):
    length = running_sum_hidden.shape[0]
    subspace_results = logit_sharpness.shape[0]
    lookup_dimension = probe_lookup_matrices.shape[2] // subspace_results
    value_size = payload_projector.shape[1] // subspace_results
    normed = (normalize(running_sum_hidden) * premix_rescaler).astype(jnp.bfloat16)
    query = jnp.dot(normed, probe_lookup_matrices[0], preferred_element_type=jnp.float32).reshape(length, subspace_results, lookup_dimension)
    keys = jnp.dot(normed, probe_lookup_matrices[1], preferred_element_type=jnp.float32).reshape(length, subspace_results, lookup_dimension)
    probe_unit_vectors = normalize(query).astype(jnp.bfloat16)
    lookup_unit_vectors = normalize(keys).astype(jnp.bfloat16)
    payload_vectors = jnp.dot(normed, payload_projector, preferred_element_type=jnp.float32).astype(jnp.bfloat16).reshape(length, subspace_results, value_size)

    def one_subspace(inputs):
        query_head, key_head, value_head, scale_head = inputs
        scores = jnp.dot(query_head, key_head.T, preferred_element_type=jnp.float32) * (scale_head / lookup_dimension)
        weight_exp = jnp.exp(scores)
        totals = lax.optimization_barrier(jnp.sum(weight_exp, axis=1, keepdims=True))
        numer = jnp.dot(weight_exp.astype(jnp.bfloat16), value_head, preferred_element_type=jnp.float32)
        return (numer / totals).astype(jnp.bfloat16)
    mixed_positions = lax.map(one_subspace, (jnp.transpose(probe_unit_vectors, (1, 0, 2)), jnp.transpose(lookup_unit_vectors, (1, 0, 2)), jnp.transpose(payload_vectors, (1, 0, 2)), logit_sharpness))
    mixed_positions = jnp.transpose(mixed_positions, (1, 0, 2)).reshape(length, subspace_results * value_size)
    middle = running_sum_hidden + jnp.dot(mixed_positions, mixing_projector, preferred_element_type=jnp.float32)
    normed_mid = (normalize(middle) * premlp_rescaler).astype(jnp.bfloat16)
    expanded = jax.nn.gelu(jnp.dot(normed_mid, widening_matrix, preferred_element_type=jnp.float32), approximate=True).astype(jnp.bfloat16)
    return middle + jnp.dot(expanded, narrowing_matrix, preferred_element_type=jnp.float32)

def reference(nucleotide_features, location_table, premix_rescaler, probe_lookup_matrices, payload_projector, logit_sharpness, mixing_projector, premlp_rescaler, widening_matrix, narrowing_matrix):
    reversed_tokens = jnp.flip(nucleotide_features, 0)
    plus_sequence = nucleotide_features.astype(jnp.float32) + location_table.astype(jnp.float32)
    complement_sequence = reversed_tokens.astype(jnp.float32) + location_table.astype(jnp.float32)
    plus_result = twin_helix_transformer(plus_sequence, premix_rescaler, probe_lookup_matrices, payload_projector, logit_sharpness, mixing_projector, premlp_rescaler, widening_matrix, narrowing_matrix)
    complement_result = twin_helix_transformer(complement_sequence, premix_rescaler, probe_lookup_matrices, payload_projector, logit_sharpness, mixing_projector, premlp_rescaler, widening_matrix, narrowing_matrix)
    return 0.5 * (plus_result + jnp.flip(complement_result, 0))
```

```python
import jax
import jax.numpy as jnp
from jax import lax
from jax.sharding import PartitionSpec as P

epsilon = 1e-06


def normalize(payload_vectors):
    return payload_vectors * lax.rsqrt(
        jnp.mean(payload_vectors * payload_vectors, axis=-1, keepdims=True) + epsilon
    )


def flip_rows(rows, tile):
    length, width = rows.shape
    blocks = rows.reshape(length // tile, tile, width)[::-1]
    exchange = jnp.flip(jnp.eye(tile, dtype=rows.dtype), 0)
    flipped = jnp.einsum("ij,njd->nid", exchange, blocks, preferred_element_type=jnp.float32)
    return flipped.reshape(length, width)


def shards(
    nucleotide_features,
    location_table,
    premix_rescaler,
    probe_lookup_matrices,
    payload_projector,
    logit_sharpness,
    mixing_projector,
    premlp_rescaler,
    widening_matrix,
    narrowing_matrix,
):
    f32, bf16 = jnp.float32, jnp.bfloat16
    rows_here, width = nucleotide_features.shape
    heads = logit_sharpness.shape[0]
    lookup = probe_lookup_matrices.shape[2] // heads
    value_size = payload_projector.shape[1] // heads
    groups, seq, mp = (lax.axis_size(name) for name in ("groups", "seq", "mp"))
    here_g, here_s, here_m = (lax.axis_index(name) for name in ("groups", "seq", "mp"))
    length = rows_here * seq
    part = rows_here // mp
    half = width // groups

    x_part = lax.dynamic_slice_in_dim(nucleotide_features, here_m * part, part, 0)
    x_all = lax.all_gather(x_part, ("seq", "mp"), axis=0, tiled=True)
    loc_part = lax.dynamic_slice(location_table, (here_m * part, here_g * half), (part, half))
    loc_all = lax.all_gather(loc_part, ("groups", "seq", "mp"), axis=0, tiled=True)
    loc_all = jnp.concatenate([loc_all[g * length : (g + 1) * length] for g in range(groups)], axis=1)
    mixing_all = lax.all_gather(mixing_projector, "mp", axis=0, tiled=True)

    def chunk(position):
        start = position * rows_here
        mirrored = (seq - 1 - position) * rows_here
        x_f = lax.dynamic_slice_in_dim(x_all, start, rows_here, 0).astype(f32)
        loc_f = lax.dynamic_slice_in_dim(loc_all, start, rows_here, 0).astype(f32)
        loc_back = flip_rows(lax.dynamic_slice_in_dim(loc_all, mirrored, rows_here, 0), 128)
        stream = jnp.stack([x_f + loc_f, x_f + loc_back])
        return stream, (normalize(stream) * premix_rescaler).astype(bf16)

    stream_here, normed_here = chunk(here_s)
    query = jnp.einsum("tsd,de->tse", normed_here, probe_lookup_matrices[0], preferred_element_type=f32)
    query_n = normalize(query.reshape(2, rows_here, heads, lookup)).astype(bf16)
    numer = totals = 0.0
    for position in range(seq):
        normed = chunk(position)[1]
        keys = jnp.einsum("tsd,de->tse", normed, probe_lookup_matrices[1], preferred_element_type=f32)
        key_n = normalize(keys.reshape(2, rows_here, heads, lookup)).astype(bf16)
        value = jnp.einsum("tsd,de->tse", normed, payload_projector, preferred_element_type=f32)
        value = value.astype(bf16).reshape(2, rows_here, heads, value_size)
        scores = jnp.einsum("tqhe,tkhe->thqk", query_n, key_n, preferred_element_type=f32)
        weight_exp = jnp.exp(scores * (logit_sharpness / lookup)[None, :, None, None])
        totals = totals + jnp.sum(weight_exp, axis=-1)
        numer = numer + jnp.einsum("thqk,tkhe->tqhe", weight_exp.astype(bf16), value, preferred_element_type=f32)
    attended = (numer / jnp.transpose(totals, (0, 2, 1))[..., None]).astype(bf16)
    attended = attended.reshape(2, rows_here, heads * value_size)

    attended_all = lax.all_gather(attended, "mp", axis=0)
    mixing_blocks = mixing_all.reshape(mp, heads * value_size, width)
    middle = stream_here + jnp.einsum("mtse,med->tsd", attended_all, mixing_blocks, preferred_element_type=f32)
    normed_mid = (normalize(middle) * premlp_rescaler).astype(bf16)
    expanded = jnp.einsum("tsd,df->tsf", normed_mid, widening_matrix, preferred_element_type=f32)
    expanded = jax.nn.gelu(expanded, approximate=True).astype(bf16)
    share = width // mp
    narrow = narrowing_matrix.reshape(narrowing_matrix.shape[0], mp, share)
    reduced = jnp.einsum("tsf,fmd->msd", expanded, narrow, preferred_element_type=f32)
    reduced = lax.psum_scatter(reduced.astype(bf16), "mp", scatter_dimension=0, tiled=False)
    middle_share = lax.dynamic_slice_in_dim(middle[0] + middle[1], here_m * share, share, 1)
    return 0.5 * (middle_share + reduced.astype(f32))


def solution(mesh):
    return jax.shard_map(
        shards,
        mesh=mesh,
        in_specs=(
            P(("groups", "seq"), None),
            P("seq", None),
            P(),
            P(None, None, "mp"),
            P(None, "mp"),
            P("mp"),
            P("mp", None),
            P(),
            P(None, "mp"),
            P("mp", None),
        ),
        out_specs=P(("groups", "seq"), "mp"),
        check_vma=False,
    )
```

```python
import functools

import jax
import jax.numpy as jnp
from jax import lax
from jax.experimental import pallas as pl
from jax.experimental.pallas import tpu as pltpu
from jax.sharding import PartitionSpec as P

epsilon = 1e-06
f32, bf16 = jnp.float32, jnp.bfloat16
AXES = ("groups", "seq", "mp")


def swap(block, g=0, s=0, m=0):
    groups, seq, mp = (lax.axis_size(name) for name in AXES)
    code = (g * seq + s) * mp + m
    return lax.ppermute(block, AXES, [(i, i ^ code) for i in range(groups * seq * mp)])


def unit(block):
    return block * lax.rsqrt(jnp.mean(block * block, axis=-1, keepdims=True) + epsilon)


def dot(a, b):
    return jnp.dot(a, b, preferred_element_type=f32)


def chunk_kernel(kind, last, dims, scal, *refs):
    groups, mp, heads, lookup, value_size, padded = dims
    nx = mp // 2
    refs = list(refs)
    take = lambda n: [refs.pop(0) for _ in range(n)]
    own = kind == "own"
    x_refs = take(1) if own else take(2)
    fwd_refs = take(1) if own else take(2)
    back_refs = take(1) if kind == "far" else take(2)
    flip_ref, gain_ref, sharp_ref, wk_ref, wv_ref = take(5)
    (wq_ref,) = take(1) if own else (None,)
    q_ref, numer_in = (None, None) if own else take(2)
    if own:
        numer_out, q_ref, back_out = take(3)
    elif last:
        (attended_out,) = take(1)
    else:
        (numer_out,) = take(1)
    (normed,) = take(1)
    here_m, here_g = scal[0], scal[1]

    def x_piece(k):
        return x_refs[0][here_m ^ k] if own else x_refs[k & 1][k >> 1]

    def loc_piece(some, k):
        if len(some) == 1:
            return some[0][here_m ^ k]
        return jnp.concatenate([some[k & 1][(h ^ here_g) * nx + (k >> 1), 0] for h in range(groups)], axis=1)

    gain = gain_ref[...]
    for k in range(mp):
        x_f = x_piece(k).astype(f32)
        back = dot(flip_ref[...], loc_piece(back_refs, k ^ (mp - 1)))
        place = here_m ^ k if own else k
        if own:
            back_out[place] = back.astype(bf16)
        for t, loc in enumerate((loc_piece(fwd_refs, k).astype(f32), back)):
            normed[t, place] = (unit(x_f + loc) * gain).astype(bf16)
    rows = normed[...].reshape(-1, normed.shape[-1])
    length = rows.shape[0] // 2
    if own:
        query = dot(rows, wq_ref[...])
        for h in range(heads):
            cols = slice(h * lookup, (h + 1) * lookup)
            q_ref[:, cols] = unit(query[:, cols]).astype(bf16)
    keys = dot(rows, wk_ref[...])
    value = dot(rows, wv_ref[...])
    column = lax.broadcasted_iota(jnp.int32, value.shape, 1) % padded
    value = jnp.where(column == value_size, 1.0, value).astype(bf16)
    for t in range(2):
        mine = slice(t * length, (t + 1) * length)
        attended = []
        for h in range(heads):
            cols = slice(h * lookup, (h + 1) * lookup)
            key_n = unit(keys[mine, cols]).astype(bf16)
            scores = lax.dot_general(
                q_ref[mine, cols], key_n, (((1,), (1,)), ((), ())), preferred_element_type=f32
            )
            weight = jnp.exp(scores * (sharp_ref[h] / lookup)).astype(bf16)
            numer = dot(weight, value[mine, h * padded : (h + 1) * padded])
            if not own:
                numer = numer + numer_in[t, h]
            if last:
                attended.append(numer[:, :value_size] / numer[:, value_size : value_size + 1])
            else:
                numer_out[t, h] = numer
        if last:
            attended_out[t] = jnp.concatenate(attended, axis=1).astype(bf16)


def whole(array):
    return pl.BlockSpec(array.shape, lambda i, scal: (0,) * array.ndim)


def chunk_call(kind, last, dims, scal, x_parts, fwd_parts, back_parts, flip, gain, sharp, wk, wv, wq, q, numer):
    groups, mp, heads, lookup, value_size, padded = dims
    own = kind == "own"
    part, width = x_parts[0].shape[-2:]
    rows = part * mp

    def piece(which):
        return lambda a: pl.BlockSpec((a.shape[0], 1) + a.shape[2:], lambda i, scal: (0, scal[which], 0, 0))

    args, specs = [], []

    def add(arrays, spec):
        for a in arrays:
            args.append(a)
            specs.append(spec(a))

    add(x_parts, whole)
    add(fwd_parts, whole if own else piece(2))
    add(back_parts, whole if kind == "far" else piece(3))
    add([flip, gain], whole)
    add([sharp], lambda a: pl.BlockSpec(memory_space=pltpu.SMEM))
    add([wk, wv] + ([wq] if own else [q, numer]), whole)
    numer_shape = jax.ShapeDtypeStruct((2, heads, rows, padded), f32)
    if own:
        outs = [
            numer_shape,
            jax.ShapeDtypeStruct((2 * rows, heads * lookup), bf16),
            jax.ShapeDtypeStruct((mp, part, width), bf16),
        ]
    elif last:
        outs = [jax.ShapeDtypeStruct((2, rows, heads * value_size), bf16)]
    else:
        outs = [numer_shape]
    flops = 2 * 2 * rows * (width * (heads * (lookup + padded)) + heads * rows * (lookup + padded))
    return pl.pallas_call(
        functools.partial(chunk_kernel, kind, last, dims),
        out_shape=outs,
        grid_spec=pltpu.PrefetchScalarGridSpec(
            num_scalar_prefetch=1,
            grid=(1,),
            in_specs=specs,
            out_specs=[whole(o) for o in outs],
            scratch_shapes=[pltpu.VMEM((2, mp, part, width), bf16)],
        ),
        compiler_params=pltpu.CompilerParams(vmem_limit_bytes=56 * 2**20),
        cost_estimate=pl.CostEstimate(flops=flops, bytes_accessed=12 * 2**20, transcendentals=2 * heads * rows * rows),
        name="chunk_" + kind + ("_last" if last else ""),
    )(scal, *args)


def mid_kernel(dims, scal, *refs):
    mp, share = dims
    att = refs[:mp]
    x_ref, loc_ref, back_ref, wo_ref, gain_ref, w1_ref, w2_ref, even_out, odd_out, middle_out, summed = refs[mp:]
    here_m = scal[0]
    middles, expanded = [], []
    for t, loc in enumerate((loc_ref, back_ref)):
        middle = x_ref[...].astype(f32) + loc[...].astype(f32)
        for k in range(mp):
            middle = middle + dot(att[k][t], wo_ref[here_m ^ k])
        middles.append(middle)
        normed = (unit(middle) * gain_ref[...]).astype(bf16)
        expanded.append(jax.nn.gelu(dot(normed, w1_ref[...]), approximate=True).astype(bf16))
    both = middles[0] + middles[1]
    out = dot(expanded[0], w2_ref[...]) + dot(expanded[1], w2_ref[...])
    for j in range(mp):
        cols = slice(j * share, (j + 1) * share)
        summed[j] = out[:, cols]
        middle_out_part = both[:, cols]

        @pl.when(here_m == j)
        def _():
            middle_out[...] = middle_out_part

    for k in range(mp):
        block = summed[here_m ^ k].astype(bf16)
        if k & 1:
            odd_out[k >> 1] = block
        else:
            even_out[k >> 1] = block


def mid_call(scal, att, x, loc, back, wo, gain, w1, w2):
    mp = len(att)
    rows, width = x.shape
    share = width // mp
    args = list(att) + [x, loc, back, wo, gain, w1, w2]
    outs = [
        jax.ShapeDtypeStruct((mp // 2, rows, share), bf16),
        jax.ShapeDtypeStruct((mp // 2, rows, share), bf16),
        jax.ShapeDtypeStruct((rows, share), f32),
    ]
    flops = 2 * 2 * rows * width * (width + 2 * w1.shape[1])
    return pl.pallas_call(
        functools.partial(mid_kernel, (mp, share)),
        out_shape=outs,
        grid_spec=pltpu.PrefetchScalarGridSpec(
            num_scalar_prefetch=1,
            grid=(1,),
            in_specs=[whole(a) for a in args],
            out_specs=[whole(o) for o in outs],
            scratch_shapes=[pltpu.VMEM((mp, rows, share), f32)],
        ),
        compiler_params=pltpu.CompilerParams(vmem_limit_bytes=56 * 2**20),
        cost_estimate=pl.CostEstimate(flops=flops, bytes_accessed=16 * 2**20, transcendentals=2 * rows * w1.shape[1]),
        name="middle",
    )(scal, *args)


def shards(
    nucleotide_features,
    location_table,
    premix_rescaler,
    probe_lookup_matrices,
    payload_projector,
    logit_sharpness,
    mixing_projector,
    premlp_rescaler,
    widening_matrix,
    narrowing_matrix,
):
    rows, width = nucleotide_features.shape
    heads = logit_sharpness.shape[0]
    lookup = probe_lookup_matrices.shape[2] // heads
    value_size = payload_projector.shape[1] // heads
    padded = (value_size // 128 + 1) * 128
    groups, seq, mp = (lax.axis_size(name) for name in AXES)
    here_g, here_m = lax.axis_index("groups"), lax.axis_index("mp")
    nx = mp // 2
    part, half = rows // mp, width // groups
    dims = (groups, mp, heads, lookup, value_size, padded)

    x_own = nucleotide_features.reshape(mp, part, width)
    loc_own = location_table.reshape(mp, part, width)

    loc_part = lax.dynamic_slice(location_table, (here_m * part, here_g * half), (part, half))
    loc_far = jnp.stack([swap(loc_part, s=r) for r in range(1, seq)])
    loc_even = jnp.stack(
        [loc_far if h == 0 and kx == 0 else swap(loc_far, g=h, m=2 * kx) for h in range(groups) for kx in range(nx)]
    )
    loc_odd = swap(loc_even, m=1)
    loc_parts = [loc_even, loc_odd]

    x_near = jnp.stack([lax.dynamic_index_in_dim(x_own, here_m ^ (2 * kx), 0, False) for kx in range(nx)])
    x_even = {1: swap(x_near, s=1)}
    for r in range(seq - 1, 1, -1):
        arrived = swap(x_near[0], s=r)
        x_even[r] = jnp.stack([arrived] + [swap(arrived, m=2 * kx) for kx in range(1, nx)])
    x_parts = {r: [x_even[r], swap(x_even[r], m=1)] for r in x_even}

    mixing_all = lax.all_gather(mixing_projector, "mp", axis=0)

    flip = jnp.flip(jnp.eye(part, dtype=bf16), 0)
    gain = premix_rescaler.reshape(1, width)
    wq, wk = probe_lookup_matrices[0], probe_lookup_matrices[1]
    wv = jnp.pad(payload_projector.reshape(width, heads, value_size), ((0, 0), (0, 0), (0, padded - value_size)))
    wv = wv.reshape(width, heads * padded)
    common = (flip, gain, logit_sharpness, wk, wv)

    def scalars(r):
        return jnp.stack([here_m, here_g, jnp.int32(max(r - 1, 0)), jnp.int32(max((r ^ (seq - 1)) - 1, 0))]).astype(
            jnp.int32
        )

    numer, q, back = chunk_call(
        "own", False, dims, scalars(0), [x_own], [loc_own], loc_parts, *common, wq, None, None
    )
    order = [seq - 1] + list(range(1, seq - 1))
    for r in order:
        kind = "far" if r == seq - 1 else "near"
        back_parts = [loc_own] if kind == "far" else loc_parts
        (numer,) = chunk_call(
            kind, r == order[-1], dims, scalars(r), x_parts[r], loc_parts, back_parts, *common, None, q, numer
        )
    attended = numer

    attended_even = [attended] + [swap(attended, m=2 * kx) for kx in range(1, nx)]
    attended_odd = [swap(a, m=1) for a in attended_even]
    pieces = [(attended_odd if k & 1 else attended_even)[k >> 1] for k in range(mp)]
    even, odd, middle_share = mid_call(
        scalars(0),
        pieces,
        nucleotide_features,
        location_table,
        back.reshape(rows, width),
        mixing_all,
        premlp_rescaler.reshape(1, width),
        widening_matrix,
        narrowing_matrix,
    )
    paired = even.astype(f32) + swap(odd, m=1).astype(f32)
    total = middle_share + paired[0]
    for kx in range(1, nx):
        total = total + swap(paired[kx].astype(bf16), m=2 * kx).astype(f32)
    return 0.5 * total


def solution(mesh):
    return jax.shard_map(
        shards,
        mesh=mesh,
        in_specs=(
            P(("groups", "seq"), None),
            P("seq", None),
            P(),
            P(None, None, "mp"),
            P(None, "mp"),
            P("mp"),
            P("mp", None),
            P(),
            P(None, "mp"),
            P("mp", None),
        ),
        out_specs=P(("groups", "seq"), "mp"),
        check_vma=False,
    )
```

```python
import functools

import jax
import jax.numpy as jnp
from jax import lax
from jax.experimental import pallas as pl
from jax.experimental.pallas import tpu as pltpu
from jax.sharding import PartitionSpec as P

epsilon = 1e-06
f32, bf16 = jnp.float32, jnp.bfloat16
AXES = ("groups", "seq", "mp")


def swap(block, g=0, s=0, m=0):
    groups, seq, mp = (lax.axis_size(name) for name in AXES)
    code = (g * seq + s) * mp + m
    return lax.ppermute(block, AXES, [(i, i ^ code) for i in range(groups * seq * mp)])


def unit(block):
    return block * lax.rsqrt(jnp.mean(block * block, axis=-1, keepdims=True) + epsilon)


def dot(a, b):
    return jnp.dot(a, b, preferred_element_type=f32)


def chunk_kernel(dims, pieces, strands, own, last, n_x, scal, *refs):
    groups, seq, mp, heads, lookup, value_size, padded = dims
    nx = mp // 2
    refs = list(refs)
    take = lambda n: [refs.pop(0) for _ in range(n)]
    x_refs = take(n_x)
    (own_loc,) = take(1)
    loc_refs = take(0 if own and strands == (0,) else 2)
    flip_ref, gain_ref, sharp_ref, wk_ref, wv_ref = take(5)
    wq_ref = take(1)[0] if own else None
    q_refs = [] if own else take(len(strands))
    numer_in = [] if own else take(len(strands))
    out_refs = take(len(strands))
    if own:
        q_refs = take(1)
        back_out = take(1)[0] if 1 in strands else None
    halves = refs
    here_m, here_g = scal[0], scal[1]
    x_places = [(ref, i) for ref in x_refs for i in range(ref.shape[0])]
    part = own_loc.shape[1]
    length = mp * part
    per_half = mp // len(halves)

    def loc_piece(r, k):
        if r == 0:
            return own_loc[here_m ^ k]
        some = loc_refs[k & 1]
        return jnp.concatenate([some[(h ^ here_g) * nx + (k >> 1), r - 1] for h in range(groups)], axis=1)

    gain = gain_ref[...]
    keys, value = [], []
    for n, normed in enumerate(halves):
        for i in range(per_half):
            r, k = pieces[n * per_half + i]
            if own:
                x_f = x_refs[0][here_m ^ k].astype(f32)
            else:
                ref, at = x_places[n * per_half + i]
                x_f = ref[at].astype(f32)
            place = here_m ^ k if own else i
            for p, t in enumerate(strands):
                if t == 0:
                    loc = loc_piece(r, k).astype(f32)
                else:
                    loc = dot(flip_ref[...], loc_piece(r ^ (seq - 1), k ^ (mp - 1)))
                    if own:
                        back_out[place] = loc.astype(bf16)
                normed[p, place] = (unit(x_f + loc) * gain).astype(bf16)
        rows = normed[...].reshape(-1, normed.shape[-1])
        if own:
            query = dot(rows, wq_ref[...])
            for h in range(heads):
                cols = slice(h * lookup, (h + 1) * lookup)
                q_refs[0][:, cols] = unit(query[:, cols]).astype(bf16)
        keys.append(dot(rows, wk_ref[...]))
        v = dot(rows, wv_ref[...])
        column = lax.broadcasted_iota(jnp.int32, v.shape, 1) % padded
        value.append(jnp.where(column == value_size, 1.0, v).astype(bf16))
    some = per_half * part
    for p in range(len(strands)):
        mine = slice(p * some, (p + 1) * some)
        attended = []
        for h in range(heads):
            cols = slice(h * lookup, (h + 1) * lookup)
            key_n = jnp.concatenate([unit(k[mine, cols]).astype(bf16) for k in keys], axis=0)
            value_h = jnp.concatenate([v[mine, h * padded : (h + 1) * padded] for v in value], axis=0)
            scores = lax.dot_general(
                q_refs[p][:, cols], key_n, (((1,), (1,)), ((), ())), preferred_element_type=f32
            )
            weight = jnp.exp(scores * (sharp_ref[h] / lookup)).astype(bf16)
            numer = dot(weight, value_h)
            if not own:
                numer = numer + numer_in[p][h]
            if last:
                attended.append(numer[:, :value_size] / numer[:, value_size : value_size + 1])
            else:
                out_refs[p][h] = numer
        if last:
            out_refs[p][...] = jnp.concatenate(attended, axis=1).astype(bf16)


VMEM = pl.BlockSpec(memory_space=pltpu.VMEM)
SMEM = pl.BlockSpec(memory_space=pltpu.SMEM)


def chunk_call(name, dims, pieces, strands, own, last, scal, x_parts, own_loc, loc_parts, flip, gain, sharp, weights, q, numer):
    groups, seq, mp, heads, lookup, value_size, padded = dims
    _, part, width = own_loc.shape
    rows = part * mp
    args = list(x_parts) + [own_loc] + list(loc_parts) + [flip, gain, sharp] + list(weights) + list(q) + list(numer)
    specs = [SMEM if a is sharp else VMEM for a in args]
    if last:
        outs = [jax.ShapeDtypeStruct((rows, heads * value_size), bf16)] * len(strands)
    else:
        outs = [jax.ShapeDtypeStruct((heads, rows, padded), f32)] * len(strands)
    if own:
        outs = outs + [jax.ShapeDtypeStruct((rows, heads * lookup), bf16)]
        if 1 in strands:
            outs = outs + [jax.ShapeDtypeStruct((mp, part, width), bf16)]
    n_halves = 1 if own else 2
    flops = 2 * len(strands) * rows * (width * (heads * (lookup + padded)) + heads * rows * (lookup + padded))
    return pl.pallas_call(
        functools.partial(chunk_kernel, dims, pieces, strands, own, last, len(x_parts)),
        out_shape=outs,
        in_specs=[SMEM] + specs,
        out_specs=[VMEM] * len(outs),
        scratch_shapes=[pltpu.VMEM((len(strands), mp // n_halves, part, width), bf16)] * n_halves,
        compiler_params=pltpu.CompilerParams(vmem_limit_bytes=40 * 2**20),
        cost_estimate=pl.CostEstimate(
            flops=flops, bytes_accessed=10 * 2**20, transcendentals=len(strands) * heads * rows * rows
        ),
        name=name,
    )(scal, *args)


def mid_kernel(last, mp, groups, scal, *refs):
    refs = list(refs)
    take = lambda n: [refs.pop(0) for _ in range(n)]
    att = take(mp)
    wo = take(mp)
    x_ref, loc_ref, gain_ref, w1_ref, w2_ref = take(5)
    here_m, here_g = scal[0], scal[1]
    middle = x_ref[...].astype(f32) + loc_ref[...].astype(f32)
    for k in range(mp):
        if len(wo[k].shape) == 2:
            middle = middle + dot(att[k][...], wo[k][...])
        else:
            a = att[k][...]
            middle = middle + jnp.concatenate([dot(a, wo[k][here_g ^ h]) for h in range(groups)], axis=1)
    normed = (unit(middle) * gain_ref[...]).astype(bf16)
    expanded = jax.nn.gelu(dot(normed, w1_ref[...]), approximate=True).astype(bf16)
    out = dot(expanded, w2_ref[...])
    share = out.shape[1] // mp
    if not last:
        out_ref, middle_out = take(2)
        out_ref[...] = out
    else:
        out_in, middle_in, even_out, odd_out, middle_out, summed = take(6)
        out = out + out_in[...]
        for j in range(mp):
            summed[j] = out[:, j * share : (j + 1) * share].astype(bf16)
        for k in range(mp):
            (odd_out if k & 1 else even_out)[k >> 1] = summed[here_m ^ k]
    for j in range(mp):
        block = middle[:, j * share : (j + 1) * share]

        @pl.when(here_m == j)
        def _():
            middle_out[...] = block + middle_in[...] if last else block


def mid_call(name, last, groups, scal, att, wo, x, loc, gain, w1, w2, before):
    mp = len(att)
    rows, width = x.shape
    share = width // mp
    args = list(att) + list(wo) + [x, loc, gain, w1, w2] + list(before)
    if last:
        outs = [jax.ShapeDtypeStruct((mp // 2, rows, share), bf16)] * 2
    else:
        outs = [jax.ShapeDtypeStruct((rows, width), f32)]
    outs = outs + [jax.ShapeDtypeStruct((rows, share), f32)]
    return pl.pallas_call(
        functools.partial(mid_kernel, last, mp, groups),
        out_shape=outs,
        in_specs=[SMEM] + [VMEM] * len(args),
        out_specs=[VMEM] * len(outs),
        scratch_shapes=[pltpu.VMEM((mp, rows, share), bf16)] if last else [],
        compiler_params=pltpu.CompilerParams(vmem_limit_bytes=40 * 2**20),
        cost_estimate=pl.CostEstimate(
            flops=2 * rows * width * (width + 2 * w1.shape[1]),
            bytes_accessed=14 * 2**20,
            transcendentals=rows * w1.shape[1],
        ),
        name=name,
    )(scal, *args)


def together(*arrays):
    return lax.optimization_barrier(arrays)


def shards(
    nucleotide_features,
    location_table,
    premix_rescaler,
    probe_lookup_matrices,
    payload_projector,
    logit_sharpness,
    mixing_projector,
    premlp_rescaler,
    widening_matrix,
    narrowing_matrix,
):
    rows, width = nucleotide_features.shape
    heads = logit_sharpness.shape[0]
    lookup = probe_lookup_matrices.shape[2] // heads
    value_size = payload_projector.shape[1] // heads
    padded = (value_size // 128 + 1) * 128
    groups, seq, mp = (lax.axis_size(name) for name in AXES)
    here_g, here_m = lax.axis_index("groups"), lax.axis_index("mp")
    nx = mp // 2
    part, half = rows // mp, width // groups
    dims = (groups, seq, mp, heads, lookup, value_size, padded)
    scal = jnp.stack([here_m, here_g]).astype(jnp.int32)
    x_own = nucleotide_features.reshape(mp, part, width)
    loc_own = location_table.reshape(mp, part, width)

    flip = jnp.flip(jnp.eye(part, dtype=bf16), 0)
    gain = premix_rescaler.reshape(1, width)
    wq, wk = probe_lookup_matrices[0], probe_lookup_matrices[1]
    wv = jnp.pad(payload_projector.reshape(width, heads, value_size), ((0, 0), (0, 0), (0, padded - value_size)))
    wv = wv.reshape(width, heads * padded)

    def chunk(name, pieces, strands, own, last, x_parts, loc_parts, q=(), numer=()):
        weights = (wk, wv, wq) if own else (wk, wv)
        return chunk_call(
            name, dims, tuple(pieces), strands, own, last, scal, x_parts, loc_own, loc_parts,
            flip, gain, logit_sharpness, weights, q, numer,
        )

    loc_part = lax.dynamic_slice(location_table, (here_m * part, here_g * half), (part, half))
    loc_z = [swap(loc_part, s=r) for r in range(1, seq)]
    mix_part = lax.dynamic_slice_in_dim(mixing_projector, here_g * half, half, 1)
    mix_x = [swap(mix_part, m=2 * kx) for kx in range(1, nx)]
    x_near = jnp.stack([lax.dynamic_index_in_dim(x_own, here_m ^ (2 * kx), 0, False) for kx in range(nx)])
    own_pieces = [(0, k) for k in range(mp)]
    numer0, q0 = chunk("own_forward", own_pieces, (0,), True, False, [x_own], [])

    x_near, *held = together(x_near, *loc_z, *mix_x)
    loc_z, mix_x = held[: seq - 1], held[seq - 1 :]
    loc_far = jnp.stack(loc_z)
    x_z = [swap(x_near, s=1)] + [swap(x_near[0], s=r) for r in range(2, seq)]
    combos = [(h, kx) for h in range(groups) for kx in range(nx)]
    loc_xy = [swap(loc_far, g=h, m=2 * kx) for h, kx in combos if (h, kx) != (0, 0)]

    numer0, q0, *held = together(numer0, q0, *x_z, loc_far, *loc_xy, *mix_x)
    x_z, loc_far, loc_xy, mix_x = held[: seq - 1], held[seq - 1], held[seq : seq + len(combos) - 1], held[seq + len(combos) - 1 :]
    pairs = [(r, r + 1) for r in range(2, seq, 2)]
    even = {pair: [jnp.stack([x_z[r - 1] for r in pair])] for pair in pairs}
    for pair in pairs:
        even[pair] += [swap(even[pair][0], m=2 * kx) for kx in range(1, nx)]
    loc_even = jnp.stack([loc_far, *loc_xy])
    loc_parts = [loc_even, swap(loc_even, m=1)]
    near = [x_z[0], swap(x_z[0], m=1)]
    odd_first = {pair: swap(even[pair][0], m=1) for pair in pairs}
    mix_even = [mixing_projector] + [jnp.stack([a] + [swap(a, g=h) for h in range(1, groups)]) for a in mix_x]

    numer1, q1, back = chunk("own_back", own_pieces, (1,), True, False, [x_own], loc_parts)
    q, numer = [q0, q1], [numer0, numer1]
    near_pieces = [(1, 2 * kx) for kx in range(nx)] + [(1, 2 * kx + 1) for kx in range(nx)]
    numer = chunk("near", near_pieces, (0, 1), False, False, near, loc_parts, q, numer)

    for n, pair in enumerate(pairs):
        pieces = [(r, 2 * kx) for kx in range(nx) for r in pair]
        numer = chunk("even", pieces, (0, 1), False, False, even[pair], loc_parts, q, numer)
        odd = [odd_first[pair]] + [swap(a, m=1) for a in even[pair][1:]]
        pieces = [(r, k + 1) for r, k in pieces]
        if n < len(pairs) - 1:
            numer = chunk("odd", pieces, (0, 1), False, False, odd, loc_parts, q, numer)
    attended = []
    for t in range(2):
        (a,) = chunk("odd_last", pieces, (t,), False, True, odd, loc_parts, q[t : t + 1], numer[t : t + 1])
        attended.append(a)
    mix = [mix_even[k >> 1] if k % 2 == 0 else swap(mix_even[k >> 1], m=1) for k in range(mp)]

    before = ()
    for t in range(2):
        a_even = [attended[t]] + [swap(attended[t], m=2 * kx) for kx in range(1, nx)]
        a_odd = [swap(a, m=1) for a in a_even]
        att = [(a_odd if k & 1 else a_even)[k >> 1] for k in range(mp)]
        loc = location_table if t == 0 else back.reshape(rows, width)
        before = mid_call(
            "middle", t == 1, groups, scal, att, mix, nucleotide_features, loc,
            premlp_rescaler.reshape(1, width), widening_matrix, narrowing_matrix, before,
        )
    even_out, odd_out, middle_share = before
    paired = even_out.astype(f32) + swap(odd_out, m=1).astype(f32)
    total = middle_share + paired[0]
    for kx in range(1, nx):
        total = total + swap(paired[kx].astype(bf16), m=2 * kx).astype(f32)
    return 0.5 * total


def solution(mesh):
    return jax.shard_map(
        shards,
        mesh=mesh,
        in_specs=(
            P(("groups", "seq"), None),
            P("seq", None),
            P(),
            P(None, None, "mp"),
            P(None, "mp"),
            P("mp"),
            P("mp", None),
            P(),
            P(None, "mp"),
            P("mp", None),
        ),
        out_specs=P(("groups", "seq"), "mp"),
        check_vma=False,
    )
```

```python
import functools

import jax
import jax.numpy as jnp
from jax import lax
from jax.experimental import pallas as pl
from jax.experimental.pallas import tpu as pltpu
from jax.sharding import PartitionSpec as P

epsilon = 1e-06
f32, bf16 = jnp.float32, jnp.bfloat16
AXES = ("groups", "seq", "mp")


def swap(block, g=0, s=0, m=0):
    groups, seq, mp = (lax.axis_size(name) for name in AXES)
    code = (g * seq + s) * mp + m
    return lax.ppermute(block, AXES, [(i, i ^ code) for i in range(groups * seq * mp)])


def unit(block):
    return block * lax.rsqrt(jnp.mean(block * block, axis=-1, keepdims=True) + epsilon)


def dot(a, b):
    return jnp.dot(a, b, preferred_element_type=f32)


def chunk_kernel(dims, pieces, strands, own, last, n_x, scal, *refs):
    groups, seq, mp, heads, lookup, value_size, padded = dims
    nx = mp // 2
    refs = list(refs)
    take = lambda n: [refs.pop(0) for _ in range(n)]
    x_refs = take(n_x)
    (own_loc,) = take(1)
    n_loc = 0 if own and strands == (0,) else 1
    loc_refs = (take(n_loc), take(n_loc))
    flip_ref, gain_ref, sharp_ref, wk_ref, wv_ref = take(5)
    wq_ref = take(1)[0] if own else None
    q_refs = [] if own else take(len(strands))
    numer_in = [] if own else take(len(strands))
    out_refs = take(2 if last else len(strands))
    if own:
        q_refs = take(1)
        back_out = take(1)[0] if 1 in strands else None
    halves = refs
    here_m, here_g = scal[0], scal[1]
    x_places = [(ref, i) for ref in x_refs for i in range(ref.shape[0])]
    part = own_loc.shape[1]
    length = mp * part
    per_half = len(pieces) // len(halves)
    splits = len(out_refs) if last else 1

    width = own_loc.shape[2]
    half = width // groups
    columns = [pl.ds(pl.multiple_of((h ^ here_g) * half, half), half) for h in range(groups)]

    def loc_piece(r, k, h):
        if r == 0:
            return own_loc[here_m ^ k, :, columns[h]]
        return loc_refs[k & 1][0][h * nx + (k >> 1), r - 1]

    keys, value = [], []
    for n, normed in enumerate(halves):
        for i in range(per_half):
            r, k = pieces[n * per_half + i]
            ref, at = (x_refs[0], here_m ^ k) if own else x_places[n * per_half + i]
            place = here_m ^ k if own else i
            for p, t in enumerate(strands):
                stream = []
                for h in range(groups):
                    if t == 0:
                        loc = loc_piece(r, k, h).astype(f32)
                    else:
                        loc = dot(flip_ref[...], loc_piece(r ^ (seq - 1), k ^ (mp - 1), h))
                        if own:
                            back_out[place, :, columns[h]] = loc.astype(bf16)
                    stream.append(ref[at, :, columns[h]].astype(f32) + loc)
                square = sum(jnp.sum(a * a, axis=-1, keepdims=True) for a in stream)
                scale = lax.rsqrt(square / width + epsilon)
                for h in range(groups):
                    normed[p, place, :, columns[h]] = (stream[h] * scale * gain_ref[:, columns[h]]).astype(bf16)
        rows = normed[...].reshape(-1, normed.shape[-1])
        if own:
            query = dot(rows, wq_ref[...])
            for h in range(heads):
                cols = slice(h * lookup, (h + 1) * lookup)
                q_refs[0][:, cols] = unit(query[:, cols]).astype(bf16)
        keys.append(dot(rows, wk_ref[...]))
        v = dot(rows, wv_ref[...])
        column = lax.broadcasted_iota(jnp.int32, v.shape, 1) % padded
        value.append(jnp.where(column == value_size, 1.0, v).astype(bf16))
    some = per_half * part
    for p in range(len(strands)):
        mine = slice(p * some, (p + 1) * some)
        attended = []
        for h in range(heads):
            cols = slice(h * lookup, (h + 1) * lookup)
            key_n = jnp.concatenate([unit(k[mine, cols]).astype(bf16) for k in keys], axis=0)
            value_h = jnp.concatenate([v[mine, h * padded : (h + 1) * padded] for v in value], axis=0)
            scores = lax.dot_general(
                q_refs[p][:, cols], key_n, (((1,), (1,)), ((), ())), preferred_element_type=f32
            )
            weight = jnp.exp(scores * (sharp_ref[h] / lookup)).astype(bf16)
            numer = dot(weight, value_h)
            if not own:
                numer = numer + numer_in[p][h]
            if last:
                attended.append(numer[:, :value_size] / numer[:, value_size : value_size + 1])
            else:
                out_refs[p][h] = numer
        if last:
            attended = jnp.concatenate(attended, axis=1).astype(bf16)
            block = length // splits
            for i, out_ref in enumerate(out_refs):
                out_ref[p] = attended[i * block : (i + 1) * block]


VMEM = pl.BlockSpec(memory_space=pltpu.VMEM)
SMEM = pl.BlockSpec(memory_space=pltpu.SMEM)


def chunk_call(name, dims, pieces, strands, own, last, scal, x_parts, own_loc, loc_parts, flip, gain, sharp, weights, q, numer):
    groups, seq, mp, heads, lookup, value_size, padded = dims
    _, part, width = own_loc.shape
    rows = part * mp
    args = list(x_parts) + [own_loc] + list(loc_parts) + [flip, gain, sharp] + list(weights) + list(q) + list(numer)
    specs = [SMEM if a is sharp else VMEM for a in args]
    if last:
        outs = [jax.ShapeDtypeStruct((2, rows // 2, heads * value_size), bf16)] * 2
    else:
        outs = [jax.ShapeDtypeStruct((heads, rows, padded), f32)] * len(strands)
    if own:
        outs = outs + [jax.ShapeDtypeStruct((rows, heads * lookup), bf16)]
        if 1 in strands:
            outs = outs + [jax.ShapeDtypeStruct((mp, part, width), bf16)]
    n_halves = 2 if len(pieces) == mp and not own else 1
    new = len(pieces) * part
    flops = 2 * len(strands) * new * (width * (heads * (lookup + padded)) + heads * rows * (lookup + padded))
    return pl.pallas_call(
        functools.partial(chunk_kernel, dims, pieces, strands, own, last, len(x_parts)),
        out_shape=outs,
        in_specs=[SMEM] + specs,
        out_specs=[VMEM] * len(outs),
        scratch_shapes=[pltpu.VMEM((len(strands), len(pieces) // n_halves, part, width), bf16)] * n_halves,
        compiler_params=pltpu.CompilerParams(vmem_limit_bytes=40 * 2**20),
        cost_estimate=pl.CostEstimate(
            flops=flops, bytes_accessed=10 * 2**20, transcendentals=len(strands) * heads * rows * new
        ),
        name=name,
    )(scal, *args)


def mix_kernel(lo, x_ref, loc_ref, back_ref, att0, att1, wo0, wo1, out_ref):
    rows = out_ref.shape[1]
    mixed = dot(att0[...].reshape(2 * rows, -1), wo0[...]) + dot(att1[...].reshape(2 * rows, -1), wo1[...])
    x_f = x_ref[lo : lo + rows].astype(f32)
    for t, loc in enumerate((loc_ref, back_ref)):
        out_ref[t] = x_f + loc[lo : lo + rows].astype(f32) + mixed[t * rows : (t + 1) * rows]


def mix_call(lo, x, loc, back, att, wo):
    rows, width = att[0].shape[1], x.shape[1]
    return pl.pallas_call(
        functools.partial(mix_kernel, lo),
        out_shape=jax.ShapeDtypeStruct((2, rows, width), f32),
        in_specs=[VMEM] * 7,
        out_specs=VMEM,
        compiler_params=pltpu.CompilerParams(vmem_limit_bytes=32 * 2**20),
        cost_estimate=pl.CostEstimate(
            flops=8 * rows * width * wo[0].shape[0], bytes_accessed=8 * 2**20, transcendentals=0
        ),
        name="mix",
    )(x, loc, back, *att, *wo)


def mid_kernel(groups, scal, *refs):
    partial, gain_ref, w1_ref, w2_ref, *refs = refs
    even_out, odd_out, middle_out, summed, mixed = refs[-5:]
    refs = refs[:-5]
    att, wo = refs[: len(refs) // (1 + groups)], refs[len(refs) // (1 + groups) :]
    here_m, here_g = scal[0], scal[1]
    rows = partial.shape[1]
    half = partial.shape[2] // groups
    blocks = [a_ref[...].reshape(2 * rows, -1) for a_ref in att]
    for h in range(groups):
        columns = pl.ds(pl.multiple_of((h ^ here_g) * half, half), half)
        part = partial[:, :, columns].reshape(2 * rows, half)
        mixed[:, columns] = part + sum(dot(a, w[...]) for a, w in zip(blocks, wo[h * len(att) : (h + 1) * len(att)]))
    middle = mixed[...]
    normed = (unit(middle) * gain_ref[...]).astype(bf16)
    expanded = jax.nn.gelu(dot(normed, w1_ref[...]), approximate=True).astype(bf16)
    out = dot(expanded, w2_ref[...])
    out = out[:rows] + out[rows:]
    both = middle[:rows] + middle[rows:]
    mp, _, share = summed.shape
    for j in range(mp):
        summed[j] = out[:, j * share : (j + 1) * share].astype(bf16)
    for k in range(mp):
        (odd_out if k & 1 else even_out)[k >> 1] = summed[here_m ^ k]
    for j in range(mp):
        block = both[:, j * share : (j + 1) * share]

        @pl.when(here_m == j)
        def _():
            middle_out[...] = block


def mid_call(groups, mp, scal, partial, gain, w1, w2, att, wo):
    _, rows, width = partial.shape
    share = width // mp
    args = [partial, gain, w1, w2, *att, *wo]
    return pl.pallas_call(
        functools.partial(mid_kernel, groups),
        out_shape=[jax.ShapeDtypeStruct((mp // 2, rows, share), bf16)] * 2 + [jax.ShapeDtypeStruct((rows, share), f32)],
        in_specs=[SMEM] + [VMEM] * len(args),
        out_specs=[VMEM] * 3,
        scratch_shapes=[pltpu.VMEM((mp, rows, share), bf16), pltpu.VMEM((2 * rows, width), f32)],
        compiler_params=pltpu.CompilerParams(vmem_limit_bytes=40 * 2**20),
        cost_estimate=pl.CostEstimate(
            flops=4 * rows * width * (width // 2 + 2 * w1.shape[1]),
            bytes_accessed=14 * 2**20,
            transcendentals=2 * rows * w1.shape[1],
        ),
        name="middle",
    )(scal, *args)


def together(*arrays):
    return lax.optimization_barrier(arrays)


def shards(
    nucleotide_features,
    location_table,
    premix_rescaler,
    probe_lookup_matrices,
    payload_projector,
    logit_sharpness,
    mixing_projector,
    premlp_rescaler,
    widening_matrix,
    narrowing_matrix,
):
    rows, width = nucleotide_features.shape
    heads = logit_sharpness.shape[0]
    lookup = probe_lookup_matrices.shape[2] // heads
    value_size = payload_projector.shape[1] // heads
    padded = (value_size // 128 + 1) * 128
    groups, seq, mp = (lax.axis_size(name) for name in AXES)
    here_g, here_m = lax.axis_index("groups"), lax.axis_index("mp")
    nx = mp // 2
    part, half = rows // mp, width // groups
    dims = (groups, seq, mp, heads, lookup, value_size, padded)
    scal = jnp.stack([here_m, here_g]).astype(jnp.int32)
    x_own = nucleotide_features.reshape(mp, part, width)
    loc_own = location_table.reshape(mp, part, width)

    flip = jnp.flip(jnp.eye(part, dtype=bf16), 0)
    gain = premix_rescaler.reshape(1, width)
    wq, wk = probe_lookup_matrices[0], probe_lookup_matrices[1]
    wv = jnp.pad(payload_projector.reshape(width, heads, value_size), ((0, 0), (0, 0), (0, padded - value_size)))
    wv = wv.reshape(width, heads * padded)

    def chunk(name, pieces, strands, own, last, x_parts, loc_parts, q=(), numer=()):
        weights = (wk, wv, wq) if own else (wk, wv)
        return chunk_call(
            name, dims, tuple(pieces), strands, own, last, scal, x_parts, loc_own, loc_parts,
            flip, gain, logit_sharpness, weights, q, numer,
        )

    loc_part = lax.dynamic_slice(location_table, (here_m * part, here_g * half), (part, half))
    loc_part, mixing, x_first = together(loc_part, mixing_projector, x_own)
    loc_z = [swap(loc_part, s=r) for r in range(1, seq)]
    mix_part = lax.dynamic_slice_in_dim(mixing, here_g * half, half, 1)
    mix_x = [swap(mix_part, m=2 * kx) for kx in range(1, nx)]
    x_near = jnp.stack([lax.dynamic_index_in_dim(x_first, here_m ^ (2 * kx), 0, False) for kx in range(nx)])
    own_pieces = [(0, k) for k in range(mp)]
    numer0, q0 = chunk("own_forward", own_pieces, (0,), True, False, [x_own], [])

    x_near, *held = together(x_near, *loc_z, *mix_x)
    loc_z, mix_x = held[: seq - 1], held[seq - 1 :]
    loc_far = jnp.stack(loc_z)
    combos = [(h, kx) for h in range(groups) for kx in range(nx)]
    loc_xy = [swap(loc_far, g=h, m=2 * kx) for h, kx in combos if (h, kx) != (0, 0)]
    far = {}
    x_mine = x_near[:1]
    arrived = swap(x_mine, s=2)
    for r in range(2, seq):
        if r < seq - 1:
            arrived, x_mine, numer0 = together(arrived, x_mine, numer0)
            coming = swap(x_mine, s=r + 1)
            far[r] = [arrived] + [swap(arrived, m=2 * kx) for kx in range(1, nx)]
            arrived = coming

    far[seq - 1] = [arrived]
    count = len(combos)
    held = together(numer0, loc_far, *loc_xy, *(a for r in range(2, seq) for a in far[r]))
    numer0, held = held[0], held[1:]
    loc_even, held = jnp.stack(held[:count]), held[count:]
    loc_parts = [loc_even, swap(loc_even, m=1)]
    for r in range(2, seq):
        far[r] = list(held[nx * (r - 2) : nx * (r - 1)])
    far[seq - 1] += [swap(far[seq - 1][0], m=2 * kx) for kx in range(1, nx)]
    x_near, *_ = together(x_near, arrived)
    x_one = swap(x_near, s=1)
    numer1, q1, back = chunk("own_back", own_pieces, (1,), True, False, [x_own], loc_parts)
    q, numer = [q0, q1], [numer0, numer1]

    for r in range(2, seq - 1):
        pieces = [(r, 2 * kx) for kx in range(nx)] + [(r, 2 * kx + 1) for kx in range(nx)]
        x_parts = far[r] + [swap(a, m=1) for a in far[r]]
        numer = chunk("far", pieces, (0, 1), False, False, x_parts, loc_parts, q, numer)
    r = seq - 1
    x_parts = [far[r][0], swap(far[r][0], m=1)]
    numer = chunk("half", [(r, 0), (r, 1)], (0, 1), False, False, x_parts, loc_parts, q, numer)
    mix_far = [swap(a, g=h) if h else a for h in range(groups) for a in mix_x]
    held = together(*numer, x_one, *far[r], *mix_far)
    n0, n1, x_one = held[:3]
    far[r], mix_far = held[3 : 3 + nx], held[3 + nx :]
    late = [x_one, *far[r][1:]]
    pieces = [(1, 2 * kx) for kx in range(nx)] + [(r, 2 * kx) for kx in range(1, nx)]
    numer = chunk("late_even", pieces, (0, 1), False, False, late, loc_parts, q, [n0, n1])
    late = [swap(a, m=1) for a in late]
    pieces = [(r, k + 1) for r, k in pieces]
    attended = chunk("late_odd", pieces, (0, 1), False, True, late, loc_parts, q, numer)

    wo_odd = swap(mixing_projector, m=1)
    wo_far = []
    for h in range(groups):
        some = list(mix_far[h * (nx - 1) : (h + 1) * (nx - 1)])
        wo_far += some + [swap(a, m=1) for a in some]
    w_mid = (premlp_rescaler.reshape(1, width), widening_matrix, narrowing_matrix)
    back = back.reshape(rows, width)
    a0, a1 = attended
    far0 = [swap(a0, m=2 * kx) for kx in range(1, nx)]
    partial = [
        mix_call(i * (rows // 2), nucleotide_features, location_table, back, [a, swap(a, m=1)], [mixing_projector, wo_odd])
        for i, a in enumerate(attended)
    ]
    held = together(a1, *far0)
    a1, far0 = held[0], held[1:]
    far1 = [swap(a1, m=2 * kx) for kx in range(1, nx)]
    blocks = []
    for i, far_even in enumerate((far0, far1)):
        att = list(far_even) + [swap(a, m=1) for a in far_even]
        even_out, odd_out, middle_share = mid_call(groups, mp, scal, partial[i], *w_mid, att, wo_far)
        paired = even_out.astype(f32) + swap(odd_out, m=1).astype(f32)
        total = middle_share + paired[0]
        for kx in range(1, nx):
            total = total + swap(paired[kx].astype(bf16), m=2 * kx).astype(f32)
        blocks.append(0.5 * total)
    return jnp.concatenate(blocks, axis=0)


def solution(mesh):
    return jax.shard_map(
        shards,
        mesh=mesh,
        in_specs=(
            P(("groups", "seq"), None),
            P("seq", None),
            P(),
            P(None, None, "mp"),
            P(None, "mp"),
            P("mp"),
            P("mp", None),
            P(),
            P(None, "mp"),
            P("mp", None),
        ),
        out_specs=P(("groups", "seq"), "mp"),
        check_vma=False,
    )
```

```python
import functools

import jax
import jax.numpy as jnp
from jax import lax
from jax.experimental import pallas as pl
from jax.experimental.pallas import tpu as pltpu
from jax.sharding import PartitionSpec as P

epsilon = 1e-06
LOG2E = 1.4426950408889634
f32, bf16 = jnp.float32, jnp.bfloat16
AXES = ("groups", "seq", "mp")


def swap(block, g=0, s=0, m=0):
    groups, seq, mp = (lax.axis_size(name) for name in AXES)
    code = (g * seq + s) * mp + m
    return lax.ppermute(block, AXES, [(i, i ^ code) for i in range(groups * seq * mp)])


def unit(block):
    return block * lax.rsqrt(jnp.mean(block * block, axis=-1, keepdims=True) + epsilon)


def scaled_unit(block, scale):
    mean = jnp.mean(block * block, axis=-1, keepdims=True)
    return (block * (scale * lax.rsqrt(scale * scale * mean + epsilon))).astype(bf16)


def dot(a, b):
    return jnp.dot(a, b, preferred_element_type=f32)


def chunk_kernel(dims, pieces, strands, own, last, n_x, n_loc, scal, *refs):
    groups, seq, mp, heads, lookup, value_size, padded = dims
    nx = mp // 2
    refs = list(refs)
    take = lambda n: [refs.pop(0) for _ in range(n)]
    x_refs = take(n_x)
    (own_loc,) = take(1)
    loc_refs = take(n_loc)
    flip_ref, sharp_ref, wk_ref, wv_ref = take(4)
    wq_ref = take(1)[0] if own else None
    q_refs = [] if own else take(len(strands))
    numer_in = [] if own else take(len(strands))
    out_refs = take(2 if last else len(strands))
    if own:
        q_refs = take(1)
        back_out = take(1)[0] if 1 in strands else None
    halves = list(zip(refs[::2], refs[1::2]))
    here_m, here_g = scal[0], scal[1]
    x_places = [(ref, i) for ref in x_refs for i in range(ref.shape[0])]
    part = own_loc.shape[1]
    length = mp * part
    per_half = len(pieces) // len(halves)
    splits = len(out_refs) if last else 1

    width = own_loc.shape[2]
    half = width // groups
    columns = [pl.ds(pl.multiple_of((h ^ here_g) * half, half), half) for h in range(groups)]

    def loc_piece(r, k, h):
        if r == 0:
            return own_loc[here_m ^ k, :, columns[h]]
        return loc_refs[k & 1][h * nx + (k >> 1), r - 1]

    products = []
    for n, (streams, scales) in enumerate(halves):
        for i in range(per_half):
            r, k = pieces[n * per_half + i]
            ref, at = (x_refs[0], here_m ^ k) if own else x_places[n * per_half + i]
            place = here_m ^ k if own else i
            for p, t in enumerate(strands):
                square = 0.0
                for h in range(groups):
                    if t == 0:
                        loc = loc_piece(r, k, h)
                    else:
                        loc = dot(flip_ref[...], loc_piece(r ^ (seq - 1), k ^ (mp - 1), h)).astype(bf16)
                        if own:
                            back_out[place, :, columns[h]] = loc
                    stream = ref[at, :, columns[h]] + loc
                    streams[p, place, :, columns[h]] = stream
                    square = square + jnp.sum(jnp.square(stream.astype(f32)), axis=-1, keepdims=True)
                scales[p, place] = jnp.broadcast_to(lax.rsqrt(square / width + epsilon), (part, 128))
        rows = streams[...].reshape(-1, width)
        scale = scales[...].reshape(-1, 128)
        if own:
            query = dot(rows, wq_ref[...])
            for h in range(heads):
                cols = slice(h * lookup, (h + 1) * lookup)
                q_refs[0][:, cols] = scaled_unit(query[:, cols], scale)
        products.append((scale, dot(rows, wk_ref[...]), dot(rows, wv_ref[...])))
    some = per_half * part
    ones = lax.broadcasted_iota(jnp.int32, (some, 128), 1) == value_size % 128
    for p in range(len(strands)):
        mine = slice(p * some, (p + 1) * some)
        attended = []
        for h in range(heads):
            cols = slice(h * lookup, (h + 1) * lookup)
            key_n = jnp.concatenate([scaled_unit(k[mine, cols], scale[mine]) for scale, k, v in products], axis=0)
            value_h = []
            for c in range(padded // 128):
                block = slice(h * padded + c * 128, h * padded + (c + 1) * 128)
                column = jnp.concatenate([v[mine, block] * scale[mine] for scale, k, v in products], axis=0)
                if c == value_size // 128:
                    column = jnp.where(jnp.concatenate([ones] * len(products), axis=0), 1.0, column)
                value_h.append(column.astype(bf16))
            value_h = jnp.concatenate(value_h, axis=1)
            scores = lax.dot_general(
                q_refs[p][:, cols], key_n, (((1,), (1,)), ((), ())), preferred_element_type=f32
            )
            weight = jnp.exp2(scores * (sharp_ref[h] * (LOG2E / lookup))).astype(bf16)
            numer = dot(weight, value_h)
            if not own:
                numer = numer + numer_in[p][h]
            if last:
                attended.append(numer[:, :value_size] / numer[:, value_size : value_size + 1])
            else:
                out_refs[p][h] = numer
        if last:
            attended = jnp.concatenate(attended, axis=1).astype(bf16)
            block = length // splits
            for i, out_ref in enumerate(out_refs):
                out_ref[p] = attended[i * block : (i + 1) * block]


VMEM = pl.BlockSpec(memory_space=pltpu.VMEM)
SMEM = pl.BlockSpec(memory_space=pltpu.SMEM)


def chunk_call(name, dims, pieces, strands, own, last, scal, x_parts, own_loc, loc_parts, flip, sharp, weights, q, numer):
    groups, seq, mp, heads, lookup, value_size, padded = dims
    _, part, width = own_loc.shape
    rows = part * mp
    args = list(x_parts) + [own_loc] + list(loc_parts) + [flip, sharp] + list(weights) + list(q) + list(numer)
    specs = [SMEM if a is sharp else VMEM for a in args]
    if last:
        outs = [jax.ShapeDtypeStruct((2, rows // 2, heads * value_size), bf16)] * 2
    else:
        outs = [jax.ShapeDtypeStruct((heads, rows, padded), f32)] * len(strands)
    if own:
        outs = outs + [jax.ShapeDtypeStruct((rows, heads * lookup), bf16)]
        if 1 in strands:
            outs = outs + [jax.ShapeDtypeStruct((mp, part, width), bf16)]
    n_halves = 2 if len(pieces) == mp and not own else 1
    new = len(pieces) * part
    flops = 2 * len(strands) * new * (width * (heads * (lookup + padded)) + heads * rows * (lookup + padded))
    return pl.pallas_call(
        functools.partial(chunk_kernel, dims, pieces, strands, own, last, len(x_parts), len(loc_parts)),
        out_shape=outs,
        in_specs=[SMEM] + specs,
        out_specs=[VMEM] * len(outs),
        scratch_shapes=[
            pltpu.VMEM((len(strands), len(pieces) // n_halves, part, width), bf16),
            pltpu.VMEM((len(strands), len(pieces) // n_halves, part, 128), f32),
        ]
        * n_halves,
        compiler_params=pltpu.CompilerParams(vmem_limit_bytes=40 * 2**20),
        cost_estimate=pl.CostEstimate(
            flops=flops, bytes_accessed=10 * 2**20, transcendentals=len(strands) * heads * rows * new
        ),
        name=name,
    )(scal, *args)


def mix_kernel(lo, x_ref, loc_ref, back_ref, att0, att1, wo0, wo1, out_ref):
    rows = out_ref.shape[1]
    mixed = dot(att0[...].reshape(2 * rows, -1), wo0[...]) + dot(att1[...].reshape(2 * rows, -1), wo1[...])
    x_f = x_ref[lo : lo + rows].astype(f32)
    for t, loc in enumerate((loc_ref, back_ref)):
        out_ref[t] = x_f + loc[lo : lo + rows].astype(f32) + mixed[t * rows : (t + 1) * rows]


def mix_call(lo, x, loc, back, att, wo):
    rows, width = att[0].shape[1], x.shape[1]
    return pl.pallas_call(
        functools.partial(mix_kernel, lo),
        out_shape=jax.ShapeDtypeStruct((2, rows, width), f32),
        in_specs=[VMEM] * 7,
        out_specs=VMEM,
        compiler_params=pltpu.CompilerParams(vmem_limit_bytes=32 * 2**20),
        cost_estimate=pl.CostEstimate(
            flops=8 * rows * width * wo[0].shape[0], bytes_accessed=8 * 2**20, transcendentals=0
        ),
        name="mix",
    )(x, loc, back, *att, *wo)


def mid_kernel(groups, scal, *refs):
    partial, gain_ref, w1_ref, w2_ref, *refs = refs
    even_out, odd_out, middle_out, summed, mixed = refs[-5:]
    refs = refs[:-5]
    att, wo = refs[: len(refs) // (1 + groups)], refs[len(refs) // (1 + groups) :]
    here_m, here_g = scal[0], scal[1]
    rows = partial.shape[1]
    half = partial.shape[2] // groups
    blocks = [a_ref[...].reshape(2 * rows, -1) for a_ref in att]
    for h in range(groups):
        columns = pl.ds(pl.multiple_of((h ^ here_g) * half, half), half)
        part = partial[:, :, columns].reshape(2 * rows, half)
        mixed[:, columns] = part + sum(dot(a, w[...]) for a, w in zip(blocks, wo[h * len(att) : (h + 1) * len(att)]))
    middle = mixed[...]
    normed = (unit(middle) * gain_ref[...]).astype(bf16)
    expanded = jax.nn.gelu(dot(normed, w1_ref[...]), approximate=True).astype(bf16)
    out = dot(expanded, w2_ref[...])
    out = out[:rows] + out[rows:]
    both = middle[:rows] + middle[rows:]
    mp, _, share = summed.shape
    for j in range(mp):
        summed[j] = out[:, j * share : (j + 1) * share].astype(bf16)
    for k in range(mp):
        (odd_out if k & 1 else even_out)[k >> 1] = summed[here_m ^ k]
    for j in range(mp):
        block = both[:, j * share : (j + 1) * share]

        @pl.when(here_m == j)
        def _():
            middle_out[...] = block


def mid_call(groups, mp, scal, partial, gain, w1, w2, att, wo):
    _, rows, width = partial.shape
    share = width // mp
    args = [partial, gain, w1, w2, *att, *wo]
    return pl.pallas_call(
        functools.partial(mid_kernel, groups),
        out_shape=[jax.ShapeDtypeStruct((mp // 2, rows, share), bf16)] * 2 + [jax.ShapeDtypeStruct((rows, share), f32)],
        in_specs=[SMEM] + [VMEM] * len(args),
        out_specs=[VMEM] * 3,
        scratch_shapes=[pltpu.VMEM((mp, rows, share), bf16), pltpu.VMEM((2 * rows, width), f32)],
        compiler_params=pltpu.CompilerParams(vmem_limit_bytes=40 * 2**20),
        cost_estimate=pl.CostEstimate(
            flops=4 * rows * width * (width // 2 + 2 * w1.shape[1]),
            bytes_accessed=14 * 2**20,
            transcendentals=2 * rows * w1.shape[1],
        ),
        name="middle",
    )(scal, *args)


def together(*arrays):
    return lax.optimization_barrier(arrays)


def shards(
    nucleotide_features,
    location_table,
    premix_rescaler,
    probe_lookup_matrices,
    payload_projector,
    logit_sharpness,
    mixing_projector,
    premlp_rescaler,
    widening_matrix,
    narrowing_matrix,
):
    rows, width = nucleotide_features.shape
    heads = logit_sharpness.shape[0]
    lookup = probe_lookup_matrices.shape[2] // heads
    value_size = payload_projector.shape[1] // heads
    padded = (value_size // 128 + 1) * 128
    groups, seq, mp = (lax.axis_size(name) for name in AXES)
    here_g, here_m = lax.axis_index("groups"), lax.axis_index("mp")
    nx = mp // 2
    part, half = rows // mp, width // groups
    dims = (groups, seq, mp, heads, lookup, value_size, padded)
    scal = jnp.stack([here_m, here_g]).astype(jnp.int32)
    x_own = nucleotide_features.reshape(mp, part, width)
    loc_own = location_table.reshape(mp, part, width)

    flip = jnp.flip(jnp.eye(part, dtype=bf16), 0)
    gain = premix_rescaler.reshape(width, 1)
    wq, wk = [(gain * w.astype(f32)).astype(bf16) for w in (probe_lookup_matrices[0], probe_lookup_matrices[1])]
    wv = (gain * payload_projector.astype(f32)).astype(bf16).reshape(width, heads, value_size)
    wv = jnp.pad(wv, ((0, 0), (0, 0), (0, padded - value_size))).reshape(width, heads * padded)

    def chunk(name, pieces, strands, own, last, x_parts, loc_parts, q=(), numer=()):
        weights = (wk, wv, wq) if own else (wk, wv)
        return chunk_call(
            name, dims, tuple(pieces), strands, own, last, scal, x_parts, loc_own, loc_parts,
            flip, logit_sharpness, weights, q, numer,
        )

    loc_part = lax.dynamic_slice(location_table, (here_m * part, here_g * half), (part, half))
    loc_part, x_first = together(loc_part, x_own)
    loc_z = [swap(loc_part, s=r) for r in range(1, seq)]
    x_near = jnp.stack([lax.dynamic_index_in_dim(x_first, here_m ^ (2 * kx), 0, False) for kx in range(nx)])
    x_one = swap(x_near, s=1)
    mix_part = lax.dynamic_slice_in_dim(mixing_projector, here_g * half, half, 1)
    mix_x = [swap(mix_part, m=2 * kx) for kx in range(1, nx)]
    own_pieces = [(0, k) for k in range(mp)]
    numer0, q0 = chunk("own_forward", own_pieces, (0,), True, False, [x_own], [])

    x_mine, *loc_z = together(x_near[:1], *loc_z)
    loc_far = jnp.stack(loc_z)
    loc_then, *mix_x = together(loc_far, *mix_x)
    combos = [(h, kx) for h in range(groups) for kx in range(nx)]
    loc_xy = [swap(loc_then if h and kx else loc_far, g=h, m=2 * kx) for h, kx in combos if (h, kx) != (0, 0)]
    far = {}
    arrived = swap(x_mine, s=2)
    for r in range(2, seq - 1):
        arrived, x_mine, numer0, x_one = together(arrived, x_mine, numer0, x_one)
        coming = swap(x_mine, s=r + 1)
        far[r] = [arrived] + [swap(arrived, m=2 * kx) for kx in range(1, nx)]
        arrived = coming
    flat = [a for r in range(2, seq - 1) for a in far[r]]
    numer0, x_one, arrived, *flat = together(numer0, x_one, arrived, loc_far, *loc_xy, *flat)
    loc_even, flat = jnp.stack(flat[: len(combos)]), flat[len(combos) :]
    for r in range(2, seq - 1):
        far[r] = list(flat[nx * (r - 2) : nx * (r - 1)])

    last = seq - 1
    far[last] = [arrived] + [swap(arrived, m=2 * kx) for kx in range(1, nx)]
    loc_odd = swap(loc_even, m=1)
    evens = [(1, 2 * kx) for kx in range(nx)] + [(2, 2 * kx) for kx in range(nx)]
    odds = [(r, k + 1) for r, k in evens]
    even_parts = [x_one, *far[2]]
    (numer0,) = chunk("even_forward", evens, (0,), False, False, even_parts, [loc_even], [q0], [numer0])
    numer0, loc_odd = together(numer0, loc_odd)
    loc_parts = [loc_even, loc_odd]
    numer1, q1, back = chunk("own_back", own_pieces, (1,), True, False, [x_own], loc_parts)
    numer1, arrived, *even_parts = together(numer1, arrived, *even_parts)
    odd_parts = [swap(a, m=1) for a in even_parts]
    x_half = [arrived, swap(arrived, m=1)]
    (numer1,) = chunk("even_back", evens, (1,), False, False, even_parts, loc_parts, [q1], [numer1])
    mixing, numer1, *mix_x = together(mixing_projector, numer1, *mix_x)
    mix_far = [swap(a, g=h) if h else a for h in range(groups) for a in mix_x]
    q, numer = [q0, q1], [numer0, numer1]
    numer = chunk("odd", odds, (0, 1), False, False, odd_parts, loc_parts, q, numer)
    for r in range(3, last):
        pieces = [(r, 2 * kx) for kx in range(nx)] + [(r, 2 * kx + 1) for kx in range(nx)]
        x_parts = far[r] + [swap(a, m=1) for a in far[r]]
        numer = chunk("far", pieces, (0, 1), False, False, x_parts, loc_parts, q, numer)
    n0, n1, *late = together(*numer, *far[last][1:])
    late += [swap(a, m=1) for a in late]
    numer = chunk("half", [(last, 0), (last, 1)], (0, 1), False, False, x_half, loc_parts, q, [n0, n1])
    n0, n1, *mix_far = together(*numer, *mix_far)
    pieces = [(last, 2 * kx) for kx in range(1, nx)] + [(last, 2 * kx + 1) for kx in range(1, nx)]
    a0, a1 = chunk("late", pieces, (0, 1), False, True, late, loc_parts, q, [n0, n1])

    wo_own = [mixing, swap(mixing, m=1)]
    wo_far = []
    for h in range(groups):
        some = list(mix_far[h * (nx - 1) : (h + 1) * (nx - 1)])
        wo_far += some + [swap(a, m=1) for a in some]
    w_mid = (premlp_rescaler.reshape(1, width), widening_matrix, narrowing_matrix)
    stream = (nucleotide_features, location_table, back.reshape(rows, width))

    def across(block):
        return [swap(block, m=2 * kx) for kx in range(1, nx)]

    def cores(blocks):
        return list(blocks) + [swap(a, m=1) for a in blocks]

    far0 = across(a0)
    part0 = mix_call(0, *stream, cores([a0]), wo_own)
    a1, *far0 = together(a1, *far0)
    far1 = across(a1)
    even0, odd0, share0 = mid_call(groups, mp, scal, part0, *w_mid, cores(far0), wo_far)
    even0, odd0, share0, *far1 = together(even0, odd0, share0, *far1)
    paired0 = even0.astype(f32) + swap(odd0, m=1).astype(f32)
    part1 = mix_call(rows // 2, *stream, cores([a1]), wo_own)
    part1, paired0 = together(part1, paired0)
    across0 = [swap(paired0[kx].astype(bf16), m=2 * kx) for kx in range(1, nx)]
    even1, odd1, share1 = mid_call(groups, mp, scal, part1, *w_mid, cores(far1), wo_far)
    even1, odd1, share1, *across0 = together(even1, odd1, share1, *across0)
    paired1 = even1.astype(f32) + swap(odd1, m=1).astype(f32)
    across1 = [swap(paired1[kx].astype(bf16), m=2 * kx) for kx in range(1, nx)]
    blocks = [
        0.5 * (share + paired[0] + sum(a.astype(f32) for a in arrived))
        for share, paired, arrived in ((share0, paired0, across0), (share1, paired1, across1))
    ]
    return jnp.concatenate(blocks, axis=0)


def solution(mesh):
    return jax.shard_map(
        shards,
        mesh=mesh,
        in_specs=(
            P(("groups", "seq"), None),
            P("seq", None),
            P(),
            P(None, None, "mp"),
            P(None, "mp"),
            P("mp"),
            P("mp", None),
            P(),
            P(None, "mp"),
            P("mp", None),
        ),
        out_specs=P(("groups", "seq"), "mp"),
        check_vma=False,
    )
```

```python
import functools

import jax
import jax.numpy as jnp
from jax import lax
from jax.experimental import pallas as pl
from jax.experimental.pallas import tpu as pltpu
from jax.sharding import PartitionSpec as P

epsilon = 1e-06
LOG2E = 1.4426950408889634
COST = 2**20
f32, bf16 = jnp.float32, jnp.bfloat16
AXES = ("groups", "seq", "mp")


def swap(block, g=0, s=0, m=0):
    groups, seq, mp = (lax.axis_size(name) for name in AXES)
    code = (g * seq + s) * mp + m
    return lax.ppermute(block, AXES, [(i, i ^ code) for i in range(groups * seq * mp)])


def unit(block):
    return block * lax.rsqrt(jnp.mean(block * block, axis=-1, keepdims=True) + epsilon)


def scaled_unit(block, scale):
    mean = jnp.mean(block * block, axis=-1, keepdims=True)
    return (block * (scale * lax.rsqrt(scale * scale * mean + epsilon))).astype(bf16)


def dot(a, b):
    return jnp.dot(a, b, preferred_element_type=f32)


def chunk_kernel(dims, batches, where, own, last, counts, scal, *refs):
    groups, seq, mp, heads, lookup, value_size, padded = dims
    nx = mp // 2
    strands = sorted({t for batch in batches for t, r, k in batch})
    refs = list(refs)
    take = lambda n: [refs.pop(0) for _ in range(n)]
    x_refs = take(counts[0])
    (own_loc,) = take(1)
    loc_refs = take(counts[1])
    flip_ref, sharp_ref, wk_ref, wv_ref = take(4)
    wq_ref = take(1)[0] if own else None
    q_refs = [] if own else take(len(strands))
    numer_in = [] if own else take(len(strands))
    out_refs = take(2 if last else len(strands))
    if own:
        q_refs = take(1)
        back_out = take(1)[0] if 1 in strands else None
    scratch = list(zip(refs[::2], refs[1::2]))
    here_m, here_g = scal[0], scal[1]
    part, width = own_loc.shape[1:]
    half = width // groups
    columns = [pl.ds(pl.multiple_of((h ^ here_g) * half, half), half) for h in range(groups)]

    def loc_piece(r, k, h):
        if r == 0:
            return own_loc[here_m ^ k, :, columns[h]]
        return loc_refs[k & 1][h * nx + (k >> 1), r - 1]

    products = []
    for batch, (streams, scales) in zip(batches, scratch):
        for i, (t, r, k) in enumerate(batch):
            ref, at = (x_refs[0], here_m ^ k) if own else (x_refs[where[r, k][0]], where[r, k][1])
            place = here_m ^ k if own else i
            square = 0.0
            for h in range(groups):
                if t == 0:
                    loc = loc_piece(r, k, h)
                else:
                    loc = dot(flip_ref[...], loc_piece(r ^ (seq - 1), k ^ (mp - 1), h)).astype(bf16)
                    if own:
                        back_out[place, :, columns[h]] = loc
                stream = ref[at, :, columns[h]] + loc
                streams[place, :, columns[h]] = stream
                square = square + jnp.sum(jnp.square(stream.astype(f32)), axis=-1, keepdims=True)
            scales[place] = jnp.broadcast_to(lax.rsqrt(square / width + epsilon), (part, 128))
        rows = streams[...].reshape(-1, width)
        scale = scales[...].reshape(-1, 128)
        if own:
            query = dot(rows, wq_ref[...])
            for h in range(heads):
                cols = slice(h * lookup, (h + 1) * lookup)
                q_refs[0][:, cols] = scaled_unit(query[:, cols], scale)
        products.append((scale, dot(rows, wk_ref[...]), dot(rows, wv_ref[...])))
    for p, t in enumerate(strands):
        mine = []
        for batch, product in zip(batches, products):
            places = [i for i, item in enumerate(batch) if item[0] == t]
            if places:
                rows = slice(places[0] * part, (places[-1] + 1) * part)
                mine.append([a[rows] for a in product])
        attended = []
        for h in range(heads):
            cols = slice(h * lookup, (h + 1) * lookup)
            key_n = jnp.concatenate([scaled_unit(k[:, cols], scale) for scale, k, v in mine], axis=0)
            value_h = []
            for c in range(padded // 128):
                block = slice(h * padded + c * 128, h * padded + (c + 1) * 128)
                column = jnp.concatenate([v[:, block] * scale for scale, k, v in mine], axis=0)
                if c == value_size // 128:
                    lane = lax.broadcasted_iota(jnp.int32, column.shape, 1)
                    column = jnp.where(lane == value_size % 128, 1.0, column)
                value_h.append(column.astype(bf16))
            value_h = jnp.concatenate(value_h, axis=1)
            scores = lax.dot_general(
                q_refs[p][:, cols], key_n, (((1,), (1,)), ((), ())), preferred_element_type=f32
            )
            weight = jnp.exp2(scores * (sharp_ref[h] * (LOG2E / lookup))).astype(bf16)
            numer = dot(weight, value_h)
            if not own:
                numer = numer + numer_in[p][h]
            if last:
                attended.append(numer[:, :value_size] / numer[:, value_size : value_size + 1])
            else:
                out_refs[p][h] = numer
        if last:
            attended = jnp.concatenate(attended, axis=1).astype(bf16)
            block = attended.shape[0] // len(out_refs)
            for i, out_ref in enumerate(out_refs):
                out_ref[p] = attended[i * block : (i + 1) * block]


VMEM = pl.BlockSpec(memory_space=pltpu.VMEM)
SMEM = pl.BlockSpec(memory_space=pltpu.SMEM)


def chunk_call(name, dims, batches, own, last, scal, x_parts, own_loc, loc_parts, flip, sharp, weights, q, numer):
    groups, seq, mp, heads, lookup, value_size, padded = dims
    _, part, width = own_loc.shape
    rows = part * mp
    batches = tuple(tuple(sorted(batch)) for batch in batches)
    strands = sorted({t for batch in batches for t, r, k in batch})
    where = {name: (n, i) for n, (_, names) in enumerate(x_parts) for name, i in names.items()}
    args = [a for a, _ in x_parts] + [own_loc] + list(loc_parts) + [flip, sharp] + list(weights) + list(q) + list(numer)
    specs = [SMEM if a is sharp else VMEM for a in args]
    if last:
        outs = [jax.ShapeDtypeStruct((2, rows // 2, heads * value_size), bf16)] * 2
    else:
        outs = [jax.ShapeDtypeStruct((heads, rows, padded), f32)] * len(strands)
    if own:
        outs = outs + [jax.ShapeDtypeStruct((rows, heads * lookup), bf16)]
        if 1 in strands:
            outs = outs + [jax.ShapeDtypeStruct((mp, part, width), bf16)]
    scratch = []
    for batch in batches:
        scratch += [pltpu.VMEM((len(batch), part, width), bf16), pltpu.VMEM((len(batch), part, 128), f32)]
    return pl.pallas_call(
        functools.partial(chunk_kernel, dims, batches, where, own, last, (len(x_parts), len(loc_parts))),
        out_shape=outs,
        in_specs=[SMEM] + specs,
        out_specs=[VMEM] * len(outs),
        scratch_shapes=scratch,
        compiler_params=pltpu.CompilerParams(vmem_limit_bytes=40 * 2**20),
        cost_estimate=pl.CostEstimate(flops=COST, bytes_accessed=COST, transcendentals=0),
        name=name,
    )(scal, *args)


def mix_kernel(lo, x_ref, loc_ref, back_ref, att0, att1, wo0, wo1, out_ref):
    rows = out_ref.shape[1]
    mixed = dot(att0[...].reshape(2 * rows, -1), wo0[...]) + dot(att1[...].reshape(2 * rows, -1), wo1[...])
    x_f = x_ref[lo : lo + rows].astype(f32)
    for t, loc in enumerate((loc_ref, back_ref)):
        out_ref[t] = x_f + loc[lo : lo + rows].astype(f32) + mixed[t * rows : (t + 1) * rows]


def mix_call(lo, x, loc, back, att, wo):
    rows, width = att[0].shape[1], x.shape[1]
    return pl.pallas_call(
        functools.partial(mix_kernel, lo),
        out_shape=jax.ShapeDtypeStruct((2, rows, width), f32),
        in_specs=[VMEM] * 7,
        out_specs=VMEM,
        compiler_params=pltpu.CompilerParams(vmem_limit_bytes=32 * 2**20),
        cost_estimate=pl.CostEstimate(
            flops=8 * rows * width * wo[0].shape[0], bytes_accessed=8 * 2**20, transcendentals=0
        ),
        name="mix",
    )(x, loc, back, *att, *wo)


def mid_kernel(groups, scal, *refs):
    partial, gain_ref, w1_ref, w2_ref, *refs = refs
    even_out, odd_out, middle_out, summed, mixed = refs[-5:]
    refs = refs[:-5]
    att, wo = refs[: len(refs) // (1 + groups)], refs[len(refs) // (1 + groups) :]
    here_m, here_g = scal[0], scal[1]
    rows = partial.shape[1]
    half = partial.shape[2] // groups
    blocks = [a_ref[...].reshape(2 * rows, -1) for a_ref in att]
    for h in range(groups):
        columns = pl.ds(pl.multiple_of((h ^ here_g) * half, half), half)
        part = partial[:, :, columns].reshape(2 * rows, half)
        mixed[:, columns] = part + sum(dot(a, w[...]) for a, w in zip(blocks, wo[h * len(att) : (h + 1) * len(att)]))
    middle = mixed[...]
    normed = (unit(middle) * gain_ref[...]).astype(bf16)
    expanded = jax.nn.gelu(dot(normed, w1_ref[...]), approximate=True).astype(bf16)
    out = dot(expanded, w2_ref[...])
    out = out[:rows] + out[rows:]
    both = middle[:rows] + middle[rows:]
    mp, _, share = summed.shape
    for j in range(mp):
        summed[j] = out[:, j * share : (j + 1) * share].astype(bf16)
    for k in range(mp):
        (odd_out if k & 1 else even_out)[k >> 1] = summed[here_m ^ k]
    for j in range(mp):
        block = both[:, j * share : (j + 1) * share]

        @pl.when(here_m == j)
        def _():
            middle_out[...] = block


def mid_call(groups, mp, scal, partial, gain, w1, w2, att, wo):
    _, rows, width = partial.shape
    share = width // mp
    args = [partial, gain, w1, w2, *att, *wo]
    return pl.pallas_call(
        functools.partial(mid_kernel, groups),
        out_shape=[jax.ShapeDtypeStruct((mp // 2, rows, share), bf16)] * 2 + [jax.ShapeDtypeStruct((rows, share), f32)],
        in_specs=[SMEM] + [VMEM] * len(args),
        out_specs=[VMEM] * 3,
        scratch_shapes=[pltpu.VMEM((mp, rows, share), bf16), pltpu.VMEM((2 * rows, width), f32)],
        compiler_params=pltpu.CompilerParams(vmem_limit_bytes=40 * 2**20),
        cost_estimate=pl.CostEstimate(
            flops=4 * rows * width * (width // 2 + 2 * w1.shape[1]),
            bytes_accessed=14 * 2**20,
            transcendentals=2 * rows * w1.shape[1],
        ),
        name="middle",
    )(scal, *args)


def together(*arrays):
    return lax.optimization_barrier(arrays)


def shards(
    nucleotide_features,
    location_table,
    premix_rescaler,
    probe_lookup_matrices,
    payload_projector,
    logit_sharpness,
    mixing_projector,
    premlp_rescaler,
    widening_matrix,
    narrowing_matrix,
):
    rows, width = nucleotide_features.shape
    heads = logit_sharpness.shape[0]
    lookup = probe_lookup_matrices.shape[2] // heads
    value_size = payload_projector.shape[1] // heads
    padded = (value_size // 128 + 1) * 128
    groups, seq, mp = (lax.axis_size(name) for name in AXES)
    here_g, here_m = lax.axis_index("groups"), lax.axis_index("mp")
    nx = mp // 2
    part, half = rows // mp, width // groups
    dims = (groups, seq, mp, heads, lookup, value_size, padded)
    scal = jnp.stack([here_m, here_g]).astype(jnp.int32)
    x_own = nucleotide_features.reshape(mp, part, width)
    loc_own = location_table.reshape(mp, part, width)

    flip = jnp.flip(jnp.eye(part, dtype=bf16), 0)
    gain = premix_rescaler.reshape(width, 1)
    wq, wk = [(gain * w.astype(f32)).astype(bf16) for w in (probe_lookup_matrices[0], probe_lookup_matrices[1])]
    wv = (gain * payload_projector.astype(f32)).astype(bf16).reshape(width, heads, value_size)
    wv = jnp.pad(wv, ((0, 0), (0, 0), (0, padded - value_size))).reshape(width, heads * padded)

    have = {}

    def hold(array, names):
        have.update({name: (array, i) for i, name in enumerate(names)})

    def chunk(name, batches, own, last, loc_parts, q=(), numer=()):
        weights = (wk, wv, wq) if own else (wk, wv)
        x_parts = {}
        for r, k in sorted({item[1:] for batch in batches for item in batch}):
            array, i = have[r, k]
            x_parts.setdefault(id(array), (array, {}))[1][r, k] = i
        return chunk_call(
            name, dims, batches, own, last, scal, list(x_parts.values()), loc_own, loc_parts,
            flip, logit_sharpness, weights, q, numer,
        )

    direct = range(3, seq, 2)
    near_r = [1] + [r - 1 for r in direct]
    loc_part = lax.dynamic_slice(location_table, (here_m * part, here_g * half), (part, half))
    loc_part, x_first = together(loc_part, x_own)
    loc_z = {r: swap(loc_part, s=r) for r in [*direct, 1]}
    x_mine = lax.dynamic_slice_in_dim(x_first, here_m, 1, 0)
    x_direct = [swap(x_mine, s=r) for r in direct]
    mix_part = lax.dynamic_slice_in_dim(mixing_projector, here_g * half, half, 1)
    mix_x = [swap(mix_part, m=2 * kx) for kx in range(1, nx)]
    relayed = swap(jnp.stack([loc_z[r] for r in direct]), s=1)
    loc_z.update({r - 1: relayed[i] for i, r in enumerate(direct)})

    loc_far = jnp.stack([loc_z[r] for r in range(1, seq)])
    loc_then, *mix_x = together(loc_far, *mix_x)
    combos = [(h, kx) for h in range(groups) for kx in range(nx)]
    loc_xy = [swap(loc_then if h and kx else loc_far, g=h, m=2 * kx) for h, kx in combos if (h, kx) != (0, 0)]
    x_mine, *x_direct = together(x_mine, *x_direct)
    x_near = swap(jnp.concatenate([x_mine, *x_direct]), s=1)
    x_across = [swap(a, m=2 * kx) for a in x_direct for kx in range(1, nx)]
    hold(x_own, [(0, k) for k in range(mp)])
    numer0, q0 = chunk("own_forward", [[(0, 0, k) for k in range(mp)]], True, False, [])

    held = together(numer0, loc_far, *loc_xy, x_near, *x_direct, *x_across)
    numer0, loc_even, held = held[0], jnp.stack(held[1 : 1 + len(combos)]), list(held[1 + len(combos) :])
    loc_odd = swap(loc_even, m=1)
    x_near_across = [swap(held[0], m=2 * kx) for kx in range(1, nx)]
    names = [[(r, 0) for r in near_r]] + [[(r, 0)] for r in direct]
    names += [[(r, 2 * kx)] for r in direct for kx in range(1, nx)]
    odd_names = lambda names: [(r, k + 1) for r, k in names]
    for array, some in zip(held, names):
        hold(array, some)
        hold(swap(array, m=1), odd_names(some))
    early = sorted(name for some in names for name in some)
    early = [early[i : i + 4] for i in range(0, len(early), 4)]
    for some in early:
        (numer0,) = chunk("even_forward", [[(0, r, k) for r, k in some]], False, False, [loc_even], [q0], [numer0])
    numer0, loc_odd = together(numer0, loc_odd)
    loc_parts = [loc_even, loc_odd]
    numer1, q1, back = chunk("own_back", [[(1, 0, k) for k in range(mp)]], True, False, loc_parts)
    q, numer = [q0, q1], [numer0, numer1]
    both = lambda names: [(t, r, k) for t in range(2) for r, k in names]
    for some in early:
        batches = [[(1, r, k) for r, k in some], both(odd_names(some))]
        numer = chunk("first", batches, False, False, loc_parts, q, numer)

    mix_far = [swap(a, g=h) if h else a for h in range(groups) for a in mix_x]
    n0, n1, *held = together(*numer, *x_near_across, *mix_far)
    numer, late, mix_far = [n0, n1], [], held[nx - 1 :]
    for kx, array in enumerate(held[: nx - 1]):
        some = [(r, 2 * kx + 2) for r in near_r]
        hold(array, some)
        hold(swap(array, m=1), odd_names(some))
        late += [some[i : i + 2] for i in range(0, len(some), 2)]
    late += [odd_names(some) for some in late]
    for some in late[:-1]:
        numer = chunk("second", [both(some)], False, False, loc_parts, q, numer)
    a0, a1 = chunk("last", [both(late[-1])], False, True, loc_parts, q, numer)

    wo_own = [mixing_projector, swap(mixing_projector, m=1)]
    wo_far = []
    for h in range(groups):
        some = list(mix_far[h * (nx - 1) : (h + 1) * (nx - 1)])
        wo_far += some + [swap(a, m=1) for a in some]
    w_mid = (premlp_rescaler.reshape(1, width), widening_matrix, narrowing_matrix)
    stream = (nucleotide_features, location_table, back.reshape(rows, width))

    def over_x(block):
        return [swap(block, m=2 * kx) for kx in range(1, nx)]

    def cores(blocks):
        return list(blocks) + [swap(a, m=1) for a in blocks]

    far0 = over_x(a0)
    part0 = mix_call(0, *stream, cores([a0]), wo_own)
    a1, part0, *far0 = together(a1, part0, *far0)
    far1 = over_x(a1)
    even0, odd0, share0 = mid_call(groups, mp, scal, part0, *w_mid, cores(far0), wo_far)
    even0, odd0, share0, *far1 = together(even0, odd0, share0, *far1)
    paired0 = even0.astype(f32) + swap(odd0, m=1).astype(f32)
    part1 = mix_call(rows // 2, *stream, cores([a1]), wo_own)
    part1, paired0 = together(part1, paired0)
    across0 = [swap(paired0[kx].astype(bf16), m=2 * kx) for kx in range(1, nx)]
    even1, odd1, share1 = mid_call(groups, mp, scal, part1, *w_mid, cores(far1), wo_far)
    even1, odd1, share1, *across0 = together(even1, odd1, share1, *across0)
    paired1 = even1.astype(f32) + swap(odd1, m=1).astype(f32)
    across1 = [swap(paired1[kx].astype(bf16), m=2 * kx) for kx in range(1, nx)]
    blocks = [
        0.5 * (share + paired[0] + sum(a.astype(f32) for a in arrived))
        for share, paired, arrived in ((share0, paired0, across0), (share1, paired1, across1))
    ]
    return jnp.concatenate(blocks, axis=0)


def solution(mesh):
    return jax.shard_map(
        shards,
        mesh=mesh,
        in_specs=(
            P(("groups", "seq"), None),
            P("seq", None),
            P(),
            P(None, None, "mp"),
            P(None, "mp"),
            P("mp"),
            P("mp", None),
            P(),
            P(None, "mp"),
            P("mp", None),
        ),
        out_specs=P(("groups", "seq"), "mp"),
        check_vma=False,
    )
```

```python
import functools

import jax
import jax.numpy as jnp
from jax import lax
from jax.experimental import pallas as pl
from jax.experimental.pallas import tpu as pltpu
from jax.sharding import PartitionSpec as P

epsilon = 1e-06
LOG2E = 1.4426950408889634
COST = 2**20
f32, bf16 = jnp.float32, jnp.bfloat16
AXES = ("groups", "seq", "mp")


def swap(block, g=0, s=0, m=0):
    groups, seq, mp = (lax.axis_size(name) for name in AXES)
    code = (g * seq + s) * mp + m
    return lax.ppermute(block, AXES, [(i, i ^ code) for i in range(groups * seq * mp)])


def unit(block):
    return block * lax.rsqrt(jnp.mean(block * block, axis=-1, keepdims=True) + epsilon)


def scaled_unit(block, scale):
    mean = jnp.mean(block * block, axis=-1, keepdims=True)
    return (block * (scale * lax.rsqrt(scale * scale * mean + epsilon))).astype(bf16)


def dot(a, b):
    return jnp.dot(a, b, preferred_element_type=f32)


def chunk_kernel(dims, batches, where, own, last, counts, scal, *refs):
    groups, seq, mp, heads, lookup, value_size, padded = dims
    nx = mp // 2
    strands = sorted({t for batch in batches for t, r, k in batch})
    refs = list(refs)
    take = lambda n: [refs.pop(0) for _ in range(n)]
    x_refs = take(counts[0])
    (own_loc,) = take(1)
    loc_refs = take(counts[1])
    flip_ref, sharp_ref, wk_ref, wv_ref = take(4)
    wq_ref = take(1)[0] if own else None
    q_refs = [] if own else take(len(strands))
    numer_in = [] if own else take(len(strands))
    out_refs = take(2 if last else len(strands))
    if own:
        q_refs = take(1)
        back_out = take(1)[0] if 1 in strands else None
    scratch = list(zip(refs[::2], refs[1::2]))
    here_m, here_g = scal[0], scal[1]
    part, width = own_loc.shape[1:]
    half = width // groups
    columns = [pl.ds(pl.multiple_of((h ^ here_g) * half, half), half) for h in range(groups)]

    def loc_piece(r, k, h):
        if r == 0:
            return own_loc[here_m ^ k, :, columns[h]]
        return loc_refs[k & 1][h * nx + (k >> 1), r - 1]

    products = []
    for batch, (streams, scales) in zip(batches, scratch):
        group = flip_ref.shape[0] // part
        backs = {}
        mirrored = [(r, k) for t, r, k in batch if t == 1]
        for n in range(0, len(mirrored), group):
            some = mirrored[n : n + group]
            for h in range(groups):
                pieces = [loc_piece(r ^ (seq - 1), k ^ (mp - 1), h) for r, k in reversed(some)]
                size = len(some) * part
                exchange = flip_ref[:size, group * part - size :]
                flipped = dot(exchange, jnp.concatenate(pieces, axis=0)).astype(bf16)
                for i, (r, k) in enumerate(some):
                    backs[r, k, h] = flipped[i * part : (i + 1) * part]
        for i, (t, r, k) in enumerate(batch):
            ref, at = (x_refs[0], here_m ^ k) if own else (x_refs[where[r, k][0]], where[r, k][1])
            place = here_m ^ k if own else i
            square = 0.0
            for h in range(groups):
                loc = backs[r, k, h] if t else loc_piece(r, k, h)
                if t and own:
                    back_out[place, :, columns[h]] = loc
                stream = ref[at, :, columns[h]] + loc
                streams[place, :, columns[h]] = stream
                square = square + jnp.sum(jnp.square(stream.astype(f32)), axis=-1, keepdims=True)
            scales[place] = jnp.broadcast_to(lax.rsqrt(square / width + epsilon), (part, 128))
        rows = streams[...].reshape(-1, width)
        scale = scales[...].reshape(-1, 128)
        if own:
            query = dot(rows, wq_ref[...])
            for h in range(heads):
                cols = slice(h * lookup, (h + 1) * lookup)
                q_refs[0][:, cols] = scaled_unit(query[:, cols], scale)
        products.append((scale, dot(rows, wk_ref[...]), dot(rows, wv_ref[...])))
    for p, t in enumerate(strands):
        mine = []
        for batch, product in zip(batches, products):
            places = [i for i, item in enumerate(batch) if item[0] == t]
            if places:
                rows = slice(places[0] * part, (places[-1] + 1) * part)
                mine.append([a[rows] for a in product])
        attended = []
        for h in range(heads):
            cols = slice(h * lookup, (h + 1) * lookup)
            key_n = jnp.concatenate([scaled_unit(k[:, cols], scale) for scale, k, v in mine], axis=0)
            value_h = []
            for c in range(padded // 128):
                block = slice(h * padded + c * 128, h * padded + (c + 1) * 128)
                column = jnp.concatenate([v[:, block] * scale for scale, k, v in mine], axis=0)
                if c == value_size // 128:
                    lane = lax.broadcasted_iota(jnp.int32, column.shape, 1)
                    column = jnp.where(lane == value_size % 128, 1.0, column)
                value_h.append(column.astype(bf16))
            value_h = jnp.concatenate(value_h, axis=1)
            scores = lax.dot_general(
                q_refs[p][:, cols], key_n, (((1,), (1,)), ((), ())), preferred_element_type=f32
            )
            weight = jnp.exp2(scores * (sharp_ref[h] * (LOG2E / lookup))).astype(bf16)
            numer = dot(weight, value_h)
            if not own:
                numer = numer + numer_in[p][h]
            if last:
                attended.append(numer[:, :value_size] / numer[:, value_size : value_size + 1])
            else:
                out_refs[p][h] = numer
        if last:
            attended = jnp.concatenate(attended, axis=1).astype(bf16)
            block = attended.shape[0] // len(out_refs)
            for i, out_ref in enumerate(out_refs):
                out_ref[p] = attended[i * block : (i + 1) * block]


VMEM = pl.BlockSpec(memory_space=pltpu.VMEM)
SMEM = pl.BlockSpec(memory_space=pltpu.SMEM)


def chunk_call(name, dims, batches, own, last, scal, x_parts, own_loc, loc_parts, flip, sharp, weights, q, numer):
    groups, seq, mp, heads, lookup, value_size, padded = dims
    _, part, width = own_loc.shape
    rows = part * mp
    batches = tuple(tuple(sorted(batch)) for batch in batches)
    strands = sorted({t for batch in batches for t, r, k in batch})
    where = {name: (n, i) for n, (_, names) in enumerate(x_parts) for name, i in names.items()}
    args = [a for a, _ in x_parts] + [own_loc] + list(loc_parts) + [flip, sharp] + list(weights) + list(q) + list(numer)
    specs = [SMEM if a is sharp else VMEM for a in args]
    if last:
        outs = [jax.ShapeDtypeStruct((2, rows // 2, heads * value_size), bf16)] * 2
    else:
        outs = [jax.ShapeDtypeStruct((heads, rows, padded), f32)] * len(strands)
    if own:
        outs = outs + [jax.ShapeDtypeStruct((rows, heads * lookup), bf16)]
        if 1 in strands:
            outs = outs + [jax.ShapeDtypeStruct((mp, part, width), bf16)]
    scratch = []
    for batch in batches:
        scratch += [pltpu.VMEM((len(batch), part, width), bf16), pltpu.VMEM((len(batch), part, 128), f32)]
    return pl.pallas_call(
        functools.partial(chunk_kernel, dims, batches, where, own, last, (len(x_parts), len(loc_parts))),
        out_shape=outs,
        in_specs=[SMEM] + specs,
        out_specs=[VMEM] * len(outs),
        scratch_shapes=scratch,
        compiler_params=pltpu.CompilerParams(vmem_limit_bytes=40 * 2**20),
        cost_estimate=pl.CostEstimate(flops=COST, bytes_accessed=COST, transcendentals=0),
        name=name,
    )(scal, *args)


def mix_kernel(lo, x_ref, loc_ref, back_ref, att0, att1, wo0, wo1, out_ref):
    rows = out_ref.shape[1]
    mixed = dot(att0[...].reshape(2 * rows, -1), wo0[...]) + dot(att1[...].reshape(2 * rows, -1), wo1[...])
    x_f = x_ref[lo : lo + rows].astype(f32)
    for t, loc in enumerate((loc_ref, back_ref)):
        out_ref[t] = x_f + loc[lo : lo + rows].astype(f32) + mixed[t * rows : (t + 1) * rows]


def mix_call(lo, x, loc, back, att, wo):
    rows, width = att[0].shape[1], x.shape[1]
    return pl.pallas_call(
        functools.partial(mix_kernel, lo),
        out_shape=jax.ShapeDtypeStruct((2, rows, width), f32),
        in_specs=[VMEM] * 7,
        out_specs=VMEM,
        compiler_params=pltpu.CompilerParams(vmem_limit_bytes=32 * 2**20),
        cost_estimate=pl.CostEstimate(
            flops=8 * rows * width * wo[0].shape[0], bytes_accessed=8 * 2**20, transcendentals=0
        ),
        name="mix",
    )(x, loc, back, *att, *wo)


def mid_kernel(groups, scal, *refs):
    partial, gain_ref, w1_ref, w2_ref, *refs = refs
    even_out, odd_out, middle_out, summed, mixed = refs[-5:]
    refs = refs[:-5]
    att, wo = refs[: len(refs) // (1 + groups)], refs[len(refs) // (1 + groups) :]
    here_m, here_g = scal[0], scal[1]
    rows = partial.shape[1]
    half = partial.shape[2] // groups
    blocks = [a_ref[...].reshape(2 * rows, -1) for a_ref in att]
    for h in range(groups):
        columns = pl.ds(pl.multiple_of((h ^ here_g) * half, half), half)
        part = partial[:, :, columns].reshape(2 * rows, half)
        mixed[:, columns] = part + sum(dot(a, w[...]) for a, w in zip(blocks, wo[h * len(att) : (h + 1) * len(att)]))
    middle = mixed[...]
    normed = (unit(middle) * gain_ref[...]).astype(bf16)
    expanded = jax.nn.gelu(dot(normed, w1_ref[...]), approximate=True).astype(bf16)
    out = dot(expanded, w2_ref[...])
    out = out[:rows] + out[rows:]
    both = middle[:rows] + middle[rows:]
    mp, _, share = summed.shape
    for j in range(mp):
        summed[j] = out[:, j * share : (j + 1) * share].astype(bf16)
    for k in range(mp):
        (odd_out if k & 1 else even_out)[k >> 1] = summed[here_m ^ k]
    for j in range(mp):
        block = both[:, j * share : (j + 1) * share]

        @pl.when(here_m == j)
        def _():
            middle_out[...] = block


def mid_call(groups, mp, scal, partial, gain, w1, w2, att, wo):
    _, rows, width = partial.shape
    share = width // mp
    args = [partial, gain, w1, w2, *att, *wo]
    return pl.pallas_call(
        functools.partial(mid_kernel, groups),
        out_shape=[jax.ShapeDtypeStruct((mp // 2, rows, share), bf16)] * 2 + [jax.ShapeDtypeStruct((rows, share), f32)],
        in_specs=[SMEM] + [VMEM] * len(args),
        out_specs=[VMEM] * 3,
        scratch_shapes=[pltpu.VMEM((mp, rows, share), bf16), pltpu.VMEM((2 * rows, width), f32)],
        compiler_params=pltpu.CompilerParams(vmem_limit_bytes=40 * 2**20),
        cost_estimate=pl.CostEstimate(
            flops=4 * rows * width * (width // 2 + 2 * w1.shape[1]),
            bytes_accessed=14 * 2**20,
            transcendentals=2 * rows * w1.shape[1],
        ),
        name="middle",
    )(scal, *args)


def cut_kernel(groups, scal, loc_ref, mix_ref, x_ref, loc_out, mix_out, mine_out, x_out, sems):
    here_m, here_g = scal[0], scal[1]
    half = loc_out.shape[1]
    columns = pl.ds(pl.multiple_of(here_g * half, half), half)
    copies = [
        pltpu.make_async_copy(loc_ref.at[here_m, :, columns], loc_out, sems.at[0]),
        pltpu.make_async_copy(mix_ref.at[:, columns], mix_out, sems.at[1]),
        pltpu.make_async_copy(x_ref.at[pl.ds(here_m, 1)], mine_out, sems.at[2]),
    ]
    for kx in range(x_out.shape[0]):
        copies.append(pltpu.make_async_copy(x_ref.at[here_m ^ (2 * kx)], x_out.at[kx], sems.at[3 + kx]))
    for copy in copies:
        copy.start()
    for copy in copies:
        copy.wait()


def cut_call(groups, scal, loc, mix, x):
    mp, part, width = x.shape
    outs = [(part, width // groups), (mix.shape[0], width // groups), (1, part, width), (mp // 2, part, width)]
    return pl.pallas_call(
        functools.partial(cut_kernel, groups),
        out_shape=[jax.ShapeDtypeStruct(shape, bf16) for shape in outs],
        in_specs=[SMEM] + [pl.BlockSpec(memory_space=pl.ANY)] * 3,
        out_specs=[VMEM] * 4,
        scratch_shapes=[pltpu.SemaphoreType.DMA((3 + mp // 2,))],
        compiler_params=pltpu.CompilerParams(vmem_limit_bytes=16 * 2**20),
        cost_estimate=pl.CostEstimate(flops=COST, bytes_accessed=COST, transcendentals=0),
        name="cut",
    )(scal, loc, mix, x)


def stack_kernel(*refs):
    for i, ref in enumerate(refs[:-1]):
        refs[-1][i] = ref[...]


def stack_call(arrays):
    shape = (len(arrays),) + arrays[0].shape
    return pl.pallas_call(
        stack_kernel,
        out_shape=jax.ShapeDtypeStruct(shape, arrays[0].dtype),
        in_specs=[VMEM] * len(arrays),
        out_specs=VMEM,
        compiler_params=pltpu.CompilerParams(vmem_limit_bytes=40 * 2**20),
        cost_estimate=pl.CostEstimate(flops=COST, bytes_accessed=COST, transcendentals=0),
        name="stack",
    )(*arrays)


def together(*arrays):
    return lax.optimization_barrier(arrays)


def shards(
    nucleotide_features,
    location_table,
    premix_rescaler,
    probe_lookup_matrices,
    payload_projector,
    logit_sharpness,
    mixing_projector,
    premlp_rescaler,
    widening_matrix,
    narrowing_matrix,
):
    rows, width = nucleotide_features.shape
    heads = logit_sharpness.shape[0]
    lookup = probe_lookup_matrices.shape[2] // heads
    value_size = payload_projector.shape[1] // heads
    padded = (value_size // 128 + 1) * 128
    groups, seq, mp = (lax.axis_size(name) for name in AXES)
    here_g, here_m = lax.axis_index("groups"), lax.axis_index("mp")
    nx = mp // 2
    part, half = rows // mp, width // groups
    dims = (groups, seq, mp, heads, lookup, value_size, padded)
    scal = jnp.stack([here_m, here_g]).astype(jnp.int32)
    x_own = nucleotide_features.reshape(mp, part, width)
    loc_own = location_table.reshape(mp, part, width)

    flip = jnp.flip(jnp.eye(2 * part, dtype=bf16), 0)
    gain = premix_rescaler.reshape(width, 1)
    wq, wk = [(gain * w.astype(f32)).astype(bf16) for w in (probe_lookup_matrices[0], probe_lookup_matrices[1])]
    wv = (gain * payload_projector.astype(f32)).astype(bf16).reshape(width, heads, value_size)
    wv = jnp.pad(wv, ((0, 0), (0, 0), (0, padded - value_size))).reshape(width, heads * padded)

    have = {}

    def hold(array, names):
        have.update({name: (array, i) for i, name in enumerate(names)})

    def chunk(name, batches, own, last, loc_parts, q=(), numer=()):
        weights = (wk, wv, wq) if own else (wk, wv)
        x_parts = {}
        for r, k in sorted({item[1:] for batch in batches for item in batch}):
            array, i = have[r, k]
            x_parts.setdefault(id(array), (array, {}))[1][r, k] = i
        return chunk_call(
            name, dims, batches, own, last, scal, list(x_parts.values()), loc_own, loc_parts,
            flip, logit_sharpness, weights, q, numer,
        )

    direct = range(3, seq, 2)
    loc_part, mix_part, x_mine, x_near = cut_call(groups, scal, loc_own, mixing_projector, x_own)
    mix_x = [swap(mix_part, m=2 * kx) for kx in range(1, nx)]
    loc_z = [swap(loc_part, s=r) for r in range(1, seq)]

    x_mine, x_near, *held = together(x_mine, x_near, *loc_z, *mix_x)
    loc_z, mix_x = held[: seq - 1], held[seq - 1 :]
    loc_far = stack_call(loc_z)
    x_direct = [swap(x_mine, s=r) for r in direct]
    combos = [(h, kx) for h in range(groups) for kx in range(nx)]
    loc_xy = [swap(loc_far, g=h, m=2 * kx) for h, kx in combos if (h, kx) != (0, 0)]
    x_near = swap(x_near, s=1)
    held = together(*loc_xy[:-1], *x_direct)
    loc_xy, x_direct = [*held[: len(combos) - 2], loc_xy[-1]], held[len(combos) - 2 :]
    x_relayed = [swap(a, s=1) for a in x_direct]
    x_across = [swap(a, m=2 * kx) for a in x_direct for kx in range(1, nx)]
    hold(x_own, [(0, k) for k in range(mp)])
    numer0, q0 = chunk("own_forward", [[(0, 0, k) for k in range(mp)]], True, False, [])

    held = together(numer0, loc_far, *loc_xy, x_near, *x_relayed, *x_direct, *x_across)
    numer0, loc_even, held = held[0], stack_call(held[1 : 1 + len(combos)]), list(held[1 + len(combos) :])
    loc_odd = swap(loc_even, m=1)
    x_late = [swap(a, m=2 * kx) for a in held[1 : 1 + len(direct)] for kx in range(1, nx)]
    names = [[(1, 2 * kx) for kx in range(nx)]] + [[(r - 1, 0)] for r in direct] + [[(r, 0)] for r in direct]
    names += [[(r, 2 * kx)] for r in direct for kx in range(1, nx)]
    odd_names = lambda names: [(r, k + 1) for r, k in names]
    for array, some in zip(held, names):
        hold(array, some)
    early = sorted(name for some in names for name in some)
    early = [early[i : i + 5] for i in range(0, len(early), 5)]
    for some in early:
        (numer0,) = chunk("even_forward", [[(0, r, k) for r, k in some]], False, False, [loc_even], [q0], [numer0])
    numer0, loc_odd, *held = together(numer0, loc_odd, *held, *mix_x)
    for array, some in zip(held, names):
        hold(swap(array, m=1), odd_names(some))
    mix_far = [swap(a, g=h) if h else a for h in range(groups) for a in held[len(names) :]]
    loc_parts = [loc_even, loc_odd]
    numer1, q1, back = chunk("own_back", [[(1, 0, k) for k in range(mp)]], True, False, loc_parts)
    numer1, *x_late = together(numer1, *x_late)
    names = [(r - 1, 2 * kx) for r in direct for kx in range(1, nx)]
    for name, array in zip(names, x_late):
        hold(array, [name])
        hold(swap(array, m=1), odd_names([name]))
    q, numer = [q0, q1], [numer0, numer1]
    both = lambda names: [(t, r, k) for t in range(2) for r, k in names]
    for some in early:
        batches = [[(1, r, k) for r, k in some], both(odd_names(some))]
        numer = chunk("first", batches, False, False, loc_parts, q, numer)
    n0, n1, *mix_far = together(*numer, *mix_far)
    numer = [n0, n1]
    wo_odd = [swap(a, m=1) for a in (mixing_projector, *mix_far)]
    late = [names[i : i + 2] for i in range(0, len(names), 2)]
    late = [both(some + odd_names(some)) for some in late]
    for some in late[:-1]:
        numer = chunk("second", [some], False, False, loc_parts, q, numer)
    a0, a1 = chunk("last", [late[-1]], False, True, loc_parts, q, numer)

    wo_own = [mixing_projector, wo_odd[0]]
    wo_far = []
    for h in range(groups):
        some = slice(h * (nx - 1), (h + 1) * (nx - 1))
        wo_far += [*mix_far[some], *wo_odd[1:][some]]
    w_mid = (premlp_rescaler.reshape(1, width), widening_matrix, narrowing_matrix)
    stream = (nucleotide_features, location_table, back.reshape(rows, width))

    def over_x(block):
        return [swap(block, m=2 * kx) for kx in range(1, nx)]

    def cores(blocks):
        return list(blocks) + [swap(a, m=1) for a in blocks]

    far0 = over_x(a0)
    part0 = mix_call(0, *stream, cores([a0]), wo_own)
    far1 = over_x(a1)
    part0, *far0 = together(part0, *far0)
    even0, odd0, share0 = mid_call(groups, mp, scal, part0, *w_mid, cores(far0), wo_far)
    even0, odd0, share0, *far1 = together(even0, odd0, share0, *far1)
    paired0 = even0.astype(f32) + swap(odd0, m=1).astype(f32)
    part1 = mix_call(rows // 2, *stream, cores([a1]), wo_own)
    part1, paired0 = together(part1, paired0)
    across0 = [swap(paired0[kx].astype(bf16), m=2 * kx) for kx in range(1, nx)]
    even1, odd1, share1 = mid_call(groups, mp, scal, part1, *w_mid, cores(far1), wo_far)
    even1, odd1, share1, *across0 = together(even1, odd1, share1, *across0)
    paired1 = even1.astype(f32) + swap(odd1, m=1).astype(f32)
    across1 = [swap(paired1[kx].astype(bf16), m=2 * kx) for kx in range(1, nx)]
    blocks = [
        0.5 * (share + paired[0] + sum(a.astype(f32) for a in arrived))
        for share, paired, arrived in ((share0, paired0, across0), (share1, paired1, across1))
    ]
    return jnp.concatenate(blocks, axis=0)


def solution(mesh):
    return jax.shard_map(
        shards,
        mesh=mesh,
        in_specs=(
            P(("groups", "seq"), None),
            P("seq", None),
            P(),
            P(None, None, "mp"),
            P(None, "mp"),
            P("mp"),
            P("mp", None),
            P(),
            P(None, "mp"),
            P("mp", None),
        ),
        out_specs=P(("groups", "seq"), "mp"),
        check_vma=False,
    )
```

```python
import functools

import jax
import jax.numpy as jnp
from jax import lax
from jax.experimental import pallas as pl
from jax.experimental.pallas import tpu as pltpu
from jax.sharding import PartitionSpec as P

epsilon = 1e-06
LOG2E = 1.4426950408889634
COST = 2**20
f32, bf16 = jnp.float32, jnp.bfloat16
AXES = ("groups", "seq", "mp")


def swap(block, g=0, s=0, m=0):
    groups, seq, mp = (lax.axis_size(name) for name in AXES)
    code = (g * seq + s) * mp + m
    return lax.ppermute(block, AXES, [(i, i ^ code) for i in range(groups * seq * mp)])


def unit(block):
    return block * lax.rsqrt(jnp.mean(block * block, axis=-1, keepdims=True) + epsilon)


def scaled_unit(block, scale):
    mean = jnp.mean(block * block, axis=-1, keepdims=True)
    return (block * (scale * lax.rsqrt(scale * scale * mean + epsilon))).astype(bf16)


def dot(a, b):
    return jnp.dot(a, b, preferred_element_type=f32)


def chunk_kernel(dims, batches, where, own, last, counts, scal, *refs):
    groups, seq, mp, heads, lookup, value_size, padded = dims
    nx = mp // 2
    strands = sorted({t for batch in batches for t, r, k in batch})
    refs = list(refs)
    take = lambda n: [refs.pop(0) for _ in range(n)]
    x_refs = take(counts[0])
    (own_loc,) = take(1)
    loc_refs = take(counts[1])
    flip_ref, sharp_ref, wk_ref, wv_ref = take(4)
    wq_ref = take(1)[0] if own else None
    q_refs = [] if own else take(len(strands))
    numer_in = [] if own else take(len(strands))
    out_refs = take(2 if last else len(strands))
    if own:
        q_refs = take(1)
        back_out = take(1)[0] if 1 in strands else None
    scratch = list(zip(refs[::2], refs[1::2]))
    here_m, here_g = scal[0], scal[1]
    part, width = own_loc.shape[1:]
    half = width // groups
    columns = [pl.ds(pl.multiple_of((h ^ here_g) * half, half), half) for h in range(groups)]

    def loc_piece(r, k, h):
        if r == 0:
            return own_loc[here_m ^ k, :, columns[h]]
        return loc_refs[k & 1][h * nx + (k >> 1), r - 1]

    products = []
    for batch, (streams, scales) in zip(batches, scratch):
        group = flip_ref.shape[0] // part
        backs = {}
        mirrored = [(r, k) for t, r, k in batch if t == 1]
        for n in range(0, len(mirrored), group):
            some = mirrored[n : n + group]
            for h in range(groups):
                pieces = [loc_piece(r ^ (seq - 1), k ^ (mp - 1), h) for r, k in reversed(some)]
                size = len(some) * part
                exchange = flip_ref[:size, group * part - size :]
                flipped = dot(exchange, jnp.concatenate(pieces, axis=0)).astype(bf16)
                for i, (r, k) in enumerate(some):
                    backs[r, k, h] = flipped[i * part : (i + 1) * part]
        for i, (t, r, k) in enumerate(batch):
            ref, at = (x_refs[0], here_m ^ k) if own else (x_refs[where[r, k][0]], where[r, k][1])
            place = here_m ^ k if own else i
            square = 0.0
            for h in range(groups):
                loc = backs[r, k, h] if t else loc_piece(r, k, h)
                if t and own:
                    back_out[place, :, columns[h]] = loc
                stream = ref[at, :, columns[h]] + loc
                streams[place, :, columns[h]] = stream
                square = square + jnp.sum(jnp.square(stream.astype(f32)), axis=-1, keepdims=True)
            scales[place] = jnp.broadcast_to(lax.rsqrt(square / width + epsilon), (part, 128))
        rows = streams[...].reshape(-1, width)
        scale = scales[...].reshape(-1, 128)
        if own:
            query = dot(rows, wq_ref[...])
            for h in range(heads):
                cols = slice(h * lookup, (h + 1) * lookup)
                q_refs[0][:, cols] = scaled_unit(query[:, cols], scale)
        products.append((scale, dot(rows, wk_ref[...]), dot(rows, wv_ref[...])))
    for p, t in enumerate(strands):
        mine = []
        for batch, product in zip(batches, products):
            places = [i for i, item in enumerate(batch) if item[0] == t]
            if places:
                rows = slice(places[0] * part, (places[-1] + 1) * part)
                mine.append([a[rows] for a in product])
        attended = []
        for h in range(heads):
            cols = slice(h * lookup, (h + 1) * lookup)
            key_n = jnp.concatenate([scaled_unit(k[:, cols], scale) for scale, k, v in mine], axis=0)
            value_h = []
            for c in range(padded // 128):
                block = slice(h * padded + c * 128, h * padded + (c + 1) * 128)
                column = jnp.concatenate([v[:, block] * scale for scale, k, v in mine], axis=0)
                if c == value_size // 128:
                    lane = lax.broadcasted_iota(jnp.int32, column.shape, 1)
                    column = jnp.where(lane == value_size % 128, 1.0, column)
                value_h.append(column.astype(bf16))
            value_h = jnp.concatenate(value_h, axis=1)
            scores = lax.dot_general(
                q_refs[p][:, cols], key_n, (((1,), (1,)), ((), ())), preferred_element_type=f32
            )
            weight = jnp.exp2(scores * (sharp_ref[h] * (LOG2E / lookup))).astype(bf16)
            numer = dot(weight, value_h)
            if not own:
                numer = numer + numer_in[p][h]
            if last:
                attended.append(numer[:, :value_size] / numer[:, value_size : value_size + 1])
            else:
                out_refs[p][h] = numer
        if last:
            attended = jnp.concatenate(attended, axis=1).astype(bf16)
            block = attended.shape[0] // len(out_refs)
            for i, out_ref in enumerate(out_refs):
                out_ref[p] = attended[i * block : (i + 1) * block]


VMEM = pl.BlockSpec(memory_space=pltpu.VMEM)
SMEM = pl.BlockSpec(memory_space=pltpu.SMEM)


def chunk_call(name, dims, batches, own, last, scal, x_parts, own_loc, loc_parts, flip, sharp, weights, q, numer):
    groups, seq, mp, heads, lookup, value_size, padded = dims
    _, part, width = own_loc.shape
    rows = part * mp
    batches = tuple(tuple(sorted(batch)) for batch in batches)
    strands = sorted({t for batch in batches for t, r, k in batch})
    where = {name: (n, i) for n, (_, names) in enumerate(x_parts) for name, i in names.items()}
    args = [a for a, _ in x_parts] + [own_loc] + list(loc_parts) + [flip, sharp] + list(weights) + list(q) + list(numer)
    specs = [SMEM if a is sharp else VMEM for a in args]
    if last:
        outs = [jax.ShapeDtypeStruct((2, rows // 2, heads * value_size), bf16)] * 2
    else:
        outs = [jax.ShapeDtypeStruct((heads, rows, padded), f32)] * len(strands)
    if own:
        outs = outs + [jax.ShapeDtypeStruct((rows, heads * lookup), bf16)]
        if 1 in strands:
            outs = outs + [jax.ShapeDtypeStruct((mp, part, width), bf16)]
    scratch = []
    for batch in batches:
        scratch += [pltpu.VMEM((len(batch), part, width), bf16), pltpu.VMEM((len(batch), part, 128), f32)]
    return pl.pallas_call(
        functools.partial(chunk_kernel, dims, batches, where, own, last, (len(x_parts), len(loc_parts))),
        out_shape=outs,
        in_specs=[SMEM] + specs,
        out_specs=[VMEM] * len(outs),
        scratch_shapes=scratch,
        compiler_params=pltpu.CompilerParams(vmem_limit_bytes=40 * 2**20),
        cost_estimate=pl.CostEstimate(flops=COST, bytes_accessed=COST, transcendentals=0),
        name=name,
    )(scal, *args)


def mix_kernel(lo, x_ref, loc_ref, back_ref, att0, att1, wo0, wo1, out_ref):
    rows = out_ref.shape[1]
    mixed = dot(att0[...].reshape(2 * rows, -1), wo0[...]) + dot(att1[...].reshape(2 * rows, -1), wo1[...])
    x_f = x_ref[lo : lo + rows].astype(f32)
    for t, loc in enumerate((loc_ref, back_ref)):
        out_ref[t] = x_f + loc[lo : lo + rows].astype(f32) + mixed[t * rows : (t + 1) * rows]


def mix_call(lo, x, loc, back, att, wo):
    rows, width = att[0].shape[1], x.shape[1]
    return pl.pallas_call(
        functools.partial(mix_kernel, lo),
        out_shape=jax.ShapeDtypeStruct((2, rows, width), f32),
        in_specs=[VMEM] * 7,
        out_specs=VMEM,
        compiler_params=pltpu.CompilerParams(vmem_limit_bytes=32 * 2**20),
        cost_estimate=pl.CostEstimate(
            flops=8 * rows * width * wo[0].shape[0], bytes_accessed=8 * 2**20, transcendentals=0
        ),
        name="mix",
    )(x, loc, back, *att, *wo)


def mid_kernel(groups, scal, *refs):
    partial, gain_ref, w1_ref, w2_ref, *refs = refs
    even_out, odd_out, middle_out, summed, mixed = refs[-5:]
    refs = refs[:-5]
    att, wo = refs[: len(refs) // (1 + groups)], refs[len(refs) // (1 + groups) :]
    here_m, here_g = scal[0], scal[1]
    rows = partial.shape[1]
    half = partial.shape[2] // groups
    blocks = [a_ref[...].reshape(2 * rows, -1) for a_ref in att]
    for h in range(groups):
        columns = pl.ds(pl.multiple_of((h ^ here_g) * half, half), half)
        part = partial[:, :, columns].reshape(2 * rows, half)
        mixed[:, columns] = part + sum(dot(a, w[...]) for a, w in zip(blocks, wo[h * len(att) : (h + 1) * len(att)]))
    middle = mixed[...]
    normed = (unit(middle) * gain_ref[...]).astype(bf16)
    expanded = jax.nn.gelu(dot(normed, w1_ref[...]), approximate=True).astype(bf16)
    out = dot(expanded, w2_ref[...])
    out = out[:rows] + out[rows:]
    both = middle[:rows] + middle[rows:]
    mp, _, share = summed.shape
    for j in range(mp):
        summed[j] = out[:, j * share : (j + 1) * share].astype(bf16)
    for k in range(mp):
        (odd_out if k & 1 else even_out)[k >> 1] = summed[here_m ^ k]
    for j in range(mp):
        block = both[:, j * share : (j + 1) * share]

        @pl.when(here_m == j)
        def _():
            middle_out[...] = block


def mid_call(groups, mp, scal, partial, gain, w1, w2, att, wo):
    _, rows, width = partial.shape
    share = width // mp
    args = [partial, gain, w1, w2, *att, *wo]
    return pl.pallas_call(
        functools.partial(mid_kernel, groups),
        out_shape=[jax.ShapeDtypeStruct((mp // 2, rows, share), bf16)] * 2 + [jax.ShapeDtypeStruct((rows, share), f32)],
        in_specs=[SMEM] + [VMEM] * len(args),
        out_specs=[VMEM] * 3,
        scratch_shapes=[pltpu.VMEM((mp, rows, share), bf16), pltpu.VMEM((2 * rows, width), f32)],
        compiler_params=pltpu.CompilerParams(vmem_limit_bytes=40 * 2**20),
        cost_estimate=pl.CostEstimate(
            flops=4 * rows * width * (width // 2 + 2 * w1.shape[1]),
            bytes_accessed=14 * 2**20,
            transcendentals=2 * rows * w1.shape[1],
        ),
        name="middle",
    )(scal, *args)


def cut_kernel(groups, scal, loc_ref, mix_ref, x_ref, loc_out, mix_out, mine_out, x_out, sems):
    here_m, here_g = scal[0], scal[1]
    half = loc_out.shape[1]
    columns = pl.ds(pl.multiple_of(here_g * half, half), half)
    copies = [
        pltpu.make_async_copy(loc_ref.at[here_m, :, columns], loc_out, sems.at[0]),
        pltpu.make_async_copy(mix_ref.at[:, columns], mix_out, sems.at[1]),
        pltpu.make_async_copy(x_ref.at[pl.ds(here_m, 1)], mine_out, sems.at[2]),
    ]
    for kx in range(x_out.shape[0]):
        copies.append(pltpu.make_async_copy(x_ref.at[here_m ^ (2 * kx)], x_out.at[kx], sems.at[3 + kx]))
    for copy in copies:
        copy.start()
    for copy in copies:
        copy.wait()


def cut_call(groups, scal, loc, mix, x):
    mp, part, width = x.shape
    outs = [(part, width // groups), (mix.shape[0], width // groups), (1, part, width), (mp // 2, part, width)]
    return pl.pallas_call(
        functools.partial(cut_kernel, groups),
        out_shape=[jax.ShapeDtypeStruct(shape, bf16) for shape in outs],
        in_specs=[SMEM] + [pl.BlockSpec(memory_space=pltpu.HBM)] * 3,
        out_specs=[VMEM] * 4,
        scratch_shapes=[pltpu.SemaphoreType.DMA((3 + mp // 2,))],
        compiler_params=pltpu.CompilerParams(vmem_limit_bytes=16 * 2**20),
        cost_estimate=pl.CostEstimate(flops=COST, bytes_accessed=COST, transcendentals=0),
        name="cut",
    )(scal, loc, mix, x)


def stack_kernel(*refs):
    for i, ref in enumerate(refs[:-1]):
        refs[-1][i] = ref[...]


def stack_call(arrays):
    shape = (len(arrays),) + arrays[0].shape
    return pl.pallas_call(
        stack_kernel,
        out_shape=jax.ShapeDtypeStruct(shape, arrays[0].dtype),
        in_specs=[VMEM] * len(arrays),
        out_specs=VMEM,
        compiler_params=pltpu.CompilerParams(vmem_limit_bytes=40 * 2**20),
        cost_estimate=pl.CostEstimate(flops=COST, bytes_accessed=COST, transcendentals=0),
        name="stack",
    )(*arrays)


def together(*arrays):
    return lax.optimization_barrier(arrays)


def shards(
    nucleotide_features,
    location_table,
    premix_rescaler,
    probe_lookup_matrices,
    payload_projector,
    logit_sharpness,
    mixing_projector,
    premlp_rescaler,
    widening_matrix,
    narrowing_matrix,
):
    rows, width = nucleotide_features.shape
    heads = logit_sharpness.shape[0]
    lookup = probe_lookup_matrices.shape[2] // heads
    value_size = payload_projector.shape[1] // heads
    padded = (value_size // 128 + 1) * 128
    groups, seq, mp = (lax.axis_size(name) for name in AXES)
    here_g, here_m = lax.axis_index("groups"), lax.axis_index("mp")
    nx = mp // 2
    part, half = rows // mp, width // groups
    dims = (groups, seq, mp, heads, lookup, value_size, padded)
    scal = jnp.stack([here_m, here_g]).astype(jnp.int32)
    x_own = nucleotide_features.reshape(mp, part, width)
    loc_own = location_table.reshape(mp, part, width)

    flip = jnp.flip(jnp.eye(2 * part, dtype=bf16), 0)
    gain = premix_rescaler.reshape(width, 1)
    wq, wk = [(gain * w.astype(f32)).astype(bf16) for w in (probe_lookup_matrices[0], probe_lookup_matrices[1])]
    wv = (gain * payload_projector.astype(f32)).astype(bf16).reshape(width, heads, value_size)
    wv = jnp.pad(wv, ((0, 0), (0, 0), (0, padded - value_size))).reshape(width, heads * padded)

    have = {}

    def hold(array, names):
        have.update({name: (array, i) for i, name in enumerate(names)})

    def chunk(name, batches, own, last, loc_parts, q=(), numer=()):
        flip, wq, wk, wv = prepared
        weights = (wk, wv, wq) if own else (wk, wv)
        x_parts = {}
        for r, k in sorted({item[1:] for batch in batches for item in batch}):
            array, i = have[r, k]
            x_parts.setdefault(id(array), (array, {}))[1][r, k] = i
        return chunk_call(
            name, dims, batches, own, last, scal, list(x_parts.values()), loc_own, loc_parts,
            flip, logit_sharpness, weights, q, numer,
        )

    direct = range(3, seq, 2)
    loc_part, mix_part, x_mine, x_near = cut_call(groups, scal, loc_own, mixing_projector, x_own)
    loc_z = [swap(loc_part, s=r) for r in range(1, seq)]
    mix_x = [swap(mix_part, m=2 * kx) for kx in range(1, nx)]

    x_mine, x_near, flip, wq, wk, wv, *held = together(x_mine, x_near, flip, wq, wk, wv, *loc_z, *mix_x)
    prepared = (flip, wq, wk, wv)
    loc_z, mix_x = held[: seq - 1], held[seq - 1 :]
    loc_far = stack_call(loc_z)
    x_direct = [swap(x_mine, s=r) for r in direct]
    combos = [(h, kx) for h in range(groups) for kx in range(nx)]
    loc_xy = [swap(loc_far, g=h, m=2 * kx) for h, kx in combos if (h, kx) != (0, 0)]
    x_near = swap(x_near, s=1)
    x_direct, mix_x, *held = together(x_direct, mix_x, *loc_xy[:-1])
    loc_xy = [*held, loc_xy[-1]]
    mix_far = [swap(a, g=h) if h else a for h in range(groups) for a in mix_x]
    x_relayed = [swap(a, s=1) for a in x_direct]
    x_across = [swap(a, m=2 * kx) for a in x_direct for kx in range(1, nx)]
    hold(x_own, [(0, k) for k in range(mp)])
    numer0, q0 = chunk("own_forward", [[(0, 0, k) for k in range(mp)]], True, False, [])

    x_relayed, numer0, *held = together(x_relayed, numer0, loc_far, *loc_xy, x_near, *x_direct, *x_across)
    loc_even, held = stack_call(held[: len(combos)]), held[len(combos) :]
    loc_odd = swap(loc_even, m=1)
    names = [[(1, 2 * kx) for kx in range(nx)]] + [[(r, 0)] for r in direct]
    names += [[(r, 2 * kx)] for r in direct for kx in range(1, nx)]
    odd_names = lambda names: [(r, k + 1) for r, k in names]
    both = lambda names: [(t, r, k) for t in range(2) for r, k in names]
    for array, some in zip(held, names):
        hold(array, some)
    early = [name for some in names for name in some]
    early = [early[i : i + 4] for i in range(0, len(early), 4)]
    for some in early:
        (numer0,) = chunk("even_forward", [[(0, r, k) for r, k in some]], False, False, [loc_even], [q0], [numer0])
    numer0, loc_odd, *held = together(numer0, loc_odd, *held, *x_relayed)
    relayed = [(r - 1, 0) for r in direct]
    for array, some in zip(held, names + [[name] for name in relayed]):
        hold(array, some)
        hold(swap(array, m=1), odd_names(some))
    x_relayed = held[len(names) :]
    x_late = [swap(a, m=2 * kx) for a in x_relayed for kx in range(1, nx)]
    loc_parts = [loc_even, loc_odd]
    numer1, q1, back = chunk("own_back", [[(1, 0, k) for k in range(mp)]], True, False, loc_parts)
    q, numer = [q0, q1], [numer0, numer1]
    rest = relayed
    for some in early:
        odd = odd_names(some)
        batches = [[(1, r, k) for r, k in some], both(odd[: len(odd) // 2])]
        numer = chunk("first", batches, False, False, loc_parts, q, numer)
        rest = rest + odd[len(odd) // 2 :]
    numer, *x_late = together(numer, *x_late)
    wo_odd = swap(mixing_projector, m=1)
    names = [(r - 1, 2 * kx) for r in direct for kx in range(1, nx)]
    for name, array in zip(names, x_late):
        hold(array, [name])
        hold(swap(array, m=1), odd_names([name]))
    rest = rest + odd_names(relayed)
    for some in [rest[i : i + 4] for i in range(0, len(rest), 4)]:
        batches = [both(some[: len(some) // 2]), both(some[len(some) // 2 :])]
        numer = chunk("second", batches, False, False, loc_parts, q, numer)
    numer, wo_odd = together(numer, wo_odd)
    late = [names[i : i + 2] for i in range(0, len(names), 2)]
    late = [both(some + odd_names(some)) for some in late]
    for some in late[:-1]:
        numer = chunk("third", [some], False, False, loc_parts, q, numer)
    a0, a1 = chunk("last", [late[-1]], False, True, loc_parts, q, numer)

    wo_own = [mixing_projector, wo_odd]
    w_mid = (premlp_rescaler.reshape(1, width), widening_matrix, narrowing_matrix)
    stream = (nucleotide_features, location_table, back.reshape(rows, width))

    def over_x(block):
        return [swap(block, m=2 * kx) for kx in range(1, nx)]

    def cores(blocks):
        return list(blocks) + [swap(a, m=1) for a in blocks]

    far0 = over_x(a0)
    part0 = mix_call(0, *stream, cores([a0]), wo_own)
    far1 = over_x(a1)
    part0, mix_far = together(part0, mix_far)
    wo_far = []
    for h in range(groups):
        some = mix_far[h * (nx - 1) : (h + 1) * (nx - 1)]
        wo_far += [*some, *(swap(a, m=1) for a in some)]
    part1 = mix_call(rows // 2, *stream, cores([a1]), wo_own)
    part0, part1, *far0 = together(part0, part1, *far0)
    even0, odd0, share0 = mid_call(groups, mp, scal, part0, *w_mid, cores(far0), wo_far)
    even0, odd0, share0, *far1 = together(even0, odd0, share0, *far1)
    paired0 = even0.astype(f32) + swap(odd0, m=1).astype(f32)
    part1, paired0 = together(part1, paired0)
    across0 = [swap(paired0[kx].astype(bf16), m=2 * kx) for kx in range(1, nx)]
    even1, odd1, share1 = mid_call(groups, mp, scal, part1, *w_mid, cores(far1), wo_far)
    even1, odd1, share1, *across0 = together(even1, odd1, share1, *across0)
    paired1 = even1.astype(f32) + swap(odd1, m=1).astype(f32)
    across1 = [swap(paired1[kx].astype(bf16), m=2 * kx) for kx in range(1, nx)]
    blocks = [
        0.5 * (share + paired[0] + sum(a.astype(f32) for a in arrived))
        for share, paired, arrived in ((share0, paired0, across0), (share1, paired1, across1))
    ]
    return jnp.concatenate(blocks, axis=0)


def solution(mesh):
    return jax.shard_map(
        shards,
        mesh=mesh,
        in_specs=(
            P(("groups", "seq"), None),
            P("seq", None),
            P(),
            P(None, None, "mp"),
            P(None, "mp"),
            P("mp"),
            P("mp", None),
            P(),
            P(None, "mp"),
            P("mp", None),
        ),
        out_specs=P(("groups", "seq"), "mp"),
        check_vma=False,
    )
```

```python
import functools

import jax
import jax.numpy as jnp
from jax import lax
from jax.experimental import pallas as pl
from jax.experimental.pallas import tpu as pltpu
from jax.sharding import PartitionSpec as P

epsilon = 1e-06
LOG2E = 1.4426950408889634
COST = 2**20
f32, bf16 = jnp.float32, jnp.bfloat16
AXES = ("groups", "seq", "mp")


def swap(block, g=0, s=0, m=0):
    groups, seq, mp = (lax.axis_size(name) for name in AXES)
    code = (g * seq + s) * mp + m
    return lax.ppermute(block, AXES, [(i, i ^ code) for i in range(groups * seq * mp)])


def unit(block):
    return block * lax.rsqrt(jnp.mean(block * block, axis=-1, keepdims=True) + epsilon)


def scaled_unit(block, scale):
    mean = jnp.mean(block * block, axis=-1, keepdims=True)
    return (block * (scale * lax.rsqrt(scale * scale * mean + epsilon))).astype(bf16)


def window(head, size):
    low = head * size // 128 * 128
    return low, (0 if head * size > low else size)


def dot(a, b):
    return jnp.dot(a, b, preferred_element_type=f32)


def chunk_kernel(dims, batches, where, own, last, counts, scal, *refs):
    groups, seq, mp, heads, lookup, value_size, padded = dims
    nx = mp // 2
    strands = sorted({t for batch in batches for t, r, k in batch})
    refs = list(refs)
    take = lambda n: [refs.pop(0) for _ in range(n)]
    x_refs = take(counts[0])
    (own_loc,) = take(1)
    loc_refs = take(counts[1])
    flip_ref, sharp_ref, wk_ref, wv_ref = take(4)
    wq_ref = take(1)[0] if own else None
    q_refs = [] if own else take(len(strands))
    numer_in = [] if own else take(len(strands))
    out_refs = take(2 if last else len(strands))
    if own:
        q_refs = take(1)
        back_out = take(1)[0] if 1 in strands else None
    scratch = list(zip(refs[::2], refs[1::2]))
    here_m, here_g = scal[0], scal[1]
    part, width = own_loc.shape[1:]
    half = width // groups
    columns = [pl.ds(pl.multiple_of((h ^ here_g) * half, half), half) for h in range(groups)]

    def loc_piece(r, k, h):
        if r == 0:
            return own_loc[here_m ^ k, :, columns[h]]
        return loc_refs[k & 1][h * nx + (k >> 1), r - 1]

    products = []
    for batch, (streams, scales) in zip(batches, scratch):
        group = flip_ref.shape[0] // part
        backs = {}
        mirrored = [(r, k) for t, r, k in batch if t == 1]
        for n in range(0, len(mirrored), group):
            some = mirrored[n : n + group]
            for h in range(groups):
                pieces = [loc_piece(r ^ (seq - 1), k ^ (mp - 1), h) for r, k in reversed(some)]
                size = len(some) * part
                exchange = flip_ref[:size, group * part - size :]
                flipped = dot(exchange, jnp.concatenate(pieces, axis=0)).astype(bf16)
                for i, (r, k) in enumerate(some):
                    backs[r, k, h] = flipped[i * part : (i + 1) * part]
        for i, (t, r, k) in enumerate(batch):
            ref, at = (x_refs[0], here_m ^ k) if own else (x_refs[where[r, k][0]], where[r, k][1])
            place = here_m ^ k if own else i
            square = 0.0
            for h in range(groups):
                loc = backs[r, k, h] if t else loc_piece(r, k, h)
                if t and own:
                    back_out[place, :, columns[h]] = loc
                stream = ref[at, :, columns[h]] + loc
                streams[place, :, columns[h]] = stream
                square = square + jnp.sum(jnp.square(stream.astype(f32)), axis=-1, keepdims=True)
            scales[place] = jnp.broadcast_to(lax.rsqrt(square / width + epsilon), (part, 128))
        rows = streams[...].reshape(-1, width)
        scale = scales[...].reshape(-1, 128)
        if own:
            query = dot(rows, wq_ref[...])
            for h in range(heads):
                cols = slice(h * lookup, (h + 1) * lookup)
                q_refs[0][:, cols] = scaled_unit(query[:, cols], scale)
        products.append((scale, dot(rows, wk_ref[...]), dot(rows, wv_ref[...])))
    for p, t in enumerate(strands):
        mine = []
        for batch, product in zip(batches, products):
            places = [i for i, item in enumerate(batch) if item[0] == t]
            if places:
                rows = slice(places[0] * part, (places[-1] + 1) * part)
                mine.append([a[rows] for a in product])
        attended = []
        for h in range(heads):
            cols = slice(h * lookup, (h + 1) * lookup)
            key_n = jnp.concatenate([scaled_unit(k[:, cols], scale) for scale, k, v in mine], axis=0)
            low, spare = window(h, value_size)
            value_h = []
            for c in range(padded // 128):
                block = slice(low + c * 128, low + (c + 1) * 128)
                column = jnp.concatenate([v[:, block] * scale for scale, k, v in mine], axis=0)
                if c == spare // 128:
                    lane = lax.broadcasted_iota(jnp.int32, column.shape, 1)
                    column = jnp.where(lane == spare % 128, 1.0, column)
                value_h.append(column.astype(bf16))
            value_h = jnp.concatenate(value_h, axis=1)
            scores = lax.dot_general(
                q_refs[p][:, cols], key_n, (((1,), (1,)), ((), ())), preferred_element_type=f32
            )
            weight = jnp.exp2(scores * (sharp_ref[h] * (LOG2E / lookup))).astype(bf16)
            numer = dot(weight, value_h)
            if not own:
                numer = numer + numer_in[p][h]
            if last:
                first = h * value_size - low
                attended.append(numer[:, first : first + value_size] / numer[:, spare : spare + 1])
            else:
                out_refs[p][h] = numer
        if last:
            attended = jnp.concatenate(attended, axis=1).astype(bf16)
            block = attended.shape[0] // len(out_refs)
            for i, out_ref in enumerate(out_refs):
                out_ref[p] = attended[i * block : (i + 1) * block]


VMEM = pl.BlockSpec(memory_space=pltpu.VMEM)
SMEM = pl.BlockSpec(memory_space=pltpu.SMEM)


def chunk_call(name, dims, batches, own, last, scal, x_parts, own_loc, loc_parts, flip, sharp, weights, q, numer):
    groups, seq, mp, heads, lookup, value_size, padded = dims
    _, part, width = own_loc.shape
    rows = part * mp
    batches = tuple(tuple(sorted(batch)) for batch in batches)
    strands = sorted({t for batch in batches for t, r, k in batch})
    where = {name: (n, i) for n, (_, names) in enumerate(x_parts) for name, i in names.items()}
    args = [a for a, _ in x_parts] + [own_loc] + list(loc_parts) + [flip, sharp] + list(weights) + list(q) + list(numer)
    specs = [SMEM if a is sharp else VMEM for a in args]
    if last:
        outs = [jax.ShapeDtypeStruct((2, rows // 2, heads * value_size), bf16)] * 2
    else:
        outs = [jax.ShapeDtypeStruct((heads, rows, padded), f32)] * len(strands)
    if own:
        outs = outs + [jax.ShapeDtypeStruct((rows, heads * lookup), bf16)]
        if 1 in strands:
            outs = outs + [jax.ShapeDtypeStruct((mp, part, width), bf16)]
    scratch = []
    for batch in batches:
        scratch += [pltpu.VMEM((len(batch), part, width), bf16), pltpu.VMEM((len(batch), part, 128), f32)]
    return pl.pallas_call(
        functools.partial(chunk_kernel, dims, batches, where, own, last, (len(x_parts), len(loc_parts))),
        out_shape=outs,
        in_specs=[SMEM] + specs,
        out_specs=[VMEM] * len(outs),
        scratch_shapes=scratch,
        compiler_params=pltpu.CompilerParams(vmem_limit_bytes=40 * 2**20),
        cost_estimate=pl.CostEstimate(flops=COST, bytes_accessed=COST, transcendentals=0),
        name=name,
    )(scal, *args)


def mix_kernel(lo, x_ref, loc_ref, back_ref, att0, att1, wo0, wo1, out_ref):
    rows = out_ref.shape[1]
    mixed = dot(att0[...].reshape(2 * rows, -1), wo0[...]) + dot(att1[...].reshape(2 * rows, -1), wo1[...])
    x_f = x_ref[lo : lo + rows].astype(f32)
    for t, loc in enumerate((loc_ref, back_ref)):
        out_ref[t] = x_f + loc[lo : lo + rows].astype(f32) + mixed[t * rows : (t + 1) * rows]


def mix_call(lo, x, loc, back, att, wo):
    rows, width = att[0].shape[1], x.shape[1]
    return pl.pallas_call(
        functools.partial(mix_kernel, lo),
        out_shape=jax.ShapeDtypeStruct((2, rows, width), f32),
        in_specs=[VMEM] * 7,
        out_specs=VMEM,
        compiler_params=pltpu.CompilerParams(vmem_limit_bytes=32 * 2**20),
        cost_estimate=pl.CostEstimate(
            flops=8 * rows * width * wo[0].shape[0], bytes_accessed=8 * 2**20, transcendentals=0
        ),
        name="mix",
    )(x, loc, back, *att, *wo)


def mid_kernel(groups, scal, *refs):
    partial, gain_ref, w1_ref, w2_ref, *refs = refs
    even_out, odd_out, middle_out, summed, mixed = refs[-5:]
    refs = refs[:-5]
    att, wo = refs[: len(refs) // (1 + groups)], refs[len(refs) // (1 + groups) :]
    here_m, here_g = scal[0], scal[1]
    rows = partial.shape[1]
    half = partial.shape[2] // groups
    blocks = [a_ref[...].reshape(2 * rows, -1) for a_ref in att]
    for h in range(groups):
        columns = pl.ds(pl.multiple_of((h ^ here_g) * half, half), half)
        part = partial[:, :, columns].reshape(2 * rows, half)
        mixed[:, columns] = part + sum(dot(a, w[...]) for a, w in zip(blocks, wo[h * len(att) : (h + 1) * len(att)]))
    middle = mixed[...]
    normed = (unit(middle) * gain_ref[...]).astype(bf16)
    expanded = jax.nn.gelu(dot(normed, w1_ref[...]), approximate=True).astype(bf16)
    out = dot(expanded, w2_ref[...])
    out = out[:rows] + out[rows:]
    both = middle[:rows] + middle[rows:]
    mp, _, share = summed.shape
    for j in range(mp):
        summed[j] = out[:, j * share : (j + 1) * share].astype(bf16)
    for k in range(mp):
        (odd_out if k & 1 else even_out)[k >> 1] = summed[here_m ^ k]
    for j in range(mp):
        block = both[:, j * share : (j + 1) * share]

        @pl.when(here_m == j)
        def _():
            middle_out[...] = block


def mid_call(groups, mp, scal, partial, gain, w1, w2, att, wo):
    _, rows, width = partial.shape
    share = width // mp
    args = [partial, gain, w1, w2, *att, *wo]
    return pl.pallas_call(
        functools.partial(mid_kernel, groups),
        out_shape=[jax.ShapeDtypeStruct((mp // 2, rows, share), bf16)] * 2 + [jax.ShapeDtypeStruct((rows, share), f32)],
        in_specs=[SMEM] + [VMEM] * len(args),
        out_specs=[VMEM] * 3,
        scratch_shapes=[pltpu.VMEM((mp, rows, share), bf16), pltpu.VMEM((2 * rows, width), f32)],
        compiler_params=pltpu.CompilerParams(vmem_limit_bytes=40 * 2**20),
        cost_estimate=pl.CostEstimate(
            flops=4 * rows * width * (width // 2 + 2 * w1.shape[1]),
            bytes_accessed=14 * 2**20,
            transcendentals=2 * rows * w1.shape[1],
        ),
        name="middle",
    )(scal, *args)


def stack_kernel(*refs):
    for i, ref in enumerate(refs[:-1]):
        refs[-1][i] = ref[...]


def stack_call(arrays):
    shape = (len(arrays),) + arrays[0].shape
    return pl.pallas_call(
        stack_kernel,
        out_shape=jax.ShapeDtypeStruct(shape, arrays[0].dtype),
        in_specs=[VMEM] * len(arrays),
        out_specs=VMEM,
        compiler_params=pltpu.CompilerParams(vmem_limit_bytes=40 * 2**20),
        cost_estimate=pl.CostEstimate(flops=COST, bytes_accessed=COST, transcendentals=0),
        name="stack",
    )(*arrays)


def together(*arrays):
    return lax.optimization_barrier(arrays)


def shards(
    nucleotide_features,
    location_table,
    premix_rescaler,
    probe_lookup_matrices,
    payload_projector,
    logit_sharpness,
    mixing_projector,
    premlp_rescaler,
    widening_matrix,
    narrowing_matrix,
):
    rows, width = nucleotide_features.shape
    heads = logit_sharpness.shape[0]
    lookup = probe_lookup_matrices.shape[2] // heads
    value_size = payload_projector.shape[1] // heads
    padded = (value_size // 128 + 1) * 128
    groups, seq, mp = (lax.axis_size(name) for name in AXES)
    here_g, here_m = lax.axis_index("groups"), lax.axis_index("mp")
    nx = mp // 2
    part, half = rows // mp, width // groups
    dims = (groups, seq, mp, heads, lookup, value_size, padded)
    scal = jnp.stack([here_m, here_g]).astype(jnp.int32)
    x_own = nucleotide_features.reshape(mp, part, width)
    loc_own = location_table.reshape(mp, part, width)

    place = lax.broadcasted_iota(jnp.int32, (2 * part, 2 * part), 0) + lax.broadcasted_iota(jnp.int32, (2 * part, 2 * part), 1)
    flip = (place == 2 * part - 1).astype(bf16)
    gain = premix_rescaler.reshape(width, 1)
    wq, wk = [(gain * w.astype(f32)).astype(bf16) for w in (probe_lookup_matrices[0], probe_lookup_matrices[1])]
    wv = (gain * payload_projector.astype(f32)).astype(bf16)
    wv = jnp.pad(wv, ((0, 0), (0, -wv.shape[1] % 128)))

    have = {}

    def hold(array, names):
        have.update({name: (array, i) for i, name in enumerate(names)})

    def chunk(name, batches, own, last, loc_parts, q=(), numer=()):
        flip, wq, wk, wv = prepared
        weights = (wk, wv, wq) if own else (wk, wv)
        x_parts = {}
        for r, k in sorted({item[1:] for batch in batches for item in batch}):
            array, i = have[r, k]
            x_parts.setdefault(id(array), (array, {}))[1][r, k] = i
        return chunk_call(
            name, dims, batches, own, last, scal, list(x_parts.values()), loc_own, loc_parts,
            flip, logit_sharpness, weights, q, numer,
        )

    direct = range(3, seq, 2)
    loc_part = lax.dynamic_slice(location_table, (here_m * part, here_g * half), (part, half))
    loc_part, mix_first, x_first = together(loc_part, mixing_projector, x_own)
    mix_part = lax.dynamic_slice_in_dim(mix_first, here_g * half, half, 1)
    mix_x = [swap(mix_part, m=2 * kx) for kx in range(1, nx)]
    loc_z = [swap(loc_part, s=r) for r in range(1, seq)]
    x_parts = [lax.dynamic_slice_in_dim(x_first, here_m ^ (2 * kx), 1, 0) for kx in range(nx)]
    x_near = [swap(x_parts[0], s=1)]

    x_near, x_parts, flip, wq, wk, wv, loc_z = together(x_near, x_parts, flip, wq, wk, wv, loc_z)
    prepared = (flip, wq, wk, wv)
    loc_far = stack_call(loc_z)
    x_direct = [swap(x_parts[0], s=r) for r in direct]
    loc_xy = [loc_far] + [swap(loc_far, m=2 * kx) for kx in range(1, nx)]
    loc_y = [swap(loc_far, g=h) for h in range(1, groups)]
    x_near = x_near + [swap(a, s=1) for a in x_parts[1:]]
    x_direct, x_near, mix_x, loc_xy, loc_y = together(x_direct, x_near, mix_x, loc_xy, loc_y)
    loc_xy = loc_xy + [a for h in range(1, groups) for a in (loc_y[h - 1], *(swap(a, g=h) for a in loc_xy[1:]))]
    mix_far = [swap(a, g=h) if h else a for h in range(groups) for a in mix_x]
    x_relayed = [swap(a, s=1) for a in x_direct]
    x_across = [swap(a, m=2 * kx) for a in x_direct for kx in range(1, nx)]
    hold(x_own, [(0, k) for k in range(mp)])
    numer0, q0 = chunk("own_forward", [[(0, 0, k) for k in range(mp)]], True, False, [])

    x_relayed, numer0, loc_xy, *held = together(x_relayed, numer0, loc_xy, *x_near, *x_direct, *x_across)
    loc_even = stack_call(loc_xy)
    loc_odd = swap(loc_even, m=1)
    names = [[(1, 2 * kx)] for kx in range(nx)] + [[(r, 0)] for r in direct]
    names += [[(r, 2 * kx)] for r in direct for kx in range(1, nx)]
    odd_names = lambda names: [(r, k + 1) for r, k in names]
    both = lambda names: [(t, r, k) for t in range(2) for r, k in names]
    for array, some in zip(held, names):
        hold(array, some)
    early = [name for some in names for name in some]
    early = [early[i : i + 4] for i in range(0, len(early), 4)]
    for some in early:
        (numer0,) = chunk("even_forward", [[(0, r, k) for r, k in some]], False, False, [loc_even], [q0], [numer0])
    numer0, loc_odd, *held = together(numer0, loc_odd, *held, *x_relayed)
    relayed = [(r - 1, 0) for r in direct]
    for array, some in zip(held, names + [[name] for name in relayed]):
        hold(array, some)
        hold(swap(array, m=1), odd_names(some))
    x_relayed = held[len(names) :]
    x_late = [swap(a, m=2 * kx) for a in x_relayed for kx in range(1, nx)]
    loc_parts = [loc_even, loc_odd]
    numer1, q1, back = chunk("own_back", [[(1, 0, k) for k in range(mp)]], True, False, loc_parts)
    q, numer = [q0, q1], [numer0, numer1]
    rest = relayed
    for some in early:
        odd = odd_names(some)
        batches = [[(1, r, k) for r, k in some], both(odd[: len(odd) // 2])]
        numer = chunk("first", batches, False, False, loc_parts, q, numer)
        rest = rest + odd[len(odd) // 2 :]
    numer, *x_late = together(numer, *x_late)
    wo_odd = swap(mixing_projector, m=1)
    names = [(r - 1, 2 * kx) for r in direct for kx in range(1, nx)]
    for name, array in zip(names, x_late):
        hold(array, [name])
        hold(swap(array, m=1), odd_names([name]))
    rest = rest + odd_names(relayed)
    for some in [rest[i : i + 4] for i in range(0, len(rest), 4)]:
        batches = [both(some[: len(some) // 2]), both(some[len(some) // 2 :])]
        numer = chunk("second", batches, False, False, loc_parts, q, numer)
    numer, wo_odd = together(numer, wo_odd)
    late = [names[i : i + 2] for i in range(0, len(names), 2)]
    late = [both(some + odd_names(some)) for some in late]
    for some in late[:-1]:
        numer = chunk("third", [some], False, False, loc_parts, q, numer)
    a0, a1 = chunk("last", [late[-1]], False, True, loc_parts, q, numer)

    wo_own = [mixing_projector, wo_odd]
    w_mid = (premlp_rescaler.reshape(1, width), widening_matrix, narrowing_matrix)
    stream = (nucleotide_features, location_table, back.reshape(rows, width))

    def over_x(block):
        return [swap(block, m=2 * kx) for kx in range(1, nx)]

    def cores(blocks):
        return list(blocks) + [swap(a, m=1) for a in blocks]

    far0 = over_x(a0)
    part0 = mix_call(0, *stream, cores([a0]), wo_own)
    far1 = over_x(a1)
    part0, mix_far = together(part0, mix_far)
    wo_far = []
    for h in range(groups):
        some = mix_far[h * (nx - 1) : (h + 1) * (nx - 1)]
        wo_far += [*some, *(swap(a, m=1) for a in some)]
    part1 = mix_call(rows // 2, *stream, cores([a1]), wo_own)
    part0, part1, *far0 = together(part0, part1, *far0)
    even0, odd0, share0 = mid_call(groups, mp, scal, part0, *w_mid, cores(far0), wo_far)
    even0, odd0, share0, *far1 = together(even0, odd0, share0, *far1)
    paired0 = even0.astype(f32) + swap(odd0, m=1).astype(f32)
    part1, paired0 = together(part1, paired0)
    across0 = [swap(paired0[kx].astype(bf16), m=2 * kx) for kx in range(1, nx)]
    even1, odd1, share1 = mid_call(groups, mp, scal, part1, *w_mid, cores(far1), wo_far)
    even1, odd1, share1, *across0 = together(even1, odd1, share1, *across0)
    paired1 = even1.astype(f32) + swap(odd1, m=1).astype(f32)
    across1 = [swap(paired1[kx].astype(bf16), m=2 * kx) for kx in range(1, nx)]
    blocks = [
        0.5 * (share + paired[0] + sum(a.astype(f32) for a in arrived))
        for share, paired, arrived in ((share0, paired0, across0), (share1, paired1, across1))
    ]
    return jnp.concatenate(blocks, axis=0)


def solution(mesh):
    return jax.shard_map(
        shards,
        mesh=mesh,
        in_specs=(
            P(("groups", "seq"), None),
            P("seq", None),
            P(),
            P(None, None, "mp"),
            P(None, "mp"),
            P("mp"),
            P("mp", None),
            P(),
            P(None, "mp"),
            P("mp", None),
        ),
        out_specs=P(("groups", "seq"), "mp"),
        check_vma=False,
    )
```

```python
import functools

import jax
import jax.numpy as jnp
from jax import lax
from jax.experimental import pallas as pl
from jax.experimental.pallas import tpu as pltpu
from jax.sharding import PartitionSpec as P

epsilon = 1e-06
LOG2E = 1.4426950408889634
COST = 2**20
f32, bf16 = jnp.float32, jnp.bfloat16
AXES = ("groups", "seq", "mp")


def swap(block, g=0, s=0, m=0):
    groups, seq, mp = (lax.axis_size(name) for name in AXES)
    code = (g * seq + s) * mp + m
    return lax.ppermute(block, AXES, [(i, i ^ code) for i in range(groups * seq * mp)])


def unit(block):
    return block * lax.rsqrt(jnp.mean(block * block, axis=-1, keepdims=True) + epsilon)


def scaled_unit(block, scale):
    mean = jnp.mean(block * block, axis=-1, keepdims=True)
    return (block * (scale * lax.rsqrt(scale * scale * mean + epsilon))).astype(bf16)


def window(head, size):
    low = head * size // 128 * 128
    return low, (0 if head * size > low else size)


def dot(a, b):
    return jnp.dot(a, b, preferred_element_type=f32)


def chunk_kernel(dims, batches, where, own, last, counts, scal, *refs):
    groups, seq, mp, heads, lookup, value_size, padded = dims
    nx = mp // 2
    strands = sorted({t for batch in batches for t, r, k in batch})
    refs = list(refs)
    take = lambda n: [refs.pop(0) for _ in range(n)]
    x_refs = take(counts[0])
    (own_loc,) = take(1)
    loc_refs = take(counts[1])
    flip_ref, sharp_ref, wk_ref, wv_ref = take(4)
    wq_ref = take(1)[0] if own else None
    q_refs = [] if own else take(len(strands))
    numer_in = [] if own else take(len(strands))
    out_refs = take(2 if last else len(strands))
    if own:
        q_refs = take(1)
        back_out = take(1)[0] if 1 in strands else None
    scratch = list(zip(refs[::2], refs[1::2]))
    here_m, here_g = scal[0], scal[1]
    part, width = own_loc.shape[1:]
    half = width // groups
    columns = [pl.ds(pl.multiple_of((h ^ here_g) * half, half), half) for h in range(groups)]

    def loc_piece(r, k, h):
        if r == 0:
            return own_loc[here_m ^ k, :, columns[h]]
        return loc_refs[k & 1][h * nx + (k >> 1), r - 1]

    products = []
    for batch, (streams, scales) in zip(batches, scratch):
        group = flip_ref.shape[0] // part
        backs = {}
        mirrored = [(r, k) for t, r, k in batch if t == 1]
        for n in range(0, len(mirrored), group):
            some = mirrored[n : n + group]
            for h in range(groups):
                pieces = [loc_piece(r ^ (seq - 1), k ^ (mp - 1), h) for r, k in reversed(some)]
                size = len(some) * part
                exchange = flip_ref[:size, group * part - size :]
                flipped = dot(exchange, jnp.concatenate(pieces, axis=0)).astype(bf16)
                for i, (r, k) in enumerate(some):
                    backs[r, k, h] = flipped[i * part : (i + 1) * part]
        for i, (t, r, k) in enumerate(batch):
            ref, at = (x_refs[0], here_m ^ k) if own else (x_refs[where[r, k][0]], where[r, k][1])
            place = here_m ^ k if own else i
            square = 0.0
            for h in range(groups):
                loc = backs[r, k, h] if t else loc_piece(r, k, h)
                if t and own:
                    back_out[place, :, columns[h]] = loc
                stream = ref[at, :, columns[h]] + loc
                streams[place, :, columns[h]] = stream
                square = square + jnp.sum(jnp.square(stream.astype(f32)), axis=-1, keepdims=True)
            scales[place] = jnp.broadcast_to(lax.rsqrt(square / width + epsilon), (part, 128))
        rows = streams[...].reshape(-1, width)
        scale = scales[...].reshape(-1, 128)
        if own:
            query = dot(rows, wq_ref[...])
            for h in range(heads):
                cols = slice(h * lookup, (h + 1) * lookup)
                q_refs[0][:, cols] = scaled_unit(query[:, cols], scale)
        products.append((scale, dot(rows, wk_ref[...]), dot(rows, wv_ref[...])))
    for p, t in enumerate(strands):
        mine = []
        for batch, product in zip(batches, products):
            places = [i for i, item in enumerate(batch) if item[0] == t]
            if places:
                rows = slice(places[0] * part, (places[-1] + 1) * part)
                mine.append([a[rows] for a in product])
        attended = []
        for h in range(heads):
            cols = slice(h * lookup, (h + 1) * lookup)
            key_n = jnp.concatenate([scaled_unit(k[:, cols], scale) for scale, k, v in mine], axis=0)
            low, spare = window(h, value_size)
            value_h = []
            for c in range(padded // 128):
                block = slice(low + c * 128, low + (c + 1) * 128)
                column = jnp.concatenate([v[:, block] * scale for scale, k, v in mine], axis=0)
                if c == spare // 128:
                    lane = lax.broadcasted_iota(jnp.int32, column.shape, 1)
                    column = jnp.where(lane == spare % 128, 1.0, column)
                value_h.append(column.astype(bf16))
            value_h = jnp.concatenate(value_h, axis=1)
            scores = lax.dot_general(
                q_refs[p][:, cols], key_n, (((1,), (1,)), ((), ())), preferred_element_type=f32
            )
            weight = jnp.exp2(scores * (sharp_ref[h] * (LOG2E / lookup))).astype(bf16)
            numer = dot(weight, value_h)
            if not own:
                numer = numer + numer_in[p][h]
            if last:
                first = h * value_size - low
                attended.append(numer[:, first : first + value_size] / numer[:, spare : spare + 1])
            else:
                out_refs[p][h] = numer
        if last:
            attended = jnp.concatenate(attended, axis=1).astype(bf16)
            block = attended.shape[0] // len(out_refs)
            for i, out_ref in enumerate(out_refs):
                out_ref[p] = attended[i * block : (i + 1) * block]


VMEM = pl.BlockSpec(memory_space=pltpu.VMEM)
SMEM = pl.BlockSpec(memory_space=pltpu.SMEM)


def chunk_call(name, dims, batches, own, last, scal, x_parts, own_loc, loc_parts, flip, sharp, weights, q, numer):
    groups, seq, mp, heads, lookup, value_size, padded = dims
    _, part, width = own_loc.shape
    rows = part * mp
    batches = tuple(tuple(sorted(batch)) for batch in batches)
    strands = sorted({t for batch in batches for t, r, k in batch})
    where = {name: (n, i) for n, (_, names) in enumerate(x_parts) for name, i in names.items()}
    args = [a for a, _ in x_parts] + [own_loc] + list(loc_parts) + [flip, sharp] + list(weights) + list(q) + list(numer)
    specs = [SMEM if a is sharp else VMEM for a in args]
    if last:
        outs = [jax.ShapeDtypeStruct((2, rows // 2, heads * value_size), bf16)] * 2
    else:
        outs = [jax.ShapeDtypeStruct((heads, rows, padded), f32)] * len(strands)
    if own:
        outs = outs + [jax.ShapeDtypeStruct((rows, heads * lookup), bf16)]
        if 1 in strands:
            outs = outs + [jax.ShapeDtypeStruct((mp, part, width), bf16)]
    scratch = []
    for batch in batches:
        scratch += [pltpu.VMEM((len(batch), part, width), bf16), pltpu.VMEM((len(batch), part, 128), f32)]
    return pl.pallas_call(
        functools.partial(chunk_kernel, dims, batches, where, own, last, (len(x_parts), len(loc_parts))),
        out_shape=outs,
        in_specs=[SMEM] + specs,
        out_specs=[VMEM] * len(outs),
        scratch_shapes=scratch,
        compiler_params=pltpu.CompilerParams(vmem_limit_bytes=40 * 2**20),
        cost_estimate=pl.CostEstimate(flops=COST, bytes_accessed=COST, transcendentals=0),
        name=name,
    )(scal, *args)


def mix_kernel(lo, x_ref, loc_ref, back_ref, att0, att1, wo0, wo1, out_ref):
    rows = out_ref.shape[1]
    mixed = dot(att0[...].reshape(2 * rows, -1), wo0[...]) + dot(att1[...].reshape(2 * rows, -1), wo1[...])
    x_f = x_ref[lo : lo + rows].astype(f32)
    for t, loc in enumerate((loc_ref, back_ref)):
        out_ref[t] = x_f + loc[lo : lo + rows].astype(f32) + mixed[t * rows : (t + 1) * rows]


def mix_call(lo, x, loc, back, att, wo):
    rows, width = att[0].shape[1], x.shape[1]
    return pl.pallas_call(
        functools.partial(mix_kernel, lo),
        out_shape=jax.ShapeDtypeStruct((2, rows, width), f32),
        in_specs=[VMEM] * 7,
        out_specs=VMEM,
        compiler_params=pltpu.CompilerParams(vmem_limit_bytes=32 * 2**20),
        cost_estimate=pl.CostEstimate(
            flops=COST, bytes_accessed=COST, transcendentals=0
        ),
        name="mix",
    )(x, loc, back, *att, *wo)


def mid_kernel(groups, scal, *refs):
    partial, gain_ref, w1_ref, w2_ref, *refs = refs
    even_out, odd_out, middle_out, summed, mixed = refs[-5:]
    refs = refs[:-5]
    att, wo = refs[: len(refs) // (1 + groups)], refs[len(refs) // (1 + groups) :]
    here_m, here_g = scal[0], scal[1]
    rows = partial.shape[1]
    half = partial.shape[2] // groups
    blocks = [a_ref[...].reshape(2 * rows, -1) for a_ref in att]
    for h in range(groups):
        columns = pl.ds(pl.multiple_of((h ^ here_g) * half, half), half)
        part = partial[:, :, columns].reshape(2 * rows, half)
        mixed[:, columns] = part + sum(dot(a, w[...]) for a, w in zip(blocks, wo[h * len(att) : (h + 1) * len(att)]))
    middle = mixed[...]
    normed = (unit(middle) * gain_ref[...]).astype(bf16)
    expanded = jax.nn.gelu(dot(normed, w1_ref[...]), approximate=True).astype(bf16)
    out = dot(expanded, w2_ref[...])
    out = out[:rows] + out[rows:]
    both = middle[:rows] + middle[rows:]
    mp, _, share = summed.shape
    for j in range(mp):
        summed[j] = out[:, j * share : (j + 1) * share].astype(bf16)
    for k in range(mp):
        (odd_out if k & 1 else even_out)[k >> 1] = summed[here_m ^ k]
    for j in range(mp):
        block = both[:, j * share : (j + 1) * share]

        @pl.when(here_m == j)
        def _():
            middle_out[...] = block


def mid_call(groups, mp, scal, partial, gain, w1, w2, att, wo):
    _, rows, width = partial.shape
    share = width // mp
    args = [partial, gain, w1, w2, *att, *wo]
    return pl.pallas_call(
        functools.partial(mid_kernel, groups),
        out_shape=[jax.ShapeDtypeStruct((mp // 2, rows, share), bf16)] * 2 + [jax.ShapeDtypeStruct((rows, share), f32)],
        in_specs=[SMEM] + [VMEM] * len(args),
        out_specs=[VMEM] * 3,
        scratch_shapes=[pltpu.VMEM((mp, rows, share), bf16), pltpu.VMEM((2 * rows, width), f32)],
        compiler_params=pltpu.CompilerParams(vmem_limit_bytes=40 * 2**20),
        cost_estimate=pl.CostEstimate(
            flops=COST,
            bytes_accessed=COST,
            transcendentals=0,
        ),
        name="middle",
    )(scal, *args)


def stack_kernel(*refs):
    for i, ref in enumerate(refs[:-1]):
        refs[-1][i] = ref[...]


def stack_call(arrays):
    shape = (len(arrays),) + arrays[0].shape
    return pl.pallas_call(
        stack_kernel,
        out_shape=jax.ShapeDtypeStruct(shape, arrays[0].dtype),
        in_specs=[VMEM] * len(arrays),
        out_specs=VMEM,
        compiler_params=pltpu.CompilerParams(vmem_limit_bytes=40 * 2**20),
        cost_estimate=pl.CostEstimate(flops=COST, bytes_accessed=COST, transcendentals=0),
        name="stack",
    )(*arrays)


def together(*arrays):
    return lax.optimization_barrier(arrays)


def shards(
    nucleotide_features,
    location_table,
    premix_rescaler,
    probe_lookup_matrices,
    payload_projector,
    logit_sharpness,
    mixing_projector,
    premlp_rescaler,
    widening_matrix,
    narrowing_matrix,
):
    rows, width = nucleotide_features.shape
    heads = logit_sharpness.shape[0]
    lookup = probe_lookup_matrices.shape[2] // heads
    value_size = payload_projector.shape[1] // heads
    padded = (value_size // 128 + 1) * 128
    groups, seq, mp = (lax.axis_size(name) for name in AXES)
    here_g, here_m = lax.axis_index("groups"), lax.axis_index("mp")
    nx = mp // 2
    part, half = rows // mp, width // groups
    dims = (groups, seq, mp, heads, lookup, value_size, padded)
    scal = jnp.stack([here_m, here_g]).astype(jnp.int32)
    x_own = nucleotide_features.reshape(mp, part, width)
    loc_own = location_table.reshape(mp, part, width)

    place = lax.broadcasted_iota(jnp.int32, (2 * part, 2 * part), 0) + lax.broadcasted_iota(jnp.int32, (2 * part, 2 * part), 1)
    flip = (place == 2 * part - 1).astype(bf16)
    gain = premix_rescaler.reshape(width, 1)
    wq, wk = [(gain * w.astype(f32)).astype(bf16) for w in (probe_lookup_matrices[0], probe_lookup_matrices[1])]
    wv = (gain * payload_projector.astype(f32)).astype(bf16)
    wv = jnp.pad(wv, ((0, 0), (0, -wv.shape[1] % 128)))

    have = {}

    def hold(array, names):
        have.update({name: (array, i) for i, name in enumerate(names)})

    def chunk(name, batches, own, last, loc_parts, q=(), numer=()):
        flip, wq, wk, wv = prepared
        weights = (wk, wv, wq) if own else (wk, wv)
        x_parts = {}
        for r, k in sorted({item[1:] for batch in batches for item in batch}):
            array, i = have[r, k]
            x_parts.setdefault(id(array), (array, {}))[1][r, k] = i
        return chunk_call(
            name, dims, batches, own, last, scal, list(x_parts.values()), loc_own, loc_parts,
            flip, logit_sharpness, weights, q, numer,
        )

    direct = range(3, seq, 2)
    loc_part = lax.dynamic_slice(location_table, (here_m * part, here_g * half), (part, half))
    loc_part, mix_first, x_first = together(loc_part, mixing_projector, x_own)
    mix_part = lax.dynamic_slice_in_dim(mix_first, here_g * half, half, 1)
    mix_x = [swap(mix_part, m=2 * kx) for kx in range(1, nx)]
    loc_z = [swap(loc_part, s=r) for r in range(1, seq)]
    x_mine = lax.dynamic_slice_in_dim(x_first, here_m, 1, 0)
    x_near = swap(x_mine, s=1)

    x_mine, flip, wq, wk, wv, loc_z = together(x_mine, flip, wq, wk, wv, loc_z)
    prepared = (flip, wq, wk, wv)
    loc_far = stack_call(loc_z)
    x_direct = [swap(x_mine, s=r) for r in direct]
    loc_xy = [loc_far] + [swap(loc_far, m=2 * kx) for kx in range(1, nx)]
    loc_y = [swap(loc_far, g=h) for h in range(1, groups)]
    x_direct, x_near, mix_x, loc_xy, loc_y = together(x_direct, x_near, mix_x, loc_xy, loc_y)
    x_late = [swap(x_near, m=2 * kx) for kx in range(1, nx)]
    loc_xy = loc_xy + [a for h in range(1, groups) for a in (loc_y[h - 1], *(swap(a, g=h) for a in loc_xy[1:]))]
    mix_far = [swap(a, g=h) if h else a for h in range(groups) for a in mix_x]
    x_relayed = [swap(a, s=1) for a in x_direct]
    x_across = [swap(a, m=2 * kx) for a in x_direct for kx in range(1, nx)]
    hold(x_own, [(0, k) for k in range(mp)])
    numer0, q0 = chunk("own_forward", [[(0, 0, k) for k in range(mp)]], True, False, [])

    numer0, loc_xy, x_late, *held = together(numer0, loc_xy, x_late, x_near, *x_relayed, *x_direct, *x_across)
    loc_even = stack_call(loc_xy)
    loc_odd = swap(loc_even, m=1)
    names = [[(1, 0)]] + [[(r - 1, 0)] for r in direct] + [[(r, 0)] for r in direct]
    names += [[(r, 2 * kx)] for r in direct for kx in range(1, nx)]
    odd_names = lambda names: [(r, k + 1) for r, k in names]
    both = lambda names: [(t, r, k) for t in range(2) for r, k in names]
    for array, some in zip(held, names):
        hold(array, some)
    early = [name for some in names for name in some]
    early = [early[i : i + 4] for i in range(0, len(early), 4)]
    for some in early:
        (numer0,) = chunk("even_forward", [[(0, r, k) for r, k in some]], False, False, [loc_even], [q0], [numer0])
    x_relayed = held[1 : 1 + len(direct)]
    x_late += [swap(a, m=2 * kx) for a in x_relayed for kx in range(1, nx)]
    late_names = [(r, 2 * kx) for r in [1] + [r - 1 for r in direct] for kx in range(1, nx)]
    numer0, loc_odd, *held = together(numer0, loc_odd, *held)
    for array, some in zip(held, names):
        hold(array, some)
        hold(swap(array, m=1), odd_names(some))
    loc_parts = [loc_even, loc_odd]
    numer1, q1, back = chunk("own_back", [[(1, 0, k) for k in range(mp)]], True, False, loc_parts)
    q, numer = [q0, q1], [numer0, numer1]
    for some in early:
        numer = chunk("first", [[(1, r, k) for r, k in some], both(odd_names(some))], False, False, loc_parts, q, numer)
    numer, *x_late = together(numer, *x_late)
    wo_odd = swap(mixing_projector, m=1)
    x_late_odd = [swap(a, m=1) for a in x_late]
    for name, array in zip(late_names, x_late):
        hold(array, [name])
    late = [late_names[i : i + 2] for i in range(0, len(late_names), 2)]
    for some in late:
        numer = chunk("third", [both(some)], False, False, loc_parts, q, numer)
    numer, mix_far, wo_odd, x_late_odd = together(numer, mix_far, wo_odd, x_late_odd)
    for name, array in zip(odd_names(late_names), x_late_odd):
        hold(array, [name])
    wo_far = []
    for h in range(groups):
        some = mix_far[h * (nx - 1) : (h + 1) * (nx - 1)]
        wo_far += [*some, *(swap(a, m=1) for a in some)]
    for some in late[:-1]:
        numer = chunk("fourth", [both(odd_names(some))], False, False, loc_parts, q, numer)
    a0, a1 = chunk("last", [both(odd_names(late[-1]))], False, True, loc_parts, q, numer)
    a0, a1, wo_far = together(a0, a1, wo_far)

    wo_own = [mixing_projector, wo_odd]
    w_mid = (premlp_rescaler.reshape(1, width), widening_matrix, narrowing_matrix)
    stream = (nucleotide_features, location_table, back.reshape(rows, width))

    def over_x(block):
        return [swap(block, m=2 * kx) for kx in range(1, nx)]

    def cores(blocks):
        return list(blocks) + [swap(a, m=1) for a in blocks]

    far0 = over_x(a0)
    part0 = mix_call(0, *stream, cores([a0]), wo_own)
    far1 = over_x(a1)
    part1 = mix_call(rows // 2, *stream, cores([a1]), wo_own)
    part0, part1, *far0 = together(part0, part1, *far0)
    even0, odd0, share0 = mid_call(groups, mp, scal, part0, *w_mid, cores(far0), wo_far)
    even0, odd0, share0, *far1 = together(even0, odd0, share0, *far1)
    paired0 = even0.astype(f32) + swap(odd0, m=1).astype(f32)
    part1, paired0 = together(part1, paired0)
    across0 = [swap(paired0[kx].astype(bf16), m=2 * kx) for kx in range(1, nx)]
    even1, odd1, share1 = mid_call(groups, mp, scal, part1, *w_mid, cores(far1), wo_far)
    even1, odd1, share1, *across0 = together(even1, odd1, share1, *across0)
    paired1 = even1.astype(f32) + swap(odd1, m=1).astype(f32)
    across1 = [swap(paired1[kx].astype(bf16), m=2 * kx) for kx in range(1, nx)]
    blocks = [
        0.5 * (share + paired[0] + sum(a.astype(f32) for a in arrived))
        for share, paired, arrived in ((share0, paired0, across0), (share1, paired1, across1))
    ]
    return jnp.concatenate(blocks, axis=0)


def solution(mesh):
    return jax.shard_map(
        shards,
        mesh=mesh,
        in_specs=(
            P(("groups", "seq"), None),
            P("seq", None),
            P(),
            P(None, None, "mp"),
            P(None, "mp"),
            P("mp"),
            P("mp", None),
            P(),
            P(None, "mp"),
            P("mp", None),
        ),
        out_specs=P(("groups", "seq"), "mp"),
        check_vma=False,
    )
```

```python
import functools

import jax
import jax.numpy as jnp
from jax import lax
from jax.experimental import pallas as pl
from jax.experimental.pallas import tpu as pltpu
from jax.sharding import PartitionSpec as P

epsilon = 1e-06
LOG2E = 1.4426950408889634
COST = 2**20
f32, bf16 = jnp.float32, jnp.bfloat16
AXES = ("groups", "seq", "mp")


def swap(block, g=0, s=0, m=0):
    groups, seq, mp = (lax.axis_size(name) for name in AXES)
    code = (g * seq + s) * mp + m
    return lax.ppermute(block, AXES, [(i, i ^ code) for i in range(groups * seq * mp)])


def unit(block):
    return block * lax.rsqrt(jnp.mean(block * block, axis=-1, keepdims=True) + epsilon)


def scaled_unit(block, scale):
    mean = jnp.mean(block * block, axis=-1, keepdims=True)
    return (block * (scale * lax.rsqrt(scale * scale * mean + epsilon))).astype(bf16)


def window(head, size):
    low = head * size // 128 * 128
    return low, (0 if head * size > low else size)


def dot(a, b):
    return jnp.dot(a, b, preferred_element_type=f32)


def chunk_kernel(dims, batches, where, own, last, counts, scal, *refs):
    groups, seq, mp, heads, lookup, value_size, padded = dims
    nx = mp // 2
    strands = sorted({t for batch in batches for t, r, k in batch})
    refs = list(refs)
    take = lambda n: [refs.pop(0) for _ in range(n)]
    x_refs = take(counts[0])
    (own_loc,) = take(1)
    loc_refs = take(counts[1])
    flip_ref, sharp_ref, wk_ref, wv_ref = take(4)
    wq_ref = take(1)[0] if own else None
    q_refs = [] if own else take(len(strands))
    numer_in = [] if own else take(len(strands))
    out_refs = take(2 if last else len(strands))
    if own:
        q_refs = take(1)
        back_out = take(1)[0] if 1 in strands else None
    scratch = list(zip(refs[::2], refs[1::2]))
    here_m, here_g = scal[0], scal[1]
    part, width = own_loc.shape[1:]
    half = width // groups
    columns = [pl.ds(pl.multiple_of((h ^ here_g) * half, half), half) for h in range(groups)]

    def loc_piece(r, k, h):
        if r == 0:
            return own_loc[here_m ^ k, :, columns[h]]
        return loc_refs[k & 1][h * nx + (k >> 1), r - 1]

    products = []
    for batch, (streams, scales) in zip(batches, scratch):
        group = flip_ref.shape[0] // part
        backs = {}
        mirrored = [(r, k) for t, r, k in batch if t == 1]
        for n in range(0, len(mirrored), group):
            some = mirrored[n : n + group]
            for h in range(groups):
                pieces = [loc_piece(r ^ (seq - 1), k ^ (mp - 1), h) for r, k in reversed(some)]
                size = len(some) * part
                exchange = flip_ref[:size, group * part - size :]
                flipped = dot(exchange, jnp.concatenate(pieces, axis=0)).astype(bf16)
                for i, (r, k) in enumerate(some):
                    backs[r, k, h] = flipped[i * part : (i + 1) * part]
        for i, (t, r, k) in enumerate(batch):
            ref, at = (x_refs[0], here_m ^ k) if own else (x_refs[where[r, k][0]], where[r, k][1])
            place = here_m ^ k if own else i
            square = 0.0
            for h in range(groups):
                loc = backs[r, k, h] if t else loc_piece(r, k, h)
                if t and own:
                    back_out[place, :, columns[h]] = loc
                stream = ref[at, :, columns[h]] + loc
                streams[place, :, columns[h]] = stream
                square = square + jnp.sum(jnp.square(stream.astype(f32)), axis=-1, keepdims=True)
            scales[place] = jnp.broadcast_to(lax.rsqrt(square / width + epsilon), (part, 128))
        rows = streams[...].reshape(-1, width)
        scale = scales[...].reshape(-1, 128)
        if own:
            query = dot(rows, wq_ref[...])
            for h in range(heads):
                cols = slice(h * lookup, (h + 1) * lookup)
                q_refs[0][:, cols] = scaled_unit(query[:, cols], scale)
        products.append((scale, dot(rows, wk_ref[...]), dot(rows, wv_ref[...])))
    for p, t in enumerate(strands):
        mine = []
        for batch, product in zip(batches, products):
            places = [i for i, item in enumerate(batch) if item[0] == t]
            if places:
                rows = slice(places[0] * part, (places[-1] + 1) * part)
                mine.append([a[rows] for a in product])
        attended = []
        for h in range(heads):
            cols = slice(h * lookup, (h + 1) * lookup)
            key_n = jnp.concatenate([scaled_unit(k[:, cols], scale) for scale, k, v in mine], axis=0)
            low, spare = window(h, value_size)
            value_h = []
            for c in range(padded // 128):
                block = slice(low + c * 128, low + (c + 1) * 128)
                column = jnp.concatenate([v[:, block] * scale for scale, k, v in mine], axis=0)
                if c == spare // 128:
                    lane = lax.broadcasted_iota(jnp.int32, column.shape, 1)
                    column = jnp.where(lane == spare % 128, 1.0, column)
                value_h.append(column.astype(bf16))
            value_h = jnp.concatenate(value_h, axis=1)
            scores = lax.dot_general(
                q_refs[p][:, cols], key_n, (((1,), (1,)), ((), ())), preferred_element_type=f32
            )
            weight = jnp.exp2(scores * (sharp_ref[h] * (LOG2E / lookup))).astype(bf16)
            numer = dot(weight, value_h)
            if not own:
                numer = numer + numer_in[p][h]
            if last:
                first = h * value_size - low
                attended.append(numer[:, first : first + value_size] / numer[:, spare : spare + 1])
            else:
                out_refs[p][h] = numer
        if last:
            attended = jnp.concatenate(attended, axis=1).astype(bf16)
            block = attended.shape[0] // len(out_refs)
            for i, out_ref in enumerate(out_refs):
                out_ref[p] = attended[i * block : (i + 1) * block]


VMEM = pl.BlockSpec(memory_space=pltpu.VMEM)
SMEM = pl.BlockSpec(memory_space=pltpu.SMEM)


def chunk_call(name, dims, batches, own, last, scal, x_parts, own_loc, loc_parts, flip, sharp, weights, q, numer):
    groups, seq, mp, heads, lookup, value_size, padded = dims
    _, part, width = own_loc.shape
    rows = part * mp
    batches = tuple(tuple(sorted(batch)) for batch in batches)
    strands = sorted({t for batch in batches for t, r, k in batch})
    where = {name: (n, i) for n, (_, names) in enumerate(x_parts) for name, i in names.items()}
    args = [a for a, _ in x_parts] + [own_loc] + list(loc_parts) + [flip, sharp] + list(weights) + list(q) + list(numer)
    specs = [SMEM if a is sharp else VMEM for a in args]
    if last:
        outs = [jax.ShapeDtypeStruct((2, rows // 2, heads * value_size), bf16)] * 2
    else:
        outs = [jax.ShapeDtypeStruct((heads, rows, padded), f32)] * len(strands)
    if own:
        outs = outs + [jax.ShapeDtypeStruct((rows, heads * lookup), bf16)]
        if 1 in strands:
            outs = outs + [jax.ShapeDtypeStruct((mp, part, width), bf16)]
    scratch = []
    for batch in batches:
        scratch += [pltpu.VMEM((len(batch), part, width), bf16), pltpu.VMEM((len(batch), part, 128), f32)]
    return pl.pallas_call(
        functools.partial(chunk_kernel, dims, batches, where, own, last, (len(x_parts), len(loc_parts))),
        out_shape=outs,
        in_specs=[SMEM] + specs,
        out_specs=[VMEM] * len(outs),
        scratch_shapes=scratch,
        compiler_params=pltpu.CompilerParams(vmem_limit_bytes=40 * 2**20),
        cost_estimate=pl.CostEstimate(flops=COST, bytes_accessed=COST, transcendentals=0),
        name=name,
    )(scal, *args)


def mix_kernel(lo, x_ref, loc_ref, back_ref, att0, att1, wo0, wo1, out_ref):
    rows = out_ref.shape[1]
    mixed = dot(att0[...].reshape(2 * rows, -1), wo0[...]) + dot(att1[...].reshape(2 * rows, -1), wo1[...])
    x_f = x_ref[lo : lo + rows].astype(f32)
    for t, loc in enumerate((loc_ref, back_ref)):
        out_ref[t] = x_f + loc[lo : lo + rows].astype(f32) + mixed[t * rows : (t + 1) * rows]


def mix_call(lo, x, loc, back, att, wo):
    rows, width = att[0].shape[1], x.shape[1]
    return pl.pallas_call(
        functools.partial(mix_kernel, lo),
        out_shape=jax.ShapeDtypeStruct((2, rows, width), f32),
        in_specs=[VMEM] * 7,
        out_specs=VMEM,
        compiler_params=pltpu.CompilerParams(vmem_limit_bytes=32 * 2**20),
        cost_estimate=pl.CostEstimate(
            flops=COST, bytes_accessed=COST, transcendentals=0
        ),
        name="mix",
    )(x, loc, back, *att, *wo)


def mid_kernel(groups, scal, *refs):
    partial, gain_ref, w1_ref, w2_ref, *refs = refs
    even_out, odd_out, middle_out, summed, mixed = refs[-5:]
    refs = refs[:-5]
    att, wo = refs[: len(refs) // (1 + groups)], refs[len(refs) // (1 + groups) :]
    here_m, here_g = scal[0], scal[1]
    rows = partial.shape[1]
    half = partial.shape[2] // groups
    middles, outs = [], []
    for t in range(2):
        blocks = [a_ref[t] for a_ref in att]
        mine = pl.ds(t * rows, rows)
        for h in range(groups):
            columns = pl.ds(pl.multiple_of((h ^ here_g) * half, half), half)
            products = [dot(a, w[...]) for a, w in zip(blocks, wo[h * len(att) : (h + 1) * len(att)])]
            mixed[mine, columns] = partial[t, :, columns] + sum(products)
        middle = mixed[mine, :]
        normed = (unit(middle) * gain_ref[...]).astype(bf16)
        expanded = jax.nn.gelu(dot(normed, w1_ref[...]), approximate=True).astype(bf16)
        outs.append(dot(expanded, w2_ref[...]))
        middles.append(middle)
    out = outs[0] + outs[1]
    both = middles[0] + middles[1]
    mp, _, share = summed.shape
    for j in range(mp):
        summed[j] = out[:, j * share : (j + 1) * share].astype(bf16)
    for k in range(mp):
        (odd_out if k & 1 else even_out)[k >> 1] = summed[here_m ^ k]
    for j in range(mp):
        block = both[:, j * share : (j + 1) * share]

        @pl.when(here_m == j)
        def _():
            middle_out[...] = block


def mid_call(groups, mp, scal, partial, gain, w1, w2, att, wo):
    _, rows, width = partial.shape
    share = width // mp
    args = [partial, gain, w1, w2, *att, *wo]
    return pl.pallas_call(
        functools.partial(mid_kernel, groups),
        out_shape=[jax.ShapeDtypeStruct((mp // 2, rows, share), bf16)] * 2 + [jax.ShapeDtypeStruct((rows, share), f32)],
        in_specs=[SMEM] + [VMEM] * len(args),
        out_specs=[VMEM] * 3,
        scratch_shapes=[pltpu.VMEM((mp, rows, share), bf16), pltpu.VMEM((2 * rows, width), f32)],
        compiler_params=pltpu.CompilerParams(vmem_limit_bytes=40 * 2**20),
        cost_estimate=pl.CostEstimate(
            flops=COST,
            bytes_accessed=COST,
            transcendentals=0,
        ),
        name="middle",
    )(scal, *args)


def stack_kernel(*refs):
    for i, ref in enumerate(refs[:-1]):
        refs[-1][i] = ref[...]


def stack_call(arrays):
    shape = (len(arrays),) + arrays[0].shape
    return pl.pallas_call(
        stack_kernel,
        out_shape=jax.ShapeDtypeStruct(shape, arrays[0].dtype),
        in_specs=[VMEM] * len(arrays),
        out_specs=VMEM,
        compiler_params=pltpu.CompilerParams(vmem_limit_bytes=40 * 2**20),
        cost_estimate=pl.CostEstimate(flops=COST, bytes_accessed=COST, transcendentals=0),
        name="stack",
    )(*arrays)


def together(*arrays):
    return lax.optimization_barrier(arrays)


def shards(
    nucleotide_features,
    location_table,
    premix_rescaler,
    probe_lookup_matrices,
    payload_projector,
    logit_sharpness,
    mixing_projector,
    premlp_rescaler,
    widening_matrix,
    narrowing_matrix,
):
    rows, width = nucleotide_features.shape
    heads = logit_sharpness.shape[0]
    lookup = probe_lookup_matrices.shape[2] // heads
    value_size = payload_projector.shape[1] // heads
    padded = (value_size // 128 + 1) * 128
    groups, seq, mp = (lax.axis_size(name) for name in AXES)
    here_g, here_m = lax.axis_index("groups"), lax.axis_index("mp")
    nx = mp // 2
    part, half = rows // mp, width // groups
    dims = (groups, seq, mp, heads, lookup, value_size, padded)
    scal = jnp.stack([here_m, here_g]).astype(jnp.int32)
    x_own = nucleotide_features.reshape(mp, part, width)
    loc_own = location_table.reshape(mp, part, width)

    place = lax.broadcasted_iota(jnp.int32, (2 * part, 2 * part), 0) + lax.broadcasted_iota(jnp.int32, (2 * part, 2 * part), 1)
    flip = (place == 2 * part - 1).astype(bf16)
    gain = premix_rescaler.reshape(width, 1)
    wq, wk = [(gain * w.astype(f32)).astype(bf16) for w in (probe_lookup_matrices[0], probe_lookup_matrices[1])]
    wv = (gain * payload_projector.astype(f32)).astype(bf16)
    wv = jnp.pad(wv, ((0, 0), (0, -wv.shape[1] % 128)))

    have = {}

    def hold(array, names):
        have.update({name: (array, i) for i, name in enumerate(names)})

    def chunk(name, batches, own, last, loc_parts, q=(), numer=()):
        flip, wq, wk, wv = prepared
        weights = (wk, wv, wq) if own else (wk, wv)
        x_parts = {}
        for r, k in sorted({item[1:] for batch in batches for item in batch}):
            array, i = have[r, k]
            x_parts.setdefault(id(array), (array, {}))[1][r, k] = i
        return chunk_call(
            name, dims, batches, own, last, scal, list(x_parts.values()), loc_own, loc_parts,
            flip, logit_sharpness, weights, q, numer,
        )

    direct = range(3, seq, 2)
    loc_part = lax.dynamic_slice(location_table, (here_m * part, here_g * half), (part, half))
    loc_part, mix_first, x_first = together(loc_part, mixing_projector, x_own)
    mix_part = lax.dynamic_slice_in_dim(mix_first, here_g * half, half, 1)
    loc_z = [swap(loc_part, s=r) for r in range(1, seq)]
    mix_x = [swap(mix_part, m=2 * kx) for kx in range(1, nx)]
    x_mine = lax.dynamic_slice_in_dim(x_first, here_m, 1, 0)

    x_mine, flip, wq, wk, wv, loc_z = together(x_mine, flip, wq, wk, wv, loc_z)
    prepared = (flip, wq, wk, wv)
    loc_far = stack_call(loc_z)
    x_direct = [swap(x_mine, s=r) for r in direct]
    loc_xy = [loc_far] + [swap(loc_far, m=2 * kx) for kx in range(1, nx)]
    loc_y = [swap(loc_far, g=h) for h in range(1, groups)]
    x_direct, x_mine, mix_x, loc_y = together(x_direct, x_mine, mix_x, loc_y)
    loc_xy = loc_xy + [a for h in range(1, groups) for a in (loc_y[h - 1], *(swap(a, g=h) for a in loc_xy[1:]))]
    x_relayed = [swap(a, s=1) for a in x_direct]
    x_near = swap(x_mine, s=1)
    x_across = [swap(a, m=2 * kx) for a in x_direct for kx in range(1, nx)]
    hold(x_own, [(0, k) for k in range(mp)])
    numer0, q0 = chunk("own_forward", [[(0, 0, k) for k in range(mp)]], True, False, [])

    numer0, loc_xy, x_near, *held = together(numer0, loc_xy, x_near, *x_relayed, *x_direct, *x_across)
    loc_even = stack_call(loc_xy)
    loc_odd = swap(loc_even, m=1)
    names = [[(r - 1, 0)] for r in direct] + [[(r, 0)] for r in direct]
    names += [[(r, 2 * kx)] for r in direct for kx in range(1, nx)]
    odd_names = lambda names: [(r, k + 1) for r, k in names]
    both = lambda names: [(t, r, k) for t in range(2) for r, k in names]
    for array, some in zip(held, names):
        hold(array, some)
    early = [name for some in names for name in some]
    early = [early[i : i + 4] for i in range(0, len(early), 4)]
    for some in early:
        (numer0,) = chunk("even_forward", [[(0, r, k) for r, k in some]], False, False, [loc_even], [q0], [numer0])
    x_relayed = held[: len(direct)]
    x_late = [swap(a, m=2 * kx) for a in [*x_relayed, x_near] for kx in range(1, nx)]
    late_names = [(r, 2 * kx) for r in [*(r - 1 for r in direct), 1] for kx in range(1, nx)]
    numer0, loc_odd, mix_x, x_near, *held = together(numer0, loc_odd, mix_x, x_near, *held)
    mix_far = [swap(a, g=h) if h else a for h in range(groups) for a in mix_x]
    names.append([(1, 0)])
    for array, some in zip([*held, x_near], names):
        hold(array, some)
        hold(swap(array, m=1), odd_names(some))
    loc_parts = [loc_even, loc_odd]
    numer1, q1, back = chunk("own_back", [[(1, 0, k) for k in range(mp)]], True, False, loc_parts)
    q, numer = [q0, q1], [numer0, numer1]
    for some in early:
        numer = chunk("first", [[(1, r, k) for r, k in some], both(odd_names(some))], False, False, loc_parts, q, numer)
    numer = chunk("second", [both([(1, 0), (1, 1)])], False, False, loc_parts, q, numer)
    numer, *x_late = together(numer, *x_late)
    wo_odd = swap(mixing_projector, m=1)
    x_late_odd = [swap(a, m=1) for a in x_late]
    for name, array in zip(late_names, x_late):
        hold(array, [name])
    late = [late_names[i : i + 2] for i in range(0, len(late_names), 2)]
    for some in late:
        numer = chunk("third", [both(some)], False, False, loc_parts, q, numer)
    numer, mix_far, wo_odd, x_late_odd = together(numer, mix_far, wo_odd, x_late_odd)
    for name, array in zip(odd_names(late_names), x_late_odd):
        hold(array, [name])
    wo_far = []
    for h in range(groups):
        some = mix_far[h * (nx - 1) : (h + 1) * (nx - 1)]
        wo_far += [*some, *(swap(a, m=1) for a in some)]
    for some in late[:-1]:
        numer = chunk("fourth", [both(odd_names(some))], False, False, loc_parts, q, numer)
    a0, a1 = chunk("last", [both(odd_names(late[-1]))], False, True, loc_parts, q, numer)
    a0, a1, wo_far = together(a0, a1, wo_far)

    wo_own = [mixing_projector, wo_odd]
    w_mid = (premlp_rescaler.reshape(1, width), widening_matrix, narrowing_matrix)
    stream = (nucleotide_features, location_table, back.reshape(rows, width))

    def over_x(block):
        return [swap(block, m=2 * kx) for kx in range(1, nx)]

    def cores(blocks):
        return list(blocks) + [swap(a, m=1) for a in blocks]

    far0 = over_x(a0)
    part0 = mix_call(0, *stream, cores([a0]), wo_own)
    far1 = over_x(a1)
    part1 = mix_call(rows // 2, *stream, cores([a1]), wo_own)
    part0, part1, *far0 = together(part0, part1, *far0)
    even0, odd0, share0 = mid_call(groups, mp, scal, part0, *w_mid, cores(far0), wo_far)
    even0, odd0, share0, *far1 = together(even0, odd0, share0, *far1)
    paired0 = even0.astype(f32) + swap(odd0, m=1).astype(f32)
    part1, paired0 = together(part1, paired0)
    across0 = [swap(paired0[kx].astype(bf16), m=2 * kx) for kx in range(1, nx)]
    even1, odd1, share1 = mid_call(groups, mp, scal, part1, *w_mid, cores(far1), wo_far)
    even1, odd1, share1, *across0 = together(even1, odd1, share1, *across0)
    paired1 = even1.astype(f32) + swap(odd1, m=1).astype(f32)
    across1 = [swap(paired1[kx].astype(bf16), m=2 * kx) for kx in range(1, nx)]
    blocks = [
        0.5 * (share + paired[0] + sum(a.astype(f32) for a in arrived))
        for share, paired, arrived in ((share0, paired0, across0), (share1, paired1, across1))
    ]
    return jnp.concatenate(blocks, axis=0)


def solution(mesh):
    return jax.shard_map(
        shards,
        mesh=mesh,
        in_specs=(
            P(("groups", "seq"), None),
            P("seq", None),
            P(),
            P(None, None, "mp"),
            P(None, "mp"),
            P("mp"),
            P("mp", None),
            P(),
            P(None, "mp"),
            P("mp", None),
        ),
        out_specs=P(("groups", "seq"), "mp"),
        check_vma=False,
    )
```

```python
import functools

import jax
import jax.numpy as jnp
from jax import lax
from jax.experimental import pallas as pl
from jax.experimental.pallas import tpu as pltpu
from jax.sharding import PartitionSpec as P

epsilon = 1e-06
LOG2E = 1.4426950408889634
COST = 2**20
f32, bf16 = jnp.float32, jnp.bfloat16
AXES = ("groups", "seq", "mp")


def swap(block, g=0, s=0, m=0):
    groups, seq, mp = (lax.axis_size(name) for name in AXES)
    code = (g * seq + s) * mp + m
    return lax.ppermute(block, AXES, [(i, i ^ code) for i in range(groups * seq * mp)])


def unit(block):
    return block * lax.rsqrt(jnp.mean(block * block, axis=-1, keepdims=True) + epsilon)


def scaled_unit(block, scale):
    mean = jnp.mean(block * block, axis=-1, keepdims=True)
    return (block * (scale * lax.rsqrt(scale * scale * mean + epsilon))).astype(bf16)


def window(head, size):
    low = head * size // 128 * 128
    return low, (0 if head * size > low else size)


def dot(a, b):
    return jnp.dot(a, b, preferred_element_type=f32)


def chunk_kernel(dims, batches, where, own, last, counts, scal, *refs):
    groups, seq, mp, heads, lookup, value_size, padded = dims
    nx = mp // 2
    strands = sorted({t for batch in batches for t, r, k in batch})
    refs = list(refs)
    take = lambda n: [refs.pop(0) for _ in range(n)]
    x_refs = take(counts[0])
    (own_loc,) = take(1)
    loc_refs = take(counts[1])
    flip_ref, sharp_ref, wk_ref, wv_ref = take(4)
    wq_ref = take(1)[0] if own else None
    q_refs = [] if own else take(len(strands))
    numer_in = [] if own else take(len(strands))
    out_refs = take(2 if last else len(strands))
    if own:
        q_refs = take(1)
        back_out = take(1)[0] if 1 in strands else None
    scratch = list(zip(refs[::2], refs[1::2]))
    here_m, here_g = scal[0], scal[1]
    part, width = own_loc.shape[1:]
    half = width // groups
    columns = [pl.ds(pl.multiple_of((h ^ here_g) * half, half), half) for h in range(groups)]

    def loc_piece(r, k, h):
        if r == 0:
            return own_loc[here_m ^ k, :, columns[h]]
        return loc_refs[k & 1][h * nx + (k >> 1), r - 1]

    products = []
    for batch, (streams, scales) in zip(batches, scratch):
        group = flip_ref.shape[0] // part
        backs = {}
        mirrored = [(r, k) for t, r, k in batch if t == 1]
        for n in range(0, len(mirrored), group):
            some = mirrored[n : n + group]
            for h in range(groups):
                pieces = [loc_piece(r ^ (seq - 1), k ^ (mp - 1), h) for r, k in reversed(some)]
                size = len(some) * part
                exchange = flip_ref[:size, group * part - size :]
                flipped = dot(exchange, jnp.concatenate(pieces, axis=0)).astype(bf16)
                for i, (r, k) in enumerate(some):
                    backs[r, k, h] = flipped[i * part : (i + 1) * part]
        for i, (t, r, k) in enumerate(batch):
            ref, at = (x_refs[0], here_m ^ k) if own else (x_refs[where[r, k][0]], where[r, k][1])
            place = here_m ^ k if own else i
            square = 0.0
            for h in range(groups):
                loc = backs[r, k, h] if t else loc_piece(r, k, h)
                if t and own:
                    back_out[place, :, columns[h]] = loc
                stream = ref[at, :, columns[h]] + loc
                streams[place, :, columns[h]] = stream
                square = square + jnp.sum(jnp.square(stream.astype(f32)), axis=-1, keepdims=True)
            scales[place] = jnp.broadcast_to(lax.rsqrt(square / width + epsilon), (part, 128))
        rows = streams[...].reshape(-1, width)
        scale = scales[...].reshape(-1, 128)
        if own:
            query = dot(rows, wq_ref[...])
            for h in range(heads):
                cols = slice(h * lookup, (h + 1) * lookup)
                q_refs[0][:, cols] = scaled_unit(query[:, cols], scale)
        products.append((scale, dot(rows, wk_ref[...]), dot(rows, wv_ref[...])))
    for p, t in enumerate(strands):
        mine = []
        for batch, product in zip(batches, products):
            places = [i for i, item in enumerate(batch) if item[0] == t]
            if places:
                rows = slice(places[0] * part, (places[-1] + 1) * part)
                mine.append([a[rows] for a in product])
        attended = []
        for h in range(heads):
            cols = slice(h * lookup, (h + 1) * lookup)
            key_n = jnp.concatenate([scaled_unit(k[:, cols], scale) for scale, k, v in mine], axis=0)
            low, spare = window(h, value_size)
            value_h = []
            for c in range(padded // 128):
                block = slice(low + c * 128, low + (c + 1) * 128)
                column = jnp.concatenate([v[:, block] * scale for scale, k, v in mine], axis=0)
                if c == spare // 128:
                    lane = lax.broadcasted_iota(jnp.int32, column.shape, 1)
                    column = jnp.where(lane == spare % 128, 1.0, column)
                value_h.append(column.astype(bf16))
            value_h = jnp.concatenate(value_h, axis=1)
            scores = lax.dot_general(
                q_refs[p][:, cols], key_n, (((1,), (1,)), ((), ())), preferred_element_type=f32
            )
            weight = jnp.exp2(scores * (sharp_ref[h] * (LOG2E / lookup))).astype(bf16)
            numer = dot(weight, value_h)
            if not own:
                numer = numer + numer_in[p][h]
            if last:
                first = h * value_size - low
                attended.append(numer[:, first : first + value_size] / numer[:, spare : spare + 1])
            else:
                out_refs[p][h] = numer
        if last:
            attended = jnp.concatenate(attended, axis=1).astype(bf16)
            block = attended.shape[0] // len(out_refs)
            for i, out_ref in enumerate(out_refs):
                out_ref[p] = attended[i * block : (i + 1) * block]


VMEM = pl.BlockSpec(memory_space=pltpu.VMEM)
SMEM = pl.BlockSpec(memory_space=pltpu.SMEM)


def chunk_call(name, dims, batches, own, last, scal, x_parts, own_loc, loc_parts, flip, sharp, weights, q, numer):
    groups, seq, mp, heads, lookup, value_size, padded = dims
    _, part, width = own_loc.shape
    rows = part * mp
    batches = tuple(tuple(sorted(batch)) for batch in batches)
    strands = sorted({t for batch in batches for t, r, k in batch})
    where = {name: (n, i) for n, (_, names) in enumerate(x_parts) for name, i in names.items()}
    args = [a for a, _ in x_parts] + [own_loc] + list(loc_parts) + [flip, sharp] + list(weights) + list(q) + list(numer)
    specs = [SMEM if a is sharp else VMEM for a in args]
    if last:
        outs = [jax.ShapeDtypeStruct((2, rows // 2, heads * value_size), bf16)] * 2
    else:
        outs = [jax.ShapeDtypeStruct((heads, rows, padded), f32)] * len(strands)
    if own:
        outs = outs + [jax.ShapeDtypeStruct((rows, heads * lookup), bf16)]
        if 1 in strands:
            outs = outs + [jax.ShapeDtypeStruct((mp, part, width), bf16)]
    scratch = []
    for batch in batches:
        scratch += [pltpu.VMEM((len(batch), part, width), bf16), pltpu.VMEM((len(batch), part, 128), f32)]
    return pl.pallas_call(
        functools.partial(chunk_kernel, dims, batches, where, own, last, (len(x_parts), len(loc_parts))),
        out_shape=outs,
        in_specs=[SMEM] + specs,
        out_specs=[VMEM] * len(outs),
        scratch_shapes=scratch,
        compiler_params=pltpu.CompilerParams(vmem_limit_bytes=40 * 2**20),
        cost_estimate=pl.CostEstimate(flops=COST, bytes_accessed=COST, transcendentals=0),
        name=name,
    )(scal, *args)


def mix_kernel(lo, x_ref, loc_ref, back_ref, att0, att1, wo0, wo1, out_ref):
    rows = out_ref.shape[1]
    mixed = dot(att0[...].reshape(2 * rows, -1), wo0[...]) + dot(att1[...].reshape(2 * rows, -1), wo1[...])
    x_f = x_ref[lo : lo + rows].astype(f32)
    for t, loc in enumerate((loc_ref, back_ref)):
        out_ref[t] = x_f + loc[lo : lo + rows].astype(f32) + mixed[t * rows : (t + 1) * rows]


def mix_call(lo, x, loc, back, att, wo):
    rows, width = att[0].shape[1], x.shape[1]
    return pl.pallas_call(
        functools.partial(mix_kernel, lo),
        out_shape=jax.ShapeDtypeStruct((2, rows, width), f32),
        in_specs=[VMEM] * 7,
        out_specs=VMEM,
        compiler_params=pltpu.CompilerParams(vmem_limit_bytes=32 * 2**20),
        cost_estimate=pl.CostEstimate(
            flops=COST, bytes_accessed=COST, transcendentals=0
        ),
        name="mix",
    )(x, loc, back, *att, *wo)


def mid_kernel(groups, scal, *refs):
    partial, gain_ref, w1_ref, w2_ref, *refs = refs
    even_out, odd_out, middle_out, summed, mixed = refs[-5:]
    refs = refs[:-5]
    att, wo = refs[: len(refs) // (1 + groups)], refs[len(refs) // (1 + groups) :]
    here_m, here_g = scal[0], scal[1]
    rows = partial.shape[1]
    half = partial.shape[2] // groups
    blocks = [a_ref[...].reshape(2 * rows, -1) for a_ref in att]
    for h in range(groups):
        columns = pl.ds(pl.multiple_of((h ^ here_g) * half, half), half)
        part = partial[:, :, columns].reshape(2 * rows, half)
        mixed[:, columns] = part + sum(dot(a, w[...]) for a, w in zip(blocks, wo[h * len(att) : (h + 1) * len(att)]))
    middle = mixed[...]
    normed = (unit(middle) * gain_ref[...]).astype(bf16)
    expanded = jax.nn.gelu(dot(normed, w1_ref[...]), approximate=True).astype(bf16)
    out = dot(expanded, w2_ref[...])
    out = out[:rows] + out[rows:]
    both = middle[:rows] + middle[rows:]
    mp, _, share = summed.shape
    for j in range(mp):
        summed[j] = out[:, j * share : (j + 1) * share].astype(bf16)
    for k in range(mp):
        (odd_out if k & 1 else even_out)[k >> 1] = summed[here_m ^ k]
    for j in range(mp):
        block = both[:, j * share : (j + 1) * share]

        @pl.when(here_m == j)
        def _():
            middle_out[...] = block


def mid_call(groups, mp, scal, partial, gain, w1, w2, att, wo):
    _, rows, width = partial.shape
    share = width // mp
    args = [partial, gain, w1, w2, *att, *wo]
    return pl.pallas_call(
        functools.partial(mid_kernel, groups),
        out_shape=[jax.ShapeDtypeStruct((mp // 2, rows, share), bf16)] * 2 + [jax.ShapeDtypeStruct((rows, share), f32)],
        in_specs=[SMEM] + [VMEM] * len(args),
        out_specs=[VMEM] * 3,
        scratch_shapes=[pltpu.VMEM((mp, rows, share), bf16), pltpu.VMEM((2 * rows, width), f32)],
        compiler_params=pltpu.CompilerParams(vmem_limit_bytes=40 * 2**20),
        cost_estimate=pl.CostEstimate(
            flops=COST,
            bytes_accessed=COST,
            transcendentals=0,
        ),
        name="middle",
    )(scal, *args)


def stack_kernel(*refs):
    for i, ref in enumerate(refs[:-1]):
        refs[-1][i] = ref[...]


def stack_call(arrays):
    shape = (len(arrays),) + arrays[0].shape
    return pl.pallas_call(
        stack_kernel,
        out_shape=jax.ShapeDtypeStruct(shape, arrays[0].dtype),
        in_specs=[VMEM] * len(arrays),
        out_specs=VMEM,
        compiler_params=pltpu.CompilerParams(vmem_limit_bytes=40 * 2**20),
        cost_estimate=pl.CostEstimate(flops=COST, bytes_accessed=COST, transcendentals=0),
        name="stack",
    )(*arrays)


def together(*arrays):
    return lax.optimization_barrier(arrays)


def shards(
    nucleotide_features,
    location_table,
    premix_rescaler,
    probe_lookup_matrices,
    payload_projector,
    logit_sharpness,
    mixing_projector,
    premlp_rescaler,
    widening_matrix,
    narrowing_matrix,
):
    rows, width = nucleotide_features.shape
    heads = logit_sharpness.shape[0]
    lookup = probe_lookup_matrices.shape[2] // heads
    value_size = payload_projector.shape[1] // heads
    padded = (value_size // 128 + 1) * 128
    groups, seq, mp = (lax.axis_size(name) for name in AXES)
    here_g, here_m = lax.axis_index("groups"), lax.axis_index("mp")
    nx = mp // 2
    part, half = rows // mp, width // groups
    dims = (groups, seq, mp, heads, lookup, value_size, padded)
    scal = jnp.stack([here_m, here_g]).astype(jnp.int32)
    x_own = nucleotide_features.reshape(mp, part, width)
    loc_own = location_table.reshape(mp, part, width)

    place = lax.broadcasted_iota(jnp.int32, (2 * part, 2 * part), 0) + lax.broadcasted_iota(jnp.int32, (2 * part, 2 * part), 1)
    flip = (place == 2 * part - 1).astype(bf16)
    gain = premix_rescaler.reshape(width, 1)
    wq, wk = [(gain * w.astype(f32)).astype(bf16) for w in (probe_lookup_matrices[0], probe_lookup_matrices[1])]
    wv = (gain * payload_projector.astype(f32)).astype(bf16)
    wv = jnp.pad(wv, ((0, 0), (0, -wv.shape[1] % 128)))

    have = {}

    def hold(array, names):
        have.update({name: (array, i) for i, name in enumerate(names)})

    def chunk(name, batches, own, last, loc_parts, q=(), numer=()):
        flip, wq, wk, wv = prepared
        weights = (wk, wv, wq) if own else (wk, wv)
        x_parts = {}
        for r, k in sorted({item[1:] for batch in batches for item in batch}):
            array, i = have[r, k]
            x_parts.setdefault(id(array), (array, {}))[1][r, k] = i
        return chunk_call(
            name, dims, batches, own, last, scal, list(x_parts.values()), loc_own, loc_parts,
            flip, logit_sharpness, weights, q, numer,
        )

    direct = range(3, seq, 2)
    loc_part = lax.dynamic_slice(location_table, (here_m * part, here_g * half), (part, half))
    loc_part, mix_first, x_first = together(loc_part, mixing_projector, x_own)
    mix_part = lax.dynamic_slice_in_dim(mix_first, here_g * half, half, 1)
    loc_z = [swap(loc_part, s=r) for r in range(1, seq)]
    mix_x = [swap(mix_part, m=2 * kx) for kx in range(1, nx)]
    x_mine = lax.dynamic_slice_in_dim(x_first, here_m, 1, 0)

    x_direct = [swap(x_mine, s=r) for r in direct]
    x_mine, flip, wq, wk, wv, loc_z = together(x_mine, flip, wq, wk, wv, loc_z)
    prepared = (flip, wq, wk, wv)
    loc_far = stack_call(loc_z)
    x_near = swap(x_mine, s=1)
    loc_xy = [loc_far] + [swap(loc_far, m=2 * kx) for kx in range(1, nx)]
    loc_y = [swap(loc_far, g=h) for h in range(1, groups)]
    x_direct, x_near, mix_x, loc_y = together(x_direct, x_near, mix_x, loc_y)
    loc_xy = loc_xy + [a for h in range(1, groups) for a in (loc_y[h - 1], *(swap(a, g=h) for a in loc_xy[1:]))]
    x_relayed = [swap(a, s=1) for a in x_direct]
    x_late = [swap(x_near, m=2 * kx) for kx in range(1, nx)]
    x_across = [swap(a, m=2 * kx) for a in x_direct for kx in range(1, nx)]
    hold(x_own, [(0, k) for k in range(mp)])
    numer0, q0 = chunk("own_forward", [[(0, 0, k) for k in range(mp)]], True, False, [])

    held = (*x_relayed, *x_direct, *x_across, x_near)
    numer0, loc_xy, mix_x, x_late, *held = together(numer0, loc_xy, mix_x, x_late, *held)
    mix_far = [swap(a, g=h) if h else a for h in range(groups) for a in mix_x]
    loc_even = stack_call(loc_xy)
    loc_odd = swap(loc_even, m=1)
    names = [[(r - 1, 0)] for r in direct] + [[(r, 0)] for r in direct]
    names += [[(r, 2 * kx)] for r in direct for kx in range(1, nx)] + [[(1, 0)]]
    odd_names = lambda names: [(r, k + 1) for r, k in names]
    both = lambda names: [(t, r, k) for t in range(2) for r, k in names]
    for array, some in zip(held, names):
        hold(array, some)
    early = [name for some in names for name in some]
    early = [early[i : i + 4] for i in range(0, len(early), 4)]
    for some in early:
        (numer0,) = chunk("even_forward", [[(0, r, k) for r, k in some]], False, False, [loc_even], [q0], [numer0])
    x_relayed = held[: len(direct)]
    x_late += [swap(a, m=2 * kx) for a in x_relayed for kx in range(1, nx)]
    late_names = [(r, 2 * kx) for r in [1, *(r - 1 for r in direct)] for kx in range(1, nx)]
    numer0, loc_odd, *held = together(numer0, loc_odd, *held)
    for array, some in zip(held, names):
        hold(array, some)
        hold(swap(array, m=1), odd_names(some))
    loc_parts = [loc_even, loc_odd]
    numer1, q1, back = chunk("own_back", [[(1, 0, k) for k in range(mp)]], True, False, loc_parts)
    numer1, x_late = together(numer1, x_late)
    x_late_odd = [swap(a, m=1) for a in x_late]
    wo_odd = swap(mixing_projector, m=1)
    q, numer = [q0, q1], [numer0, numer1]
    for some in early:
        numer = chunk("first", [[(1, r, k) for r, k in some], both(odd_names(some))], False, False, loc_parts, q, numer)
    numer, mix_far, wo_odd, x_late_odd = together(numer, mix_far, wo_odd, x_late_odd)
    for name, even, odd in zip(late_names, x_late, x_late_odd):
        hold(even, [name])
        hold(odd, odd_names([name]))
    wo_far = []
    for h in range(groups):
        some = mix_far[h * (nx - 1) : (h + 1) * (nx - 1)]
        wo_far += [*some, *(swap(a, m=1) for a in some)]
    late = [late_names[i : i + 2] for i in range(0, len(late_names), 2)]
    late = [[both(some), both(odd_names(some))] for some in late]
    for some in late[:-1]:
        numer = chunk("second", some, False, False, loc_parts, q, numer)
    a0, a1 = chunk("last", late[-1], False, True, loc_parts, q, numer)
    a0, a1, wo_far = together(a0, a1, wo_far)

    wo_own = [mixing_projector, wo_odd]
    w_mid = (premlp_rescaler.reshape(1, width), widening_matrix, narrowing_matrix)
    stream = (nucleotide_features, location_table, back.reshape(rows, width))

    def over_x(block):
        return [swap(block, m=2 * kx) for kx in range(1, nx)]

    def cores(blocks):
        return list(blocks) + [swap(a, m=1) for a in blocks]

    far0 = over_x(a0)
    part0 = mix_call(0, *stream, cores([a0]), wo_own)
    far1 = over_x(a1)
    part1 = mix_call(rows // 2, *stream, cores([a1]), wo_own)
    part0, part1, *far0 = together(part0, part1, *far0)
    even0, odd0, share0 = mid_call(groups, mp, scal, part0, *w_mid, cores(far0), wo_far)
    even0, odd0, share0, *far1 = together(even0, odd0, share0, *far1)
    paired0 = even0.astype(f32) + swap(odd0, m=1).astype(f32)
    part1, paired0 = together(part1, paired0)
    across0 = [swap(paired0[kx].astype(bf16), m=2 * kx) for kx in range(1, nx)]
    even1, odd1, share1 = mid_call(groups, mp, scal, part1, *w_mid, cores(far1), wo_far)
    even1, odd1, share1, *across0 = together(even1, odd1, share1, *across0)
    paired1 = even1.astype(f32) + swap(odd1, m=1).astype(f32)
    across1 = [swap(paired1[kx].astype(bf16), m=2 * kx) for kx in range(1, nx)]
    blocks = [
        0.5 * (share + paired[0] + sum(a.astype(f32) for a in arrived))
        for share, paired, arrived in ((share0, paired0, across0), (share1, paired1, across1))
    ]
    return jnp.concatenate(blocks, axis=0)


def solution(mesh):
    return jax.shard_map(
        shards,
        mesh=mesh,
        in_specs=(
            P(("groups", "seq"), None),
            P("seq", None),
            P(),
            P(None, None, "mp"),
            P(None, "mp"),
            P("mp"),
            P("mp", None),
            P(),
            P(None, "mp"),
            P("mp", None),
        ),
        out_specs=P(("groups", "seq"), "mp"),
        check_vma=False,
    )
```

```python
import functools

import jax
import jax.numpy as jnp
from jax import lax
from jax.experimental import pallas as pl
from jax.experimental.pallas import tpu as pltpu
from jax.sharding import PartitionSpec as P

epsilon = 1e-06
LOG2E = 1.4426950408889634
COST = 2**20
f32, bf16 = jnp.float32, jnp.bfloat16
AXES = ("groups", "seq", "mp")


def swap(block, g=0, s=0, m=0):
    groups, seq, mp = (lax.axis_size(name) for name in AXES)
    code = (g * seq + s) * mp + m
    return lax.ppermute(block, AXES, [(i, i ^ code) for i in range(groups * seq * mp)])


def unit(block):
    return block * lax.rsqrt(jnp.mean(block * block, axis=-1, keepdims=True) + epsilon)


def scaled_unit(block, scale, gain=None):
    mean = jnp.mean(block * block, axis=-1, keepdims=True)
    factor = scale * lax.rsqrt(scale * scale * mean + epsilon)
    return (block * (factor if gain is None else factor * gain)).astype(bf16)


def window(head, size):
    low = head * size // 128 * 128
    return low, (0 if head * size > low else size)


def dot(a, b):
    return jnp.dot(a, b, preferred_element_type=f32)


def chunk_kernel(dims, batches, where, own, last, counts, scal, *refs):
    groups, seq, mp, heads, lookup, value_size, padded = dims
    nx = mp // 2
    strands = sorted({t for batch in batches for t, r, k in batch})
    refs = list(refs)
    take = lambda n: [refs.pop(0) for _ in range(n)]
    x_refs = take(counts[0])
    (own_loc,) = take(1)
    loc_refs = take(counts[1])
    flip_ref, sharp_ref, wk_ref, wv_ref = take(4)
    wq_ref = take(1)[0] if own else None
    q_refs = [] if own else take(len(strands))
    numer_in = [] if own else take(len(strands))
    out_refs = take(2 if last else len(strands))
    if own:
        q_refs = take(1)
        back_out = take(1)[0] if 1 in strands else None
    scratch = list(zip(refs[::2], refs[1::2]))
    here_m, here_g = scal[0], scal[1]
    part, width = own_loc.shape[1:]
    half = width // groups
    columns = [pl.ds(pl.multiple_of((h ^ here_g) * half, half), half) for h in range(groups)]

    def loc_piece(r, k, h):
        if r == 0:
            return own_loc[here_m ^ k, :, columns[h]]
        return loc_refs[k & 1][h * nx + (k >> 1), r - 1]

    products = []
    for batch, (streams, scales) in zip(batches, scratch):
        group = flip_ref.shape[0] // part
        backs = {}
        mirrored = [(r, k) for t, r, k in batch if t == 1]
        for n in range(0, len(mirrored), group):
            some = mirrored[n : n + group]
            for h in range(groups):
                pieces = [loc_piece(r ^ (seq - 1), k ^ (mp - 1), h) for r, k in reversed(some)]
                size = len(some) * part
                exchange = flip_ref[:size, group * part - size :]
                flipped = dot(exchange, jnp.concatenate(pieces, axis=0)).astype(bf16)
                for i, (r, k) in enumerate(some):
                    backs[r, k, h] = flipped[i * part : (i + 1) * part]
        for i, (t, r, k) in enumerate(batch):
            ref, at = (x_refs[0], here_m ^ k) if own else (x_refs[where[r, k][0]], where[r, k][1])
            place = here_m ^ k if own else i
            square = 0.0
            for h in range(groups):
                loc = backs[r, k, h] if t else loc_piece(r, k, h)
                if t and own:
                    back_out[place, :, columns[h]] = loc
                stream = ref[at, :, columns[h]] + loc
                streams[place, :, columns[h]] = stream
                square = square + jnp.sum(jnp.square(stream.astype(f32)), axis=-1, keepdims=True)
            scales[place] = jnp.broadcast_to(lax.rsqrt(square / width + epsilon), (part, 128))
        rows = streams[...].reshape(-1, width)
        scale = scales[...].reshape(-1, 128)
        if own:
            query = dot(rows, wq_ref[...])
            for h in range(heads):
                cols = slice(h * lookup, (h + 1) * lookup)
                q_refs[0][:, cols] = scaled_unit(query[:, cols], scale, sharp_ref[h] * (LOG2E / lookup))
        products.append((scale, dot(rows, wk_ref[...]), dot(rows, wv_ref[...])))
    for p, t in enumerate(strands):
        mine = []
        for batch, product in zip(batches, products):
            places = [i for i, item in enumerate(batch) if item[0] == t]
            if places:
                rows = slice(places[0] * part, (places[-1] + 1) * part)
                mine.append([a[rows] for a in product])
        attended = []
        for h in range(heads):
            cols = slice(h * lookup, (h + 1) * lookup)
            key_n = jnp.concatenate([scaled_unit(k[:, cols], scale) for scale, k, v in mine], axis=0)
            low, spare = window(h, value_size)
            value_h = []
            for c in range(padded // 128):
                block = slice(low + c * 128, low + (c + 1) * 128)
                column = jnp.concatenate([v[:, block] * scale for scale, k, v in mine], axis=0)
                if c == spare // 128:
                    lane = lax.broadcasted_iota(jnp.int32, column.shape, 1)
                    column = jnp.where(lane == spare % 128, 1.0, column)
                value_h.append(column.astype(bf16))
            value_h = jnp.concatenate(value_h, axis=1)
            scores = lax.dot_general(
                q_refs[p][:, cols], key_n, (((1,), (1,)), ((), ())), preferred_element_type=f32
            )
            weight = jnp.exp2(scores).astype(bf16)
            numer = dot(weight, value_h)
            if not own:
                numer = numer + numer_in[p][h]
            if last:
                first = h * value_size - low
                attended.append(numer[:, first : first + value_size] / numer[:, spare : spare + 1])
            else:
                out_refs[p][h] = numer
        if last:
            attended = jnp.concatenate(attended, axis=1).astype(bf16)
            block = attended.shape[0] // len(out_refs)
            for i, out_ref in enumerate(out_refs):
                out_ref[p] = attended[i * block : (i + 1) * block]


VMEM = pl.BlockSpec(memory_space=pltpu.VMEM)
SMEM = pl.BlockSpec(memory_space=pltpu.SMEM)


def chunk_call(name, dims, batches, own, last, scal, x_parts, own_loc, loc_parts, flip, sharp, weights, q, numer):
    groups, seq, mp, heads, lookup, value_size, padded = dims
    _, part, width = own_loc.shape
    rows = part * mp
    batches = tuple(tuple(sorted(batch)) for batch in batches)
    strands = sorted({t for batch in batches for t, r, k in batch})
    where = {name: (n, i) for n, (_, names) in enumerate(x_parts) for name, i in names.items()}
    args = [a for a, _ in x_parts] + [own_loc] + list(loc_parts) + [flip, sharp] + list(weights) + list(q) + list(numer)
    specs = [SMEM if a is sharp else VMEM for a in args]
    if last:
        outs = [jax.ShapeDtypeStruct((2, rows // 2, heads * value_size), bf16)] * 2
    else:
        outs = [jax.ShapeDtypeStruct((heads, rows, padded), f32)] * len(strands)
    if own:
        outs = outs + [jax.ShapeDtypeStruct((rows, heads * lookup), bf16)]
        if 1 in strands:
            outs = outs + [jax.ShapeDtypeStruct((mp, part, width), bf16)]
    scratch = []
    for batch in batches:
        scratch += [pltpu.VMEM((len(batch), part, width), bf16), pltpu.VMEM((len(batch), part, 128), f32)]
    return pl.pallas_call(
        functools.partial(chunk_kernel, dims, batches, where, own, last, (len(x_parts), len(loc_parts))),
        out_shape=outs,
        in_specs=[SMEM] + specs,
        out_specs=[VMEM] * len(outs),
        scratch_shapes=scratch,
        compiler_params=pltpu.CompilerParams(vmem_limit_bytes=40 * 2**20),
        cost_estimate=pl.CostEstimate(flops=COST, bytes_accessed=COST, transcendentals=0),
        name=name,
    )(scal, *args)


def mix_kernel(lo, x_ref, loc_ref, back_ref, att0, att1, wo0, wo1, out_ref):
    rows = out_ref.shape[1]
    mixed = dot(att0[...].reshape(2 * rows, -1), wo0[...]) + dot(att1[...].reshape(2 * rows, -1), wo1[...])
    x_f = x_ref[lo : lo + rows].astype(f32)
    for t, loc in enumerate((loc_ref, back_ref)):
        out_ref[t] = x_f + loc[lo : lo + rows].astype(f32) + mixed[t * rows : (t + 1) * rows]


def mix_call(lo, x, loc, back, att, wo):
    rows, width = att[0].shape[1], x.shape[1]
    return pl.pallas_call(
        functools.partial(mix_kernel, lo),
        out_shape=jax.ShapeDtypeStruct((2, rows, width), f32),
        in_specs=[VMEM] * 7,
        out_specs=VMEM,
        compiler_params=pltpu.CompilerParams(vmem_limit_bytes=32 * 2**20),
        cost_estimate=pl.CostEstimate(
            flops=8 * rows * width * wo[0].shape[0], bytes_accessed=8 * 2**20, transcendentals=0
        ),
        name="mix",
    )(x, loc, back, *att, *wo)


def mid_kernel(groups, scal, *refs):
    partial, gain_ref, w1_ref, w2_ref, *refs = refs
    even_out, odd_out, middle_out, summed, mixed = refs[-5:]
    refs = refs[:-5]
    att, wo = refs[: len(refs) // (1 + groups)], refs[len(refs) // (1 + groups) :]
    here_m, here_g = scal[0], scal[1]
    rows = partial.shape[1]
    half = partial.shape[2] // groups
    blocks = [a_ref[...].reshape(2 * rows, -1) for a_ref in att]
    for h in range(groups):
        columns = pl.ds(pl.multiple_of((h ^ here_g) * half, half), half)
        part = partial[:, :, columns].reshape(2 * rows, half)
        mixed[:, columns] = part + sum(dot(a, w[...]) for a, w in zip(blocks, wo[h * len(att) : (h + 1) * len(att)]))
    middle = mixed[...]
    normed = (unit(middle) * gain_ref[...]).astype(bf16)
    expanded = jax.nn.gelu(dot(normed, w1_ref[...]), approximate=True).astype(bf16)
    out = dot(expanded, w2_ref[...])
    out = out[:rows] + out[rows:]
    both = middle[:rows] + middle[rows:]
    mp, _, share = summed.shape
    for j in range(mp):
        summed[j] = out[:, j * share : (j + 1) * share].astype(bf16)
    for k in range(mp):
        (odd_out if k & 1 else even_out)[k >> 1] = summed[here_m ^ k]
    for j in range(mp):
        block = both[:, j * share : (j + 1) * share]

        @pl.when(here_m == j)
        def _():
            middle_out[...] = block


def mid_call(groups, mp, scal, partial, gain, w1, w2, att, wo):
    _, rows, width = partial.shape
    share = width // mp
    args = [partial, gain, w1, w2, *att, *wo]
    return pl.pallas_call(
        functools.partial(mid_kernel, groups),
        out_shape=[jax.ShapeDtypeStruct((mp // 2, rows, share), bf16)] * 2 + [jax.ShapeDtypeStruct((rows, share), f32)],
        in_specs=[SMEM] + [VMEM] * len(args),
        out_specs=[VMEM] * 3,
        scratch_shapes=[pltpu.VMEM((mp, rows, share), bf16), pltpu.VMEM((2 * rows, width), f32)],
        compiler_params=pltpu.CompilerParams(vmem_limit_bytes=40 * 2**20),
        cost_estimate=pl.CostEstimate(
            flops=4 * rows * width * (width // 2 + 2 * w1.shape[1]),
            bytes_accessed=14 * 2**20,
            transcendentals=2 * rows * w1.shape[1],
        ),
        name="middle",
    )(scal, *args)


def stack_kernel(*refs):
    for i, ref in enumerate(refs[:-1]):
        refs[-1][i] = ref[...]


def stack_call(arrays):
    shape = (len(arrays),) + arrays[0].shape
    return pl.pallas_call(
        stack_kernel,
        out_shape=jax.ShapeDtypeStruct(shape, arrays[0].dtype),
        in_specs=[VMEM] * len(arrays),
        out_specs=VMEM,
        compiler_params=pltpu.CompilerParams(vmem_limit_bytes=40 * 2**20),
        cost_estimate=pl.CostEstimate(flops=COST, bytes_accessed=COST, transcendentals=0),
        name="stack",
    )(*arrays)


def together(*arrays):
    return lax.optimization_barrier(arrays)


def shards(
    nucleotide_features,
    location_table,
    premix_rescaler,
    probe_lookup_matrices,
    payload_projector,
    logit_sharpness,
    mixing_projector,
    premlp_rescaler,
    widening_matrix,
    narrowing_matrix,
):
    rows, width = nucleotide_features.shape
    heads = logit_sharpness.shape[0]
    lookup = probe_lookup_matrices.shape[2] // heads
    value_size = payload_projector.shape[1] // heads
    padded = (value_size // 128 + 1) * 128
    groups, seq, mp = (lax.axis_size(name) for name in AXES)
    here_g, here_m = lax.axis_index("groups"), lax.axis_index("mp")
    nx = mp // 2
    part, half = rows // mp, width // groups
    dims = (groups, seq, mp, heads, lookup, value_size, padded)
    scal = jnp.stack([here_m, here_g]).astype(jnp.int32)
    x_own = nucleotide_features.reshape(mp, part, width)
    loc_own = location_table.reshape(mp, part, width)

    place = lax.broadcasted_iota(jnp.int32, (2 * part, 2 * part), 0) + lax.broadcasted_iota(jnp.int32, (2 * part, 2 * part), 1)
    flip = (place == 2 * part - 1).astype(bf16)
    gain = premix_rescaler.reshape(width, 1)
    wq, wk = [(gain * w.astype(f32)).astype(bf16) for w in (probe_lookup_matrices[0], probe_lookup_matrices[1])]
    wv = (gain * payload_projector.astype(f32)).astype(bf16)
    wv = jnp.pad(wv, ((0, 0), (0, -wv.shape[1] % 128)))

    have = {}

    def hold(array, names):
        have.update({name: (array, i) for i, name in enumerate(names)})

    def chunk(name, batches, own, last, loc_parts, q=(), numer=()):
        flip, wq, wk, wv = prepared
        weights = (wk, wv, wq) if own else (wk, wv)
        x_parts = {}
        for r, k in sorted({item[1:] for batch in batches for item in batch}):
            array, i = have[r, k]
            x_parts.setdefault(id(array), (array, {}))[1][r, k] = i
        return chunk_call(
            name, dims, batches, own, last, scal, list(x_parts.values()), loc_own, loc_parts,
            flip, logit_sharpness, weights, q, numer,
        )

    direct = range(3, seq, 2)
    loc_part = lax.dynamic_slice(location_table, (here_m * part, here_g * half), (part, half))
    loc_part, mix_first, x_first = together(loc_part, mixing_projector, x_own)
    mix_part = lax.dynamic_slice_in_dim(mix_first, here_g * half, half, 1)
    mix_x = [swap(mix_part, m=2 * kx) for kx in range(1, nx)]
    loc_z = [swap(loc_part, s=r) for r in range(1, seq)]
    x_mine = lax.dynamic_slice_in_dim(x_first, here_m, 1, 0)
    x_near = swap(x_mine, s=1)

    x_near, x_mine, flip, wq, wk, wv, loc_z = together(x_near, x_mine, flip, wq, wk, wv, loc_z)
    prepared = (flip, wq, wk, wv)
    loc_far = stack_call(loc_z)
    x_direct = [swap(x_mine, s=r) for r in direct]
    loc_xy = [loc_far] + [swap(loc_far, m=2 * kx) for kx in range(1, nx)]
    loc_y = [swap(loc_far, g=h) for h in range(1, groups)]
    x_direct, x_near, mix_x, loc_xy, loc_y = together(x_direct, x_near, mix_x, loc_xy, loc_y)
    loc_xy = loc_xy + [a for h in range(1, groups) for a in (loc_y[h - 1], *(swap(a, g=h) for a in loc_xy[1:]))]
    mix_far = [swap(a, g=h) if h else a for h in range(groups) for a in mix_x]
    x_relayed = [swap(a, s=1) for a in x_direct]
    x_across = [swap(a, m=2 * kx) for a in x_direct for kx in range(1, nx)]
    hold(x_own, [(0, k) for k in range(mp)])
    numer0, q0 = chunk("own_forward", [[(0, 0, k) for k in range(mp)]], True, False, [])

    x_late = [swap(x_near, m=2 * kx) for kx in range(1, nx)]
    numer0, loc_xy, *held = together(numer0, loc_xy, *x_relayed, x_near, *x_direct, *x_across)
    loc_even = stack_call(loc_xy)
    loc_odd = swap(loc_even, m=1)
    names = [[(r - 1, 0)] for r in direct] + [[(1, 0)]] + [[(r, 0)] for r in direct]
    names += [[(r, 2 * kx)] for r in direct for kx in range(1, nx)]
    odd_names = lambda names: [(r, k + 1) for r, k in names]
    both = lambda names: [(t, r, k) for t in range(2) for r, k in names]
    for array, some in zip(held, names):
        hold(array, some)
    early = [name for some in names for name in some]
    early = [early[i : i + 4] for i in range(0, len(early), 4)]
    for some in early:
        (numer0,) = chunk("even_forward", [[(0, r, k) for r, k in some]], False, False, [loc_even], [q0], [numer0])
    numer0, loc_odd, *held = together(numer0, loc_odd, *held)
    for array, some in zip(held, names):
        hold(array, some)
        hold(swap(array, m=1), odd_names(some))
    x_late = [swap(a, m=2 * kx) for a in held[: len(direct)] for kx in range(1, nx)] + x_late
    late_names = [(r, 2 * kx) for r in [*(r - 1 for r in direct), 1] for kx in range(1, nx)]
    loc_parts = [loc_even, loc_odd]
    numer1, q1, back = chunk("own_back", [[(1, 0, k) for k in range(mp)]], True, False, loc_parts)
    q, numer = [q0, q1], [numer0, numer1]
    rest = []
    for some in early:
        odd = odd_names(some)
        batches = [[(1, r, k) for r, k in some], both(odd[: len(odd) // 2])]
        numer = chunk("first", batches, False, False, loc_parts, q, numer)
        rest = rest + odd[len(odd) // 2 :]
    numer, *x_late = together(numer, *x_late)
    wo_odd = swap(mixing_projector, m=1)
    for name, array in zip(late_names, x_late):
        hold(array, [name])
        hold(swap(array, m=1), odd_names([name]))
    late = [late_names[i : i + 2] for i in range(0, len(late_names), 2)]
    for n, some in enumerate(late):
        batches = [both(rest[2 * n : 2 * n + 2]), both(some)]
        numer = chunk("second", [batch for batch in batches if batch], False, False, loc_parts, q, numer)
    numer, wo_odd = together(numer, wo_odd)
    rest = rest[2 * len(late) :] + odd_names(late_names)
    rest = [rest[max(i - 2, 0) : i] for i in range(len(rest), 0, -2)][::-1]
    for some in rest[:-1]:
        numer = chunk("third", [both(some)], False, False, loc_parts, q, numer)
    a0, a1 = chunk("last", [both(rest[-1])], False, True, loc_parts, q, numer)

    wo_own = [mixing_projector, wo_odd]
    w_mid = (premlp_rescaler.reshape(1, width), widening_matrix, narrowing_matrix)
    stream = (nucleotide_features, location_table, back.reshape(rows, width))

    def over_x(block):
        return [swap(block, m=2 * kx) for kx in range(1, nx)]

    def cores(blocks):
        return list(blocks) + [swap(a, m=1) for a in blocks]

    far0 = over_x(a0)
    part0 = mix_call(0, *stream, cores([a0]), wo_own)
    far1 = over_x(a1)
    part0, mix_far = together(part0, mix_far)
    wo_far = []
    for h in range(groups):
        some = mix_far[h * (nx - 1) : (h + 1) * (nx - 1)]
        wo_far += [*some, *(swap(a, m=1) for a in some)]
    part1 = mix_call(rows // 2, *stream, cores([a1]), wo_own)
    part0, part1, *far0 = together(part0, part1, *far0)
    even0, odd0, share0 = mid_call(groups, mp, scal, part0, *w_mid, cores(far0), wo_far)
    even0, odd0, share0, *far1 = together(even0, odd0, share0, *far1)
    paired0 = even0.astype(f32) + swap(odd0, m=1).astype(f32)
    part1, paired0 = together(part1, paired0)
    across0 = [swap(paired0[kx].astype(bf16), m=2 * kx) for kx in range(1, nx)]
    even1, odd1, share1 = mid_call(groups, mp, scal, part1, *w_mid, cores(far1), wo_far)
    even1, odd1, share1, *across0 = together(even1, odd1, share1, *across0)
    paired1 = even1.astype(f32) + swap(odd1, m=1).astype(f32)
    across1 = [swap(paired1[kx].astype(bf16), m=2 * kx) for kx in range(1, nx)]
    blocks = [
        0.5 * (share + paired[0] + sum(a.astype(f32) for a in arrived))
        for share, paired, arrived in ((share0, paired0, across0), (share1, paired1, across1))
    ]
    return jnp.concatenate(blocks, axis=0)


def solution(mesh):
    return jax.shard_map(
        shards,
        mesh=mesh,
        in_specs=(
            P(("groups", "seq"), None),
            P("seq", None),
            P(),
            P(None, None, "mp"),
            P(None, "mp"),
            P("mp"),
            P("mp", None),
            P(),
            P(None, "mp"),
            P("mp", None),
        ),
        out_specs=P(("groups", "seq"), "mp"),
        check_vma=False,
    )
```

```python
import functools

import jax
import jax.numpy as jnp
from jax import lax
from jax.experimental import pallas as pl
from jax.experimental.pallas import tpu as pltpu
from jax.sharding import PartitionSpec as P

epsilon = 1e-06
LOG2E = 1.4426950408889634
COST = 2**20
f32, bf16 = jnp.float32, jnp.bfloat16
AXES = ("groups", "seq", "mp")


def swap(block, g=0, s=0, m=0):
    groups, seq, mp = (lax.axis_size(name) for name in AXES)
    code = (g * seq + s) * mp + m
    return lax.ppermute(block, AXES, [(i, i ^ code) for i in range(groups * seq * mp)])


def unit(block):
    return block * lax.rsqrt(jnp.mean(block * block, axis=-1, keepdims=True) + epsilon)


def scaled_unit(block, scale, gain=None):
    mean = jnp.mean(block * block, axis=-1, keepdims=True)
    factor = scale * lax.rsqrt(scale * scale * mean + epsilon)
    return (block * (factor if gain is None else factor * gain)).astype(bf16)


def window(head, size):
    low = head * size // 128 * 128
    return low, (0 if head * size > low else size)


def dot(a, b):
    return jnp.dot(a, b, preferred_element_type=f32)


def chunk_kernel(dims, batches, where, own, last, counts, scal, *refs):
    groups, seq, mp, heads, lookup, value_size, padded = dims
    nx = mp // 2
    strands = sorted({t for batch in batches for t, r, k in batch})
    refs = list(refs)
    take = lambda n: [refs.pop(0) for _ in range(n)]
    x_refs = take(counts[0])
    (own_loc,) = take(1)
    loc_refs = take(counts[1])
    flip_ref, sharp_ref, wk_ref, wv_ref = take(4)
    wq_ref = take(1)[0] if own else None
    q_refs = [] if own else take(len(strands))
    numer_in = [] if own else take(len(strands))
    out_refs = take(2 if last else len(strands))
    if own:
        q_refs = take(1)
        back_out = take(1)[0] if 1 in strands else None
    scratch = list(zip(refs[::2], refs[1::2]))
    here_m, here_g = scal[0], scal[1]
    part, width = own_loc.shape[1:]
    half = width // groups
    columns = [pl.ds(pl.multiple_of((h ^ here_g) * half, half), half) for h in range(groups)]

    def loc_piece(r, k, h):
        if r == 0:
            return own_loc[here_m ^ k, :, columns[h]]
        return loc_refs[k & 1][h * nx + (k >> 1), r - 1]

    products = []
    for batch, (streams, scales) in zip(batches, scratch):
        group = flip_ref.shape[0] // part
        backs = {}
        mirrored = [(r, k) for t, r, k in batch if t == 1]
        for n in range(0, len(mirrored), group):
            some = mirrored[n : n + group]
            for h in range(groups):
                pieces = [loc_piece(r ^ (seq - 1), k ^ (mp - 1), h) for r, k in reversed(some)]
                size = len(some) * part
                exchange = flip_ref[:size, group * part - size :]
                flipped = dot(exchange, jnp.concatenate(pieces, axis=0)).astype(bf16)
                for i, (r, k) in enumerate(some):
                    backs[r, k, h] = flipped[i * part : (i + 1) * part]
        for i, (t, r, k) in enumerate(batch):
            ref, at = (x_refs[0], here_m ^ k) if own else (x_refs[where[r, k][0]], where[r, k][1])
            place = here_m ^ k if own else i
            square = 0.0
            for h in range(groups):
                loc = backs[r, k, h] if t else loc_piece(r, k, h)
                if t and own:
                    back_out[place, :, columns[h]] = loc
                stream = ref[at, :, columns[h]] + loc
                streams[place, :, columns[h]] = stream
                square = square + jnp.sum(jnp.square(stream.astype(f32)), axis=-1, keepdims=True)
            scales[place] = jnp.broadcast_to(lax.rsqrt(square / width + epsilon), (part, 128))
        rows = streams[...].reshape(-1, width)
        scale = scales[...].reshape(-1, 128)
        if own:
            query = dot(rows, wq_ref[...])
            for h in range(heads):
                cols = slice(h * lookup, (h + 1) * lookup)
                q_refs[0][:, cols] = scaled_unit(query[:, cols], scale, sharp_ref[h] * (LOG2E / lookup))
        products.append((scale, dot(rows, wk_ref[...]), dot(rows, wv_ref[...])))
    for p, t in enumerate(strands):
        mine = []
        for batch, product in zip(batches, products):
            places = [i for i, item in enumerate(batch) if item[0] == t]
            if places:
                rows = slice(places[0] * part, (places[-1] + 1) * part)
                mine.append([a[rows] for a in product])
        attended = []
        for h in range(heads):
            cols = slice(h * lookup, (h + 1) * lookup)
            key_n = jnp.concatenate([scaled_unit(k[:, cols], scale) for scale, k, v in mine], axis=0)
            low, spare = window(h, value_size)
            value_h = []
            for c in range(padded // 128):
                block = slice(low + c * 128, low + (c + 1) * 128)
                column = jnp.concatenate([v[:, block] * scale for scale, k, v in mine], axis=0)
                if c == spare // 128:
                    lane = lax.broadcasted_iota(jnp.int32, column.shape, 1)
                    column = jnp.where(lane == spare % 128, 1.0, column)
                value_h.append(column.astype(bf16))
            value_h = jnp.concatenate(value_h, axis=1)
            scores = lax.dot_general(
                q_refs[p][:, cols], key_n, (((1,), (1,)), ((), ())), preferred_element_type=f32
            )
            weight = jnp.exp2(scores).astype(bf16)
            numer = dot(weight, value_h)
            if not own:
                numer = numer + numer_in[p][h]
            if last:
                first = h * value_size - low
                attended.append(numer[:, first : first + value_size] / numer[:, spare : spare + 1])
            else:
                out_refs[p][h] = numer
        if last:
            attended = jnp.concatenate(attended, axis=1).astype(bf16)
            block = attended.shape[0] // len(out_refs)
            for i, out_ref in enumerate(out_refs):
                out_ref[p] = attended[i * block : (i + 1) * block]


VMEM = pl.BlockSpec(memory_space=pltpu.VMEM)
SMEM = pl.BlockSpec(memory_space=pltpu.SMEM)


def chunk_call(name, dims, batches, own, last, scal, x_parts, own_loc, loc_parts, flip, sharp, weights, q, numer):
    groups, seq, mp, heads, lookup, value_size, padded = dims
    _, part, width = own_loc.shape
    rows = part * mp
    batches = tuple(tuple(sorted(batch)) for batch in batches)
    strands = sorted({t for batch in batches for t, r, k in batch})
    where = {name: (n, i) for n, (_, names) in enumerate(x_parts) for name, i in names.items()}
    args = [a for a, _ in x_parts] + [own_loc] + list(loc_parts) + [flip, sharp] + list(weights) + list(q) + list(numer)
    specs = [SMEM if a is sharp else VMEM for a in args]
    if last:
        outs = [jax.ShapeDtypeStruct((2, rows // 2, heads * value_size), bf16)] * 2
    else:
        outs = [jax.ShapeDtypeStruct((heads, rows, padded), f32)] * len(strands)
    if own:
        outs = outs + [jax.ShapeDtypeStruct((rows, heads * lookup), bf16)]
        if 1 in strands:
            outs = outs + [jax.ShapeDtypeStruct((mp, part, width), bf16)]
    scratch = []
    for batch in batches:
        scratch += [pltpu.VMEM((len(batch), part, width), bf16), pltpu.VMEM((len(batch), part, 128), f32)]
    return pl.pallas_call(
        functools.partial(chunk_kernel, dims, batches, where, own, last, (len(x_parts), len(loc_parts))),
        out_shape=outs,
        in_specs=[SMEM] + specs,
        out_specs=[VMEM] * len(outs),
        scratch_shapes=scratch,
        compiler_params=pltpu.CompilerParams(vmem_limit_bytes=40 * 2**20),
        cost_estimate=pl.CostEstimate(flops=COST, bytes_accessed=COST, transcendentals=0),
        name=name,
    )(scal, *args)


def mix_kernel(lo, x_ref, loc_ref, back_ref, att0, att1, wo0, wo1, out_ref):
    rows = out_ref.shape[1]
    mixed = dot(att0[...].reshape(2 * rows, -1), wo0[...]) + dot(att1[...].reshape(2 * rows, -1), wo1[...])
    x_f = x_ref[lo : lo + rows].astype(f32)
    for t, loc in enumerate((loc_ref, back_ref)):
        out_ref[t] = x_f + loc[lo : lo + rows].astype(f32) + mixed[t * rows : (t + 1) * rows]


def mix_call(lo, x, loc, back, att, wo):
    rows, width = att[0].shape[1], x.shape[1]
    return pl.pallas_call(
        functools.partial(mix_kernel, lo),
        out_shape=jax.ShapeDtypeStruct((2, rows, width), f32),
        in_specs=[VMEM] * 7,
        out_specs=VMEM,
        compiler_params=pltpu.CompilerParams(vmem_limit_bytes=32 * 2**20),
        cost_estimate=pl.CostEstimate(
            flops=8 * rows * width * wo[0].shape[0], bytes_accessed=8 * 2**20, transcendentals=0
        ),
        name="mix",
    )(x, loc, back, *att, *wo)


def mid_kernel(groups, scal, *refs):
    partial, gain_ref, w1_ref, w2_ref, *refs = refs
    even_out, odd_out, middle_out, summed, mixed = refs[-5:]
    refs = refs[:-5]
    att, wo = refs[: len(refs) // (1 + groups)], refs[len(refs) // (1 + groups) :]
    here_m, here_g = scal[0], scal[1]
    rows = partial.shape[1]
    half = partial.shape[2] // groups
    blocks = [a_ref[...].reshape(2 * rows, -1) for a_ref in att]
    for h in range(groups):
        columns = pl.ds(pl.multiple_of((h ^ here_g) * half, half), half)
        part = partial[:, :, columns].reshape(2 * rows, half)
        mixed[:, columns] = part + sum(dot(a, w[...]) for a, w in zip(blocks, wo[h * len(att) : (h + 1) * len(att)]))
    middle = mixed[...]
    normed = (unit(middle) * gain_ref[...]).astype(bf16)
    expanded = jax.nn.gelu(dot(normed, w1_ref[...]), approximate=True).astype(bf16)
    out = dot(expanded, w2_ref[...])
    out = out[:rows] + out[rows:]
    both = middle[:rows] + middle[rows:]
    mp, _, share = summed.shape
    for j in range(mp):
        summed[j] = out[:, j * share : (j + 1) * share].astype(bf16)
    for k in range(mp):
        (odd_out if k & 1 else even_out)[k >> 1] = summed[here_m ^ k]
    for j in range(mp):
        block = both[:, j * share : (j + 1) * share]

        @pl.when(here_m == j)
        def _():
            middle_out[...] = block


def mid_call(groups, mp, scal, partial, gain, w1, w2, att, wo):
    _, rows, width = partial.shape
    share = width // mp
    args = [partial, gain, w1, w2, *att, *wo]
    return pl.pallas_call(
        functools.partial(mid_kernel, groups),
        out_shape=[jax.ShapeDtypeStruct((mp // 2, rows, share), bf16)] * 2 + [jax.ShapeDtypeStruct((rows, share), f32)],
        in_specs=[SMEM] + [VMEM] * len(args),
        out_specs=[VMEM] * 3,
        scratch_shapes=[pltpu.VMEM((mp, rows, share), bf16), pltpu.VMEM((2 * rows, width), f32)],
        compiler_params=pltpu.CompilerParams(vmem_limit_bytes=40 * 2**20),
        cost_estimate=pl.CostEstimate(
            flops=4 * rows * width * (width // 2 + 2 * w1.shape[1]),
            bytes_accessed=14 * 2**20,
            transcendentals=2 * rows * w1.shape[1],
        ),
        name="middle",
    )(scal, *args)


def stack_kernel(*refs):
    for i, ref in enumerate(refs[:-1]):
        refs[-1][i] = ref[...]


def stack_call(arrays):
    shape = (len(arrays),) + arrays[0].shape
    return pl.pallas_call(
        stack_kernel,
        out_shape=jax.ShapeDtypeStruct(shape, arrays[0].dtype),
        in_specs=[VMEM] * len(arrays),
        out_specs=VMEM,
        compiler_params=pltpu.CompilerParams(vmem_limit_bytes=40 * 2**20),
        cost_estimate=pl.CostEstimate(flops=COST, bytes_accessed=COST, transcendentals=0),
        name="stack",
    )(*arrays)


def together(*arrays):
    return lax.optimization_barrier(arrays)


def shards(
    nucleotide_features,
    location_table,
    premix_rescaler,
    probe_lookup_matrices,
    payload_projector,
    logit_sharpness,
    mixing_projector,
    premlp_rescaler,
    widening_matrix,
    narrowing_matrix,
):
    rows, width = nucleotide_features.shape
    heads = logit_sharpness.shape[0]
    lookup = probe_lookup_matrices.shape[2] // heads
    value_size = payload_projector.shape[1] // heads
    padded = (value_size // 128 + 1) * 128
    groups, seq, mp = (lax.axis_size(name) for name in AXES)
    here_g, here_m = lax.axis_index("groups"), lax.axis_index("mp")
    nx = mp // 2
    part, half = rows // mp, width // groups
    dims = (groups, seq, mp, heads, lookup, value_size, padded)
    scal = jnp.stack([here_m, here_g]).astype(jnp.int32)
    x_own = nucleotide_features.reshape(mp, part, width)
    loc_own = location_table.reshape(mp, part, width)

    place = lax.broadcasted_iota(jnp.int32, (2 * part, 2 * part), 0) + lax.broadcasted_iota(jnp.int32, (2 * part, 2 * part), 1)
    flip = (place == 2 * part - 1).astype(bf16)
    gain = premix_rescaler.reshape(width, 1)
    wq, wk = [(gain * w.astype(f32)).astype(bf16) for w in (probe_lookup_matrices[0], probe_lookup_matrices[1])]
    wv = (gain * payload_projector.astype(f32)).astype(bf16)
    wv = jnp.pad(wv, ((0, 0), (0, -wv.shape[1] % 128)))

    have = {}

    def hold(array, names):
        have.update({name: (array, i) for i, name in enumerate(names)})

    def chunk(name, batches, own, last, loc_parts, q=(), numer=()):
        flip, wq, wk, wv = prepared
        weights = (wk, wv, wq) if own else (wk, wv)
        x_parts = {}
        for r, k in sorted({item[1:] for batch in batches for item in batch}):
            array, i = have[r, k]
            x_parts.setdefault(id(array), (array, {}))[1][r, k] = i
        return chunk_call(
            name, dims, batches, own, last, scal, list(x_parts.values()), loc_own, loc_parts,
            flip, logit_sharpness, weights, q, numer,
        )

    direct = range(3, seq, 2)
    loc_part = lax.dynamic_slice(location_table, (here_m * part, here_g * half), (part, half))
    loc_part, mix_first, x_first = together(loc_part, mixing_projector, x_own)
    mix_part = lax.dynamic_slice_in_dim(mix_first, here_g * half, half, 1)
    mix_x = [swap(mix_part, m=2 * kx) for kx in range(1, nx)]
    loc_z = [swap(loc_part, s=r) for r in range(1, seq)]
    x_mine = lax.dynamic_slice_in_dim(x_first, here_m, 1, 0)
    x_direct = [swap(x_mine, s=r) for r in direct]

    x_mine, flip, wq, wk, wv, loc_z = together(x_mine, flip, wq, wk, wv, loc_z)
    prepared = (flip, wq, wk, wv)
    loc_far = stack_call(loc_z)
    x_near = swap(x_mine, s=1)
    loc_xy = [loc_far] + [swap(loc_far, m=2 * kx) for kx in range(1, nx)]
    loc_y = [swap(loc_far, g=h) for h in range(1, groups)]
    x_direct, x_near, mix_x, loc_y = together(x_direct, x_near, mix_x, loc_y)
    loc_xy = loc_xy + [a for h in range(1, groups) for a in (loc_y[h - 1], *(swap(a, g=h) for a in loc_xy[1:]))]
    mix_far = [swap(a, g=h) if h else a for h in range(groups) for a in mix_x]
    x_relayed = [swap(a, s=1) for a in x_direct]
    x_across = [swap(a, m=2 * kx) for a in x_direct for kx in range(1, nx)]
    hold(x_own, [(0, k) for k in range(mp)])
    numer0, q0 = chunk("own_forward", [[(0, 0, k) for k in range(mp)]], True, False, [])

    x_near_across = [swap(x_near, m=2 * kx) for kx in range(1, nx)]
    numer0, loc_xy, *held = together(numer0, loc_xy, *x_relayed, x_near, *x_direct, *x_near_across)
    loc_even = stack_call(loc_xy)
    loc_odd = swap(loc_even, m=1)
    names = [[(r - 1, 0)] for r in direct] + [[(1, 0)]] + [[(r, 0)] for r in direct]
    names += [[(1, 2 * kx)] for kx in range(1, nx)]
    odd_names = lambda names: [(r, k + 1) for r, k in names]
    both = lambda names: [(t, r, k) for t in range(2) for r, k in names]
    for array, some in zip(held, names):
        hold(array, some)
        hold(swap(array, m=1), odd_names(some))
    early = [name for some in names for name in some]
    early = [early[i : i + 4] for i in range(0, len(early), 4)]
    x_late = [swap(a, m=2 * kx) for a in held[: len(direct)] for kx in range(1, nx)] + x_across
    late_names = [(r, 2 * kx) for r in [*(r - 1 for r in direct), *direct] for kx in range(1, nx)]
    loc_parts = [loc_even, loc_odd]
    numer1, q1, back = chunk("own_back", [[(1, 0, k) for k in range(mp)]], True, False, loc_parts)
    q, numer = [q0, q1], [numer0, numer1]
    for some in early:
        numer = chunk("first", [both(some), both(odd_names(some))], False, False, loc_parts, q, numer)
    numer, *x_late = together(numer, *x_late)
    wo_odd = swap(mixing_projector, m=1)
    for name, array in zip(late_names, x_late):
        hold(array, [name])
        hold(swap(array, m=1), odd_names([name]))
    late = [late_names[i : i + 2] for i in range(0, len(late_names), 2)]
    for some in late:
        numer = chunk("second", [both(some)], False, False, loc_parts, q, numer)
    numer, wo_odd = together(numer, wo_odd)
    for some in late[:-1]:
        numer = chunk("third", [both(odd_names(some))], False, False, loc_parts, q, numer)
    a0, a1 = chunk("last", [both(odd_names(late[-1]))], False, True, loc_parts, q, numer)

    wo_own = [mixing_projector, wo_odd]
    w_mid = (premlp_rescaler.reshape(1, width), widening_matrix, narrowing_matrix)
    stream = (nucleotide_features, location_table, back.reshape(rows, width))

    def over_x(block):
        return [swap(block, m=2 * kx) for kx in range(1, nx)]

    def cores(blocks):
        return list(blocks) + [swap(a, m=1) for a in blocks]

    far0 = over_x(a0)
    part0 = mix_call(0, *stream, cores([a0]), wo_own)
    far1 = over_x(a1)
    part0, mix_far = together(part0, mix_far)
    wo_far = []
    for h in range(groups):
        some = mix_far[h * (nx - 1) : (h + 1) * (nx - 1)]
        wo_far += [*some, *(swap(a, m=1) for a in some)]
    part1 = mix_call(rows // 2, *stream, cores([a1]), wo_own)
    part0, part1, *far0 = together(part0, part1, *far0)
    even0, odd0, share0 = mid_call(groups, mp, scal, part0, *w_mid, cores(far0), wo_far)
    even0, odd0, share0, *far1 = together(even0, odd0, share0, *far1)
    paired0 = even0.astype(f32) + swap(odd0, m=1).astype(f32)
    part1, paired0 = together(part1, paired0)
    across0 = [swap(paired0[kx].astype(bf16), m=2 * kx) for kx in range(1, nx)]
    even1, odd1, share1 = mid_call(groups, mp, scal, part1, *w_mid, cores(far1), wo_far)
    even1, odd1, share1, *across0 = together(even1, odd1, share1, *across0)
    paired1 = even1.astype(f32) + swap(odd1, m=1).astype(f32)
    across1 = [swap(paired1[kx].astype(bf16), m=2 * kx) for kx in range(1, nx)]
    blocks = [
        0.5 * (share + paired[0] + sum(a.astype(f32) for a in arrived))
        for share, paired, arrived in ((share0, paired0, across0), (share1, paired1, across1))
    ]
    return jnp.concatenate(blocks, axis=0)


def solution(mesh):
    return jax.shard_map(
        shards,
        mesh=mesh,
        in_specs=(
            P(("groups", "seq"), None),
            P("seq", None),
            P(),
            P(None, None, "mp"),
            P(None, "mp"),
            P("mp"),
            P("mp", None),
            P(),
            P(None, "mp"),
            P("mp", None),
        ),
        out_specs=P(("groups", "seq"), "mp"),
        check_vma=False,
    )
```

```python
import functools

import jax
import jax.numpy as jnp
from jax import lax
from jax.experimental import pallas as pl
from jax.experimental.pallas import tpu as pltpu
from jax.sharding import PartitionSpec as P

epsilon = 1e-06
LOG2E = 1.4426950408889634
COST = 2**20
f32, bf16 = jnp.float32, jnp.bfloat16
AXES = ("groups", "seq", "mp")


def swap(block, g=0, s=0, m=0):
    groups, seq, mp = (lax.axis_size(name) for name in AXES)
    code = (g * seq + s) * mp + m
    return lax.ppermute(block, AXES, [(i, i ^ code) for i in range(groups * seq * mp)])


def unit(block):
    return block * lax.rsqrt(jnp.mean(block * block, axis=-1, keepdims=True) + epsilon)


def scaled_unit(block, scale, gain=None):
    mean = jnp.mean(block * block, axis=-1, keepdims=True)
    factor = scale * lax.rsqrt(scale * scale * mean + epsilon)
    return (block * (factor if gain is None else factor * gain)).astype(bf16)


def window(head, size):
    low = head * size // 128 * 128
    return low, (0 if head * size > low else size)


def dot(a, b):
    return jnp.dot(a, b, preferred_element_type=f32)


def chunk_kernel(dims, batches, where, own, last, counts, scal, *refs):
    groups, seq, mp, heads, lookup, value_size, padded = dims
    nx = mp // 2
    strands = sorted({t for batch in batches for t, r, k in batch})
    refs = list(refs)
    take = lambda n: [refs.pop(0) for _ in range(n)]
    x_refs = take(counts[0])
    (own_loc,) = take(1)
    loc_refs = take(counts[1])
    flip_ref, sharp_ref, wk_ref, wv_ref = take(4)
    wq_ref = take(1)[0] if own else None
    q_refs = [] if own else take(len(strands))
    numer_in = [] if own else take(len(strands))
    out_refs = take(2 if last else len(strands))
    if own:
        q_refs = take(1)
        back_out = take(1)[0] if 1 in strands else None
    scratch = list(zip(refs[::2], refs[1::2]))
    here_m, here_g = scal[0], scal[1]
    part, width = own_loc.shape[1:]
    half = width // groups
    columns = [pl.ds(pl.multiple_of((h ^ here_g) * half, half), half) for h in range(groups)]

    def loc_piece(r, k, h):
        if r == 0:
            return own_loc[here_m ^ k, :, columns[h]]
        return loc_refs[k & 1][h * nx + (k >> 1), r - 1]

    products = []
    for batch, (streams, scales) in zip(batches, scratch):
        group = flip_ref.shape[0] // part
        backs = {}
        mirrored = [(r, k) for t, r, k in batch if t == 1]
        for n in range(0, len(mirrored), group):
            some = mirrored[n : n + group]
            for h in range(groups):
                pieces = [loc_piece(r ^ (seq - 1), k ^ (mp - 1), h) for r, k in reversed(some)]
                size = len(some) * part
                exchange = flip_ref[:size, group * part - size :]
                flipped = dot(exchange, jnp.concatenate(pieces, axis=0)).astype(bf16)
                for i, (r, k) in enumerate(some):
                    backs[r, k, h] = flipped[i * part : (i + 1) * part]
        for i, (t, r, k) in enumerate(batch):
            ref, at = (x_refs[0], here_m ^ k) if own else (x_refs[where[r, k][0]], where[r, k][1])
            place = here_m ^ k if own else i
            square = 0.0
            for h in range(groups):
                loc = backs[r, k, h] if t else loc_piece(r, k, h)
                if t and own:
                    back_out[place, :, columns[h]] = loc
                stream = ref[at, :, columns[h]] + loc
                streams[place, :, columns[h]] = stream
                square = square + jnp.sum(jnp.square(stream.astype(f32)), axis=-1, keepdims=True)
            scales[place] = jnp.broadcast_to(lax.rsqrt(square / width + epsilon), (part, 128))
        rows = streams[...].reshape(-1, width)
        scale = scales[...].reshape(-1, 128)
        if own:
            query = dot(rows, wq_ref[...])
            for h in range(heads):
                cols = slice(h * lookup, (h + 1) * lookup)
                q_refs[0][:, cols] = scaled_unit(query[:, cols], scale, sharp_ref[h] * (LOG2E / lookup))
        products.append((scale, dot(rows, wk_ref[...]), dot(rows, wv_ref[...])))
    for p, t in enumerate(strands):
        mine = []
        for batch, product in zip(batches, products):
            places = [i for i, item in enumerate(batch) if item[0] == t]
            if places:
                rows = slice(places[0] * part, (places[-1] + 1) * part)
                mine.append([a[rows] for a in product])
        attended = []
        for h in range(heads):
            cols = slice(h * lookup, (h + 1) * lookup)
            key_n = jnp.concatenate([scaled_unit(k[:, cols], scale) for scale, k, v in mine], axis=0)
            low, spare = window(h, value_size)
            value_h = []
            for c in range(padded // 128):
                block = slice(low + c * 128, low + (c + 1) * 128)
                column = jnp.concatenate([v[:, block] * scale for scale, k, v in mine], axis=0)
                if c == spare // 128:
                    lane = lax.broadcasted_iota(jnp.int32, column.shape, 1)
                    column = jnp.where(lane == spare % 128, 1.0, column)
                value_h.append(column.astype(bf16))
            value_h = jnp.concatenate(value_h, axis=1)
            scores = lax.dot_general(
                q_refs[p][:, cols], key_n, (((1,), (1,)), ((), ())), preferred_element_type=f32
            )
            weight = jnp.exp2(scores).astype(bf16)
            numer = dot(weight, value_h)
            if not own:
                numer = numer + numer_in[p][h]
            if last:
                first = h * value_size - low
                attended.append(numer[:, first : first + value_size] / numer[:, spare : spare + 1])
            else:
                out_refs[p][h] = numer
        if last:
            attended = jnp.concatenate(attended, axis=1).astype(bf16)
            block = attended.shape[0] // len(out_refs)
            for i, out_ref in enumerate(out_refs):
                out_ref[p] = attended[i * block : (i + 1) * block]


VMEM = pl.BlockSpec(memory_space=pltpu.VMEM)
SMEM = pl.BlockSpec(memory_space=pltpu.SMEM)


def chunk_call(name, dims, batches, own, last, scal, x_parts, own_loc, loc_parts, flip, sharp, weights, q, numer):
    groups, seq, mp, heads, lookup, value_size, padded = dims
    _, part, width = own_loc.shape
    rows = part * mp
    batches = tuple(tuple(sorted(batch)) for batch in batches)
    strands = sorted({t for batch in batches for t, r, k in batch})
    where = {name: (n, i) for n, (_, names) in enumerate(x_parts) for name, i in names.items()}
    args = [a for a, _ in x_parts] + [own_loc] + list(loc_parts) + [flip, sharp] + list(weights) + list(q) + list(numer)
    specs = [SMEM if a is sharp else VMEM for a in args]
    if last:
        outs = [jax.ShapeDtypeStruct((2, rows // 2, heads * value_size), bf16)] * 2
    else:
        outs = [jax.ShapeDtypeStruct((heads, rows, padded), f32)] * len(strands)
    if own:
        outs = outs + [jax.ShapeDtypeStruct((rows, heads * lookup), bf16)]
        if 1 in strands:
            outs = outs + [jax.ShapeDtypeStruct((mp, part, width), bf16)]
    scratch = []
    for batch in batches:
        scratch += [pltpu.VMEM((len(batch), part, width), bf16), pltpu.VMEM((len(batch), part, 128), f32)]
    return pl.pallas_call(
        functools.partial(chunk_kernel, dims, batches, where, own, last, (len(x_parts), len(loc_parts))),
        out_shape=outs,
        in_specs=[SMEM] + specs,
        out_specs=[VMEM] * len(outs),
        scratch_shapes=scratch,
        compiler_params=pltpu.CompilerParams(vmem_limit_bytes=40 * 2**20),
        cost_estimate=pl.CostEstimate(flops=COST, bytes_accessed=COST, transcendentals=0),
        name=name,
    )(scal, *args)


def mix_kernel(lo, x_ref, loc_ref, back_ref, att0, att1, wo0, wo1, out_ref):
    rows = out_ref.shape[1]
    mixed = dot(att0[...].reshape(2 * rows, -1), wo0[...]) + dot(att1[...].reshape(2 * rows, -1), wo1[...])
    x_f = x_ref[lo : lo + rows].astype(f32)
    for t, loc in enumerate((loc_ref, back_ref)):
        out_ref[t] = x_f + loc[lo : lo + rows].astype(f32) + mixed[t * rows : (t + 1) * rows]


def mix_call(lo, x, loc, back, att, wo):
    rows, width = att[0].shape[1], x.shape[1]
    return pl.pallas_call(
        functools.partial(mix_kernel, lo),
        out_shape=jax.ShapeDtypeStruct((2, rows, width), f32),
        in_specs=[VMEM] * 7,
        out_specs=VMEM,
        compiler_params=pltpu.CompilerParams(vmem_limit_bytes=32 * 2**20),
        cost_estimate=pl.CostEstimate(
            flops=8 * rows * width * wo[0].shape[0], bytes_accessed=8 * 2**20, transcendentals=0
        ),
        name="mix",
    )(x, loc, back, *att, *wo)


def mid_kernel(groups, scal, *refs):
    partial, gain_ref, w1_ref, w2_ref, *refs = refs
    even_out, odd_out, middle_out, summed, mixed = refs[-5:]
    refs = refs[:-5]
    att, wo = refs[: len(refs) // (1 + groups)], refs[len(refs) // (1 + groups) :]
    here_m, here_g = scal[0], scal[1]
    rows = partial.shape[1]
    half = partial.shape[2] // groups
    blocks = [a_ref[...].reshape(2 * rows, -1) for a_ref in att]
    for h in range(groups):
        columns = pl.ds(pl.multiple_of((h ^ here_g) * half, half), half)
        part = partial[:, :, columns].reshape(2 * rows, half)
        mixed[:, columns] = part + sum(dot(a, w[...]) for a, w in zip(blocks, wo[h * len(att) : (h + 1) * len(att)]))
    middle = mixed[...]
    normed = (unit(middle) * gain_ref[...]).astype(bf16)
    expanded = jax.nn.gelu(dot(normed, w1_ref[...]), approximate=True).astype(bf16)
    out = dot(expanded, w2_ref[...])
    out = out[:rows] + out[rows:]
    both = middle[:rows] + middle[rows:]
    mp, _, share = summed.shape
    for j in range(mp):
        summed[j] = out[:, j * share : (j + 1) * share].astype(bf16)
    for k in range(mp):
        (odd_out if k & 1 else even_out)[k >> 1] = summed[here_m ^ k]
    for j in range(mp):
        block = both[:, j * share : (j + 1) * share]

        @pl.when(here_m == j)
        def _():
            middle_out[...] = block


def mid_call(groups, mp, scal, partial, gain, w1, w2, att, wo):
    _, rows, width = partial.shape
    share = width // mp
    args = [partial, gain, w1, w2, *att, *wo]
    return pl.pallas_call(
        functools.partial(mid_kernel, groups),
        out_shape=[jax.ShapeDtypeStruct((mp // 2, rows, share), bf16)] * 2 + [jax.ShapeDtypeStruct((rows, share), f32)],
        in_specs=[SMEM] + [VMEM] * len(args),
        out_specs=[VMEM] * 3,
        scratch_shapes=[pltpu.VMEM((mp, rows, share), bf16), pltpu.VMEM((2 * rows, width), f32)],
        compiler_params=pltpu.CompilerParams(vmem_limit_bytes=40 * 2**20),
        cost_estimate=pl.CostEstimate(
            flops=4 * rows * width * (width // 2 + 2 * w1.shape[1]),
            bytes_accessed=14 * 2**20,
            transcendentals=2 * rows * w1.shape[1],
        ),
        name="middle",
    )(scal, *args)


def stack_kernel(*refs):
    for i, ref in enumerate(refs[:-1]):
        refs[-1][i] = ref[...]


def stack_call(arrays):
    shape = (len(arrays),) + arrays[0].shape
    return pl.pallas_call(
        stack_kernel,
        out_shape=jax.ShapeDtypeStruct(shape, arrays[0].dtype),
        in_specs=[VMEM] * len(arrays),
        out_specs=VMEM,
        compiler_params=pltpu.CompilerParams(vmem_limit_bytes=40 * 2**20),
        cost_estimate=pl.CostEstimate(flops=COST, bytes_accessed=COST, transcendentals=0),
        name="stack",
    )(*arrays)


def together(*arrays):
    return lax.optimization_barrier(arrays)


def shards(
    nucleotide_features,
    location_table,
    premix_rescaler,
    probe_lookup_matrices,
    payload_projector,
    logit_sharpness,
    mixing_projector,
    premlp_rescaler,
    widening_matrix,
    narrowing_matrix,
):
    rows, width = nucleotide_features.shape
    heads = logit_sharpness.shape[0]
    lookup = probe_lookup_matrices.shape[2] // heads
    value_size = payload_projector.shape[1] // heads
    padded = (value_size // 128 + 1) * 128
    groups, seq, mp = (lax.axis_size(name) for name in AXES)
    here_g, here_m = lax.axis_index("groups"), lax.axis_index("mp")
    nx = mp // 2
    part, half = rows // mp, width // groups
    dims = (groups, seq, mp, heads, lookup, value_size, padded)
    scal = jnp.stack([here_m, here_g]).astype(jnp.int32)
    x_own = nucleotide_features.reshape(mp, part, width)
    loc_own = location_table.reshape(mp, part, width)

    place = lax.broadcasted_iota(jnp.int32, (2 * part, 2 * part), 0) + lax.broadcasted_iota(jnp.int32, (2 * part, 2 * part), 1)
    flip = (place == 2 * part - 1).astype(bf16)
    gain = premix_rescaler.reshape(width, 1)
    wq, wk = [(gain * w.astype(f32)).astype(bf16) for w in (probe_lookup_matrices[0], probe_lookup_matrices[1])]
    wv = (gain * payload_projector.astype(f32)).astype(bf16)
    wv = jnp.pad(wv, ((0, 0), (0, -wv.shape[1] % 128)))

    have = {}

    def hold(array, names):
        have.update({name: (array, i) for i, name in enumerate(names)})

    def chunk(name, batches, own, last, loc_parts, q=(), numer=()):
        flip, wq, wk, wv = prepared
        weights = (wk, wv, wq) if own else (wk, wv)
        x_parts = {}
        for r, k in sorted({item[1:] for batch in batches for item in batch}):
            array, i = have[r, k]
            x_parts.setdefault(id(array), (array, {}))[1][r, k] = i
        return chunk_call(
            name, dims, batches, own, last, scal, list(x_parts.values()), loc_own, loc_parts,
            flip, logit_sharpness, weights, q, numer,
        )

    direct = range(3, seq, 2)
    loc_part = lax.dynamic_slice(location_table, (here_m * part, here_g * half), (part, half))
    loc_part, mix_first, x_first = together(loc_part, mixing_projector, x_own)
    mix_part = lax.dynamic_slice_in_dim(mix_first, here_g * half, half, 1)
    mix_x = [swap(mix_part, m=2 * kx) for kx in range(1, nx)]
    loc_z = [swap(loc_part, s=r) for r in range(1, seq)]
    x_mine = lax.dynamic_slice_in_dim(x_first, here_m, 1, 0)
    x_direct = [swap(x_mine, s=r) for r in direct]

    x_mine, flip, wq, wk, wv, loc_z = together(x_mine, flip, wq, wk, wv, loc_z)
    prepared = (flip, wq, wk, wv)
    loc_far = stack_call(loc_z)
    x_near = swap(x_mine, s=1)
    loc_xy = [loc_far] + [swap(loc_far, m=2 * kx) for kx in range(1, nx)]
    loc_y = [swap(loc_far, g=h) for h in range(1, groups)]
    x_direct, x_near, mix_x, loc_y = together(x_direct, x_near, mix_x, loc_y)
    loc_xy = loc_xy + [a for h in range(1, groups) for a in (loc_y[h - 1], *(swap(a, g=h) for a in loc_xy[1:]))]
    mix_far = [swap(a, g=h) if h else a for h in range(groups) for a in mix_x]
    x_relayed = [swap(a, s=1) for a in x_direct]
    x_across = [swap(a, m=2 * kx) for a in x_direct for kx in range(1, nx)]
    hold(x_own, [(0, k) for k in range(mp)])
    numer0, q0 = chunk("own_forward", [[(0, 0, k) for k in range(mp)]], True, False, [])

    x_near_across = [swap(x_near, m=2 * kx) for kx in range(1, nx)]
    numer0, loc_xy, *held = together(numer0, loc_xy, *x_relayed, x_near, *x_direct, *x_near_across)
    loc_even = stack_call(loc_xy)
    loc_odd = swap(loc_even, m=1)
    names = [[(r - 1, 0)] for r in direct] + [[(1, 0)]] + [[(r, 0)] for r in direct]
    names += [[(1, 2 * kx)] for kx in range(1, nx)]
    odd_names = lambda names: [(r, k + 1) for r, k in names]
    both = lambda names: [(t, r, k) for t in range(2) for r, k in names]
    hold(stack_call([a[0] for a in held]), [name for some in names for name in some])
    hold(swap(have[names[0][0]][0], m=1), odd_names([name for some in names for name in some]))
    early = [name for some in names for name in some]
    early = [early[i : i + 4] for i in range(0, len(early), 4)]
    x_late = [swap(a, m=2 * kx) for a in held[: len(direct)] for kx in range(1, nx)] + x_across
    late_names = [(r, 2 * kx) for r in [*(r - 1 for r in direct), *direct] for kx in range(1, nx)]
    loc_parts = [loc_even, loc_odd]
    numer1, q1, back = chunk("own_back", [[(1, 0, k) for k in range(mp)]], True, False, loc_parts)
    q, numer = [q0, q1], [numer0, numer1]
    for some in early:
        numer = chunk("first", [both(some), both(odd_names(some))], False, False, loc_parts, q, numer)
    numer, mixing, *x_late = together(numer, mixing_projector, *x_late)
    x_late = stack_call([a[0] for a in x_late])
    hold(x_late, late_names)
    x_late_odd = swap(x_late, m=1)
    wo_odd = swap(mixing, m=1)
    late = [late_names[i : i + 2] for i in range(0, len(late_names), 2)]
    for some in late:
        numer = chunk("second", [both(some)], False, False, loc_parts, q, numer)
    numer, wo_odd, x_late_odd = together(numer, wo_odd, x_late_odd)
    hold(x_late_odd, odd_names(late_names))
    for some in late[:-1]:
        numer = chunk("third", [both(odd_names(some))], False, False, loc_parts, q, numer)
    a0, a1 = chunk("last", [both(odd_names(late[-1]))], False, True, loc_parts, q, numer)

    wo_own = [mixing_projector, wo_odd]
    w_mid = (premlp_rescaler.reshape(1, width), widening_matrix, narrowing_matrix)
    stream = (nucleotide_features, location_table, back.reshape(rows, width))

    def over_x(block):
        return [swap(block, m=2 * kx) for kx in range(1, nx)]

    def cores(blocks):
        return list(blocks) + [swap(a, m=1) for a in blocks]

    far0 = over_x(a0)
    part0 = mix_call(0, *stream, cores([a0]), wo_own)
    far1 = over_x(a1)
    part1 = mix_call(rows // 2, *stream, cores([a1]), wo_own)
    part0, part1, mix_far = together(part0, part1, mix_far)
    wo_far = []
    for h in range(groups):
        some = mix_far[h * (nx - 1) : (h + 1) * (nx - 1)]
        wo_far += [*some, *(swap(a, m=1) for a in some)]
    part0, part1, *far0 = together(part0, part1, *far0)
    even0, odd0, share0 = mid_call(groups, mp, scal, part0, *w_mid, cores(far0), wo_far)
    even0, odd0, share0, *far1 = together(even0, odd0, share0, *far1)
    paired0 = even0.astype(f32) + swap(odd0, m=1).astype(f32)
    part1, paired0 = together(part1, paired0)
    across0 = [swap(paired0[kx].astype(bf16), m=2 * kx) for kx in range(1, nx)]
    even1, odd1, share1 = mid_call(groups, mp, scal, part1, *w_mid, cores(far1), wo_far)
    even1, odd1, share1, *across0 = together(even1, odd1, share1, *across0)
    paired1 = even1.astype(f32) + swap(odd1, m=1).astype(f32)
    across1 = [swap(paired1[kx].astype(bf16), m=2 * kx) for kx in range(1, nx)]
    blocks = [
        0.5 * (share + paired[0] + sum(a.astype(f32) for a in arrived))
        for share, paired, arrived in ((share0, paired0, across0), (share1, paired1, across1))
    ]
    return jnp.concatenate(blocks, axis=0)


def solution(mesh):
    return jax.shard_map(
        shards,
        mesh=mesh,
        in_specs=(
            P(("groups", "seq"), None),
            P("seq", None),
            P(),
            P(None, None, "mp"),
            P(None, "mp"),
            P("mp"),
            P("mp", None),
            P(),
            P(None, "mp"),
            P("mp", None),
        ),
        out_specs=P(("groups", "seq"), "mp"),
        check_vma=False,
    )
```

```python
import functools

import jax
import jax.numpy as jnp
from jax import lax
from jax.experimental import pallas as pl
from jax.experimental.pallas import tpu as pltpu
from jax.sharding import PartitionSpec as P

epsilon = 1e-06
LOG2E = 1.4426950408889634
COST = 2**20
f32, bf16 = jnp.float32, jnp.bfloat16
AXES = ("groups", "seq", "mp")


def swap(block, g=0, s=0, m=0):
    groups, seq, mp = (lax.axis_size(name) for name in AXES)
    code = (g * seq + s) * mp + m
    return lax.ppermute(block, AXES, [(i, i ^ code) for i in range(groups * seq * mp)])


def unit(block):
    return block * lax.rsqrt(jnp.mean(block * block, axis=-1, keepdims=True) + epsilon)


def scaled_unit(block, scale, gain=None):
    mean = jnp.mean(block * block, axis=-1, keepdims=True)
    factor = scale * lax.rsqrt(scale * scale * mean + epsilon)
    return (block * (factor if gain is None else factor * gain)).astype(bf16)


def window(head, size):
    low = head * size // 128 * 128
    return low, (0 if head * size > low else size)


def dot(a, b):
    return jnp.dot(a, b, preferred_element_type=f32)


def chunk_kernel(dims, batches, where, last, counts, scal, *refs):
    groups, seq, mp, heads, lookup, value_size, padded = dims
    nx = mp // 2
    strands = sorted({t for batch in batches for t, r, k in batch})
    refs = list(refs)
    take = lambda n: [refs.pop(0) for _ in range(n)]
    x_refs = take(counts[0])
    (own_loc,) = take(1)
    loc_refs = take(counts[1])
    flip_ref, sharp_ref, wk_ref, wv_ref = take(4)
    own = batches[0][0][0] if batches[0][0][1] == 0 else None
    wq_ref = None if own is None else take(1)[0]
    q_refs = {t: take(1)[0] for t in strands if t != own}
    numer_in = {t: take(1)[0] for t in strands if t != own}
    out_refs = take(3 if last else len(strands))
    if own is not None:
        q_refs[own] = take(1)[0]
        back_out = take(1)[0] if own else None
    scratch = list(zip(refs[::2], refs[1::2]))
    here_m, here_g = scal[0], scal[1]
    part, width = own_loc.shape[1:]
    half = width // groups
    columns = [pl.ds(pl.multiple_of((h ^ here_g) * half, half), half) for h in range(groups)]

    def loc_piece(r, k, h):
        if r == 0:
            return own_loc[here_m ^ k, :, columns[h]]
        return loc_refs[k & 1][h * nx + (k >> 1), r - 1]

    products = []
    for batch, (streams, scales) in zip(batches, scratch):
        group = flip_ref.shape[0] // part
        backs = {}
        mirrored = [(r, k) for t, r, k in batch if t == 1]
        for n in range(0, len(mirrored), group):
            some = mirrored[n : n + group]
            for h in range(groups):
                pieces = [loc_piece(r ^ (seq - 1), k ^ (mp - 1), h) for r, k in reversed(some)]
                size = len(some) * part
                exchange = flip_ref[:size, group * part - size :]
                flipped = dot(exchange, jnp.concatenate(pieces, axis=0)).astype(bf16)
                for i, (r, k) in enumerate(some):
                    backs[r, k, h] = flipped[i * part : (i + 1) * part]
        for i, (t, r, k) in enumerate(batch):
            ref, at = x_refs[where[r, k][0]], where[r, k][1] if r else here_m ^ k
            place = i if r else here_m ^ k
            square = 0.0
            for h in range(groups):
                loc = backs[r, k, h] if t else loc_piece(r, k, h)
                if t and r == 0:
                    back_out[place, :, columns[h]] = loc
                stream = ref[at, :, columns[h]] + loc
                streams[place, :, columns[h]] = stream
                square = square + jnp.sum(jnp.square(stream.astype(f32)), axis=-1, keepdims=True)
            scales[place] = jnp.broadcast_to(lax.rsqrt(square / width + epsilon), (part, 128))
        rows = streams[...].reshape(-1, width)
        scale = scales[...].reshape(-1, 128)
        if batch[0][1] == 0:
            query = dot(rows, wq_ref[...])
            for h in range(heads):
                cols = slice(h * lookup, (h + 1) * lookup)
                q_refs[own][:, cols] = scaled_unit(query[:, cols], scale, sharp_ref[h] * (LOG2E / lookup))
        products.append((scale, dot(rows, wk_ref[...]), dot(rows, wv_ref[...])))
    for p, t in enumerate(strands):
        mine = []
        for batch, product in zip(batches, products):
            places = [i for i, item in enumerate(batch) if item[0] == t]
            if places:
                rows = slice(places[0] * part, (places[-1] + 1) * part)
                mine.append([a[rows] for a in product])
        attended = []
        for h in range(heads):
            cols = slice(h * lookup, (h + 1) * lookup)
            key_n = jnp.concatenate([scaled_unit(k[:, cols], scale) for scale, k, v in mine], axis=0)
            low, spare = window(h, value_size)
            value_h = []
            for c in range(padded // 128):
                block = slice(low + c * 128, low + (c + 1) * 128)
                column = jnp.concatenate([v[:, block] * scale for scale, k, v in mine], axis=0)
                if c == spare // 128:
                    lane = lax.broadcasted_iota(jnp.int32, column.shape, 1)
                    column = jnp.where(lane == spare % 128, 1.0, column)
                value_h.append(column.astype(bf16))
            value_h = jnp.concatenate(value_h, axis=1)
            scores = lax.dot_general(
                q_refs[t][:, cols], key_n, (((1,), (1,)), ((), ())), preferred_element_type=f32
            )
            weight = jnp.exp2(scores).astype(bf16)
            numer = dot(weight, value_h)
            if t != own:
                numer = numer + numer_in[t][h]
            if last:
                first = h * value_size - low
                attended.append(numer[:, first : first + value_size] / numer[:, spare : spare + 1])
            else:
                out_refs[p][h] = numer
        if last:
            attended = jnp.concatenate(attended, axis=1).astype(bf16)
            block = attended.shape[0] // 2
            for i in range(2):
                out_refs[i][p] = attended[i * block : (i + 1) * block]
                out_refs[2][i, p] = attended[i * block : (i + 1) * block]


VMEM = pl.BlockSpec(memory_space=pltpu.VMEM)
SMEM = pl.BlockSpec(memory_space=pltpu.SMEM)


def chunk_call(name, dims, batches, last, scal, x_parts, own_loc, loc_parts, flip, sharp, weights, q, numer):
    groups, seq, mp, heads, lookup, value_size, padded = dims
    _, part, width = own_loc.shape
    rows = part * mp
    batches = tuple(tuple(sorted(batch)) for batch in batches)
    strands = sorted({t for batch in batches for t, r, k in batch})
    where = {name: (n, i) for n, (_, names) in enumerate(x_parts) for name, i in names.items()}
    args = [a for a, _ in x_parts] + [own_loc] + list(loc_parts) + [flip, sharp] + list(weights) + list(q) + list(numer)
    specs = [SMEM if a is sharp else VMEM for a in args]
    if last:
        outs = [jax.ShapeDtypeStruct((2, rows // 2, heads * value_size), bf16)] * 2
        outs = outs + [jax.ShapeDtypeStruct((2, 2, rows // 2, heads * value_size), bf16)]
    else:
        outs = [jax.ShapeDtypeStruct((heads, rows, padded), f32)] * len(strands)
    if batches[0][0][1] == 0:
        outs = outs + [jax.ShapeDtypeStruct((rows, heads * lookup), bf16)]
        if batches[0][0][0]:
            outs = outs + [jax.ShapeDtypeStruct((mp, part, width), bf16)]
    scratch = []
    for batch in batches:
        scratch += [pltpu.VMEM((len(batch), part, width), bf16), pltpu.VMEM((len(batch), part, 128), f32)]
    return pl.pallas_call(
        functools.partial(chunk_kernel, dims, batches, where, last, (len(x_parts), len(loc_parts))),
        out_shape=outs,
        in_specs=[SMEM] + specs,
        out_specs=[VMEM] * len(outs),
        scratch_shapes=scratch,
        compiler_params=pltpu.CompilerParams(vmem_limit_bytes=40 * 2**20),
        cost_estimate=pl.CostEstimate(flops=COST, bytes_accessed=COST, transcendentals=0),
        name=name,
    )(scal, *args)


def mix_kernel(n, x_ref, loc_ref, back_ref, att0, att1, wo0, wo1, out_ref):
    rows = out_ref.shape[1]
    lo = n * rows
    mixed = dot(att0[...].reshape(2 * rows, -1), wo0[...]) + dot(att1[n].reshape(2 * rows, -1), wo1[...])
    x_f = x_ref[lo : lo + rows].astype(f32)
    for t, loc in enumerate((loc_ref, back_ref)):
        out_ref[t] = x_f + loc[lo : lo + rows].astype(f32) + mixed[t * rows : (t + 1) * rows]


def mix_call(n, x, loc, back, att, wo):
    rows, width = att[0].shape[1], x.shape[1]
    return pl.pallas_call(
        functools.partial(mix_kernel, n),
        out_shape=jax.ShapeDtypeStruct((2, rows, width), f32),
        in_specs=[VMEM] * 7,
        out_specs=VMEM,
        compiler_params=pltpu.CompilerParams(vmem_limit_bytes=32 * 2**20),
        cost_estimate=pl.CostEstimate(
            flops=8 * rows * width * wo[0].shape[0], bytes_accessed=8 * 2**20, transcendentals=0
        ),
        name="mix",
    )(x, loc, back, *att, *wo)


def mid_kernel(groups, scal, *refs):
    partial, gain_ref, w1_ref, w2_ref, *refs = refs
    even_out, odd_out, middle_out, summed, mixed = refs[-5:]
    refs = refs[:-5]
    att, wo = refs[: len(refs) // (1 + groups)], refs[len(refs) // (1 + groups) :]
    here_m, here_g = scal[0], scal[1]
    rows = partial.shape[1]
    half = partial.shape[2] // groups
    blocks = [a_ref[...].reshape(2 * rows, -1) for a_ref in att]
    for h in range(groups):
        columns = pl.ds(pl.multiple_of((h ^ here_g) * half, half), half)
        part = partial[:, :, columns].reshape(2 * rows, half)
        mixed[:, columns] = part + sum(dot(a, w[...]) for a, w in zip(blocks, wo[h * len(att) : (h + 1) * len(att)]))
    middle = mixed[...]
    normed = (unit(middle) * gain_ref[...]).astype(bf16)
    expanded = jax.nn.gelu(dot(normed, w1_ref[...]), approximate=True).astype(bf16)
    out = dot(expanded, w2_ref[...])
    out = out[:rows] + out[rows:]
    both = middle[:rows] + middle[rows:]
    mp, _, share = summed.shape
    for j in range(mp):
        summed[j] = out[:, j * share : (j + 1) * share].astype(bf16)
    for k in range(mp):
        (odd_out if k & 1 else even_out)[k >> 1] = summed[here_m ^ k]
    for j in range(mp):
        block = both[:, j * share : (j + 1) * share]

        @pl.when(here_m == j)
        def _():
            middle_out[...] = block


def mid_call(groups, mp, scal, partial, gain, w1, w2, att, wo):
    _, rows, width = partial.shape
    share = width // mp
    args = [partial, gain, w1, w2, *att, *wo]
    return pl.pallas_call(
        functools.partial(mid_kernel, groups),
        out_shape=[jax.ShapeDtypeStruct((mp // 2, rows, share), bf16)] * 2 + [jax.ShapeDtypeStruct((rows, share), f32)],
        in_specs=[SMEM] + [VMEM] * len(args),
        out_specs=[VMEM] * 3,
        scratch_shapes=[pltpu.VMEM((mp, rows, share), bf16), pltpu.VMEM((2 * rows, width), f32)],
        compiler_params=pltpu.CompilerParams(vmem_limit_bytes=40 * 2**20),
        cost_estimate=pl.CostEstimate(
            flops=4 * rows * width * (width // 2 + 2 * w1.shape[1]),
            bytes_accessed=14 * 2**20,
            transcendentals=2 * rows * w1.shape[1],
        ),
        name="middle",
    )(scal, *args)


def stack_kernel(*refs):
    for i, ref in enumerate(refs[:-1]):
        refs[-1][i] = ref[...]


def stack_call(arrays):
    shape = (len(arrays),) + arrays[0].shape
    return pl.pallas_call(
        stack_kernel,
        out_shape=jax.ShapeDtypeStruct(shape, arrays[0].dtype),
        in_specs=[VMEM] * len(arrays),
        out_specs=VMEM,
        compiler_params=pltpu.CompilerParams(vmem_limit_bytes=40 * 2**20),
        cost_estimate=pl.CostEstimate(flops=COST, bytes_accessed=COST, transcendentals=0),
        name="stack",
    )(*arrays)


def together(*arrays):
    return lax.optimization_barrier(arrays)


def shards(
    nucleotide_features,
    location_table,
    premix_rescaler,
    probe_lookup_matrices,
    payload_projector,
    logit_sharpness,
    mixing_projector,
    premlp_rescaler,
    widening_matrix,
    narrowing_matrix,
):
    rows, width = nucleotide_features.shape
    heads = logit_sharpness.shape[0]
    lookup = probe_lookup_matrices.shape[2] // heads
    value_size = payload_projector.shape[1] // heads
    padded = (value_size // 128 + 1) * 128
    groups, seq, mp = (lax.axis_size(name) for name in AXES)
    here_g, here_m = lax.axis_index("groups"), lax.axis_index("mp")
    nx = mp // 2
    part, half = rows // mp, width // groups
    dims = (groups, seq, mp, heads, lookup, value_size, padded)
    scal = jnp.stack([here_m, here_g]).astype(jnp.int32)
    x_own = nucleotide_features.reshape(mp, part, width)
    loc_own = location_table.reshape(mp, part, width)

    place = lax.broadcasted_iota(jnp.int32, (2 * part, 2 * part), 0) + lax.broadcasted_iota(jnp.int32, (2 * part, 2 * part), 1)
    flip = (place == 2 * part - 1).astype(bf16)
    gain = premix_rescaler.reshape(width, 1)
    wq, wk = [(gain * w.astype(f32)).astype(bf16) for w in (probe_lookup_matrices[0], probe_lookup_matrices[1])]
    wv = (gain * payload_projector.astype(f32)).astype(bf16)
    wv = jnp.pad(wv, ((0, 0), (0, -wv.shape[1] % 128)))

    have = {}

    def hold(array, names):
        have.update({name: (array, i) for i, name in enumerate(names)})

    def chunk(name, batches, last, loc_parts, q=(), numer=()):
        flip, wq, wk, wv = prepared
        weights = (wk, wv, wq) if batches[0][0][1] == 0 else (wk, wv)
        x_parts = {}
        for r, k in sorted({item[1:] for batch in batches for item in batch}):
            array, i = have[r, k]
            x_parts.setdefault(id(array), (array, {}))[1][r, k] = i
        return chunk_call(
            name, dims, batches, last, scal, list(x_parts.values()), loc_own, loc_parts,
            flip, logit_sharpness, weights, q, numer,
        )

    direct = range(3, seq, 2)
    loc_part = lax.dynamic_slice(location_table, (here_m * part, here_g * half), (part, half))
    loc_part, mix_first, x_first = together(loc_part, mixing_projector, x_own)
    mix_part = lax.dynamic_slice_in_dim(mix_first, here_g * half, half, 1)
    mix_x = [swap(mix_part, m=2 * kx) for kx in range(1, nx)]
    loc_z = [swap(loc_part, s=r) for r in range(1, seq)]
    x_mine = lax.dynamic_slice_in_dim(x_first, here_m, 1, 0)
    x_direct = [swap(x_mine, s=r) for r in direct]

    x_mine, flip, wq, wk, wv, loc_z = together(x_mine, flip, wq, wk, wv, loc_z)
    prepared = (flip, wq, wk, wv)
    loc_far = stack_call(loc_z)
    x_near = swap(x_mine, s=1)
    loc_xy = [loc_far] + [swap(loc_far, m=2 * kx) for kx in range(1, nx)]
    loc_y = [swap(loc_far, g=h) for h in range(1, groups)]
    x_direct, x_near, mix_x, loc_y = together(x_direct, x_near, mix_x, loc_y)
    loc_xy = loc_xy + [a for h in range(1, groups) for a in (loc_y[h - 1], *(swap(a, g=h) for a in loc_xy[1:]))]
    mix_far = [swap(a, g=h) if h else a for h in range(groups) for a in mix_x]
    x_relayed = [swap(a, s=1) for a in x_direct]
    x_across = [swap(a, m=2 * kx) for a in x_direct for kx in range(1, nx)]
    hold(x_own, [(0, k) for k in range(mp)])
    numer0, q0 = chunk("own_forward", [[(0, 0, k) for k in range(mp)]], False, [])

    x_near_across = [swap(x_near, m=2 * kx) for kx in range(1, nx)]
    numer0, loc_xy, *held = together(numer0, loc_xy, *x_relayed, x_near, *x_direct, *x_near_across)
    loc_even = stack_call(loc_xy)
    loc_odd = swap(loc_even, m=1)
    names = [[(r - 1, 0)] for r in direct] + [[(1, 0)]] + [[(r, 0)] for r in direct]
    names += [[(1, 2 * kx)] for kx in range(1, nx)]
    odd_names = lambda names: [(r, k + 1) for r, k in names]
    both = lambda names: [(t, r, k) for t in range(2) for r, k in names]
    hold(stack_call([a[0] for a in held]), [name for some in names for name in some])
    hold(swap(have[names[0][0]][0], m=1), odd_names([name for some in names for name in some]))
    early = [name for some in names for name in some]
    early = [early[i : i + 4] for i in range(0, len(early), 4)]
    x_late = [swap(a, m=2 * kx) for a in held[: len(direct)] for kx in range(1, nx)] + x_across
    late_names = [(r, 2 * kx) for r in [*(r - 1 for r in direct), *direct] for kx in range(1, nx)]
    loc_parts = [loc_even, loc_odd]
    batches = [[(1, 0, k) for k in range(mp)], both(early[0]), both(odd_names(early[0]))]
    n0, n1, q1, back = chunk("first", batches, False, loc_parts, [q0], [numer0])
    q, numer = [q0, q1], [n0, n1]
    for some in early[1:]:
        numer = chunk("more", [both(some), both(odd_names(some))], False, loc_parts, q, numer)
    numer, mix_far, *x_late = together(numer, mix_far, *x_late)
    x_late = stack_call([a[0] for a in x_late])
    hold(x_late, late_names)
    x_late_odd = swap(x_late, m=1)
    late = [late_names[i : i + 2] for i in range(0, len(late_names), 2)]
    for some in late:
        numer = chunk("second", [both(some)], False, loc_parts, q, numer)
    numer, x_late_odd = together(numer, x_late_odd)
    hold(x_late_odd, odd_names(late_names))
    for some in late[:-1]:
        numer = chunk("third", [both(odd_names(some))], False, loc_parts, q, numer)
    a0, a1, blocks = chunk("last", [both(odd_names(late[-1]))], True, loc_parts, q, numer)

    mixing, blocks = together(mixing_projector, blocks)
    wo_own = [mixing, swap(mixing, m=1)]
    w_mid = (premlp_rescaler.reshape(1, width), widening_matrix, narrowing_matrix)
    stream = (nucleotide_features, location_table, back.reshape(rows, width))

    def over_x(block):
        return [swap(block, m=2 * kx) for kx in range(1, nx)]

    def cores(blocks):
        return list(blocks) + [swap(a, m=1) for a in blocks]

    far0 = over_x(a0)
    blocks_odd = swap(blocks, m=1)
    part0 = mix_call(0, *stream, [a0, blocks_odd], wo_own)
    far1 = over_x(a1)
    part1 = mix_call(1, *stream, [a1, blocks_odd], wo_own)
    part0, part1, mix_far = together(part0, part1, mix_far)
    wo_far = []
    for h in range(groups):
        some = mix_far[h * (nx - 1) : (h + 1) * (nx - 1)]
        wo_far += [*some, *(swap(a, m=1) for a in some)]
    part0, part1, *far0 = together(part0, part1, *far0)
    even0, odd0, share0 = mid_call(groups, mp, scal, part0, *w_mid, cores(far0), wo_far)
    even0, odd0, share0, *far1 = together(even0, odd0, share0, *far1)
    paired0 = even0.astype(f32) + swap(odd0, m=1).astype(f32)
    part1, paired0 = together(part1, paired0)
    across0 = [swap(paired0[kx].astype(bf16), m=2 * kx) for kx in range(1, nx)]
    even1, odd1, share1 = mid_call(groups, mp, scal, part1, *w_mid, cores(far1), wo_far)
    even1, odd1, share1, *across0 = together(even1, odd1, share1, *across0)
    paired1 = even1.astype(f32) + swap(odd1, m=1).astype(f32)
    across1 = [swap(paired1[kx].astype(bf16), m=2 * kx) for kx in range(1, nx)]
    blocks = [
        0.5 * (share + paired[0] + sum(a.astype(f32) for a in arrived))
        for share, paired, arrived in ((share0, paired0, across0), (share1, paired1, across1))
    ]
    return jnp.concatenate(blocks, axis=0)


def solution(mesh):
    return jax.shard_map(
        shards,
        mesh=mesh,
        in_specs=(
            P(("groups", "seq"), None),
            P("seq", None),
            P(),
            P(None, None, "mp"),
            P(None, "mp"),
            P("mp"),
            P("mp", None),
            P(),
            P(None, "mp"),
            P("mp", None),
        ),
        out_specs=P(("groups", "seq"), "mp"),
        check_vma=False,
    )
```

```python
import functools

import jax
import jax.numpy as jnp
from jax import lax
from jax.experimental import pallas as pl
from jax.experimental.pallas import tpu as pltpu
from jax.sharding import PartitionSpec as P

epsilon = 1e-06
LOG2E = 1.4426950408889634
COST = 2**20
f32, bf16 = jnp.float32, jnp.bfloat16
AXES = ("groups", "seq", "mp")


def swap(block, g=0, s=0, m=0):
    groups, seq, mp = (lax.axis_size(name) for name in AXES)
    code = (g * seq + s) * mp + m
    return lax.ppermute(block, AXES, [(i, i ^ code) for i in range(groups * seq * mp)])


def unit(block):
    return block * lax.rsqrt(jnp.mean(block * block, axis=-1, keepdims=True) + epsilon)


def scaled_unit(block, scale, gain=None):
    mean = jnp.mean(block * block, axis=-1, keepdims=True)
    factor = scale * lax.rsqrt(scale * scale * mean + epsilon)
    return (block * (factor if gain is None else factor * gain)).astype(bf16)


def window(head, size):
    low = head * size // 128 * 128
    return low, (0 if head * size > low else size)


def dot(a, b):
    return jnp.dot(a, b, preferred_element_type=f32)


def chunk_kernel(dims, batches, where, last, counts, scal, *refs):
    groups, seq, mp, heads, lookup, value_size, padded = dims
    nx = mp // 2
    strands = sorted({t for batch in batches for t, r, k in batch})
    refs = list(refs)
    take = lambda n: [refs.pop(0) for _ in range(n)]
    x_refs = take(counts[0])
    (own_loc,) = take(1)
    loc_refs = take(counts[1])
    flip_ref, sharp_ref, wk_ref, wv_ref = take(4)
    own = batches[0][0][0] if batches[0][0][1] == 0 else None
    wq_ref = None if own is None else take(1)[0]
    q_refs = {t: take(1)[0] for t in strands if t != own}
    numer_in = {t: take(1)[0] for t in strands if t != own}
    out_refs = take(3 if last else len(strands))
    if own is not None:
        q_refs[own] = take(1)[0]
        back_out = take(1)[0] if own else None
    scratch = list(zip(refs[::2], refs[1::2]))
    here_m, here_g = scal[0], scal[1]
    part, width = own_loc.shape[1:]
    half = width // groups
    columns = [pl.ds(pl.multiple_of((h ^ here_g) * half, half), half) for h in range(groups)]

    def loc_piece(r, k, h):
        if r == 0:
            return own_loc[here_m ^ k, :, columns[h]]
        return loc_refs[k & 1][h * nx + (k >> 1), r - 1]

    products = []
    for batch, (streams, scales) in zip(batches, scratch):
        group = flip_ref.shape[0] // part
        backs = {}
        mirrored = [(r, k) for t, r, k in batch if t == 1]
        for n in range(0, len(mirrored), group):
            some = mirrored[n : n + group]
            for h in range(groups):
                pieces = [loc_piece(r ^ (seq - 1), k ^ (mp - 1), h) for r, k in reversed(some)]
                size = len(some) * part
                exchange = flip_ref[:size, group * part - size :]
                flipped = dot(exchange, jnp.concatenate(pieces, axis=0)).astype(bf16)
                for i, (r, k) in enumerate(some):
                    backs[r, k, h] = flipped[i * part : (i + 1) * part]
        for i, (t, r, k) in enumerate(batch):
            ref, at = x_refs[where[r, k][0]], where[r, k][1] if r else here_m ^ k
            place = i if r else here_m ^ k
            square = 0.0
            for h in range(groups):
                loc = backs[r, k, h] if t else loc_piece(r, k, h)
                if t and r == 0:
                    back_out[place, :, columns[h]] = loc
                stream = ref[at, :, columns[h]] + loc
                streams[place, :, columns[h]] = stream
                square = square + jnp.sum(jnp.square(stream.astype(f32)), axis=-1, keepdims=True)
            scales[place] = jnp.broadcast_to(lax.rsqrt(square / width + epsilon), (part, 128))
        rows = streams[...].reshape(-1, width)
        scale = scales[...].reshape(-1, 128)
        if batch[0][1] == 0:
            query = dot(rows, wq_ref[...])
            for h in range(heads):
                cols = slice(h * lookup, (h + 1) * lookup)
                q_refs[own][:, cols] = scaled_unit(query[:, cols], scale, sharp_ref[h] * (LOG2E / lookup))
        products.append((scale, dot(rows, wk_ref[...]), dot(rows, wv_ref[...])))
    for p, t in enumerate(strands):
        mine = []
        for batch, product in zip(batches, products):
            places = [i for i, item in enumerate(batch) if item[0] == t]
            if places:
                rows = slice(places[0] * part, (places[-1] + 1) * part)
                mine.append([a[rows] for a in product])
        attended = []
        for h in range(heads):
            cols = slice(h * lookup, (h + 1) * lookup)
            key_n = jnp.concatenate([scaled_unit(k[:, cols], scale) for scale, k, v in mine], axis=0)
            low, spare = window(h, value_size)
            value_h = []
            for c in range(padded // 128):
                block = slice(low + c * 128, low + (c + 1) * 128)
                column = jnp.concatenate([v[:, block] * scale for scale, k, v in mine], axis=0)
                if c == spare // 128:
                    lane = lax.broadcasted_iota(jnp.int32, column.shape, 1)
                    column = jnp.where(lane == spare % 128, 1.0, column)
                value_h.append(column.astype(bf16))
            value_h = jnp.concatenate(value_h, axis=1)
            scores = lax.dot_general(
                q_refs[t][:, cols], key_n, (((1,), (1,)), ((), ())), preferred_element_type=f32
            )
            weight = jnp.exp2(scores).astype(bf16)
            numer = dot(weight, value_h)
            if t != own:
                numer = numer + numer_in[t][h]
            if last:
                first = h * value_size - low
                attended.append(numer[:, first : first + value_size] / numer[:, spare : spare + 1])
            else:
                out_refs[p][h] = numer
        if last:
            attended = jnp.concatenate(attended, axis=1).astype(bf16)
            block = attended.shape[0] // 2
            for i in range(2):
                out_refs[i][p] = attended[i * block : (i + 1) * block]
                out_refs[2][i, p] = attended[i * block : (i + 1) * block]


VMEM = pl.BlockSpec(memory_space=pltpu.VMEM)
SMEM = pl.BlockSpec(memory_space=pltpu.SMEM)


def chunk_call(name, dims, batches, last, scal, x_parts, own_loc, loc_parts, flip, sharp, weights, q, numer):
    groups, seq, mp, heads, lookup, value_size, padded = dims
    _, part, width = own_loc.shape
    rows = part * mp
    batches = tuple(tuple(sorted(batch)) for batch in batches)
    strands = sorted({t for batch in batches for t, r, k in batch})
    where = {name: (n, i) for n, (_, names) in enumerate(x_parts) for name, i in names.items()}
    args = [a for a, _ in x_parts] + [own_loc] + list(loc_parts) + [flip, sharp] + list(weights) + list(q) + list(numer)
    specs = [SMEM if a is sharp else VMEM for a in args]
    if last:
        outs = [jax.ShapeDtypeStruct((2, rows // 2, heads * value_size), bf16)] * 2
        outs = outs + [jax.ShapeDtypeStruct((2, 2, rows // 2, heads * value_size), bf16)]
    else:
        outs = [jax.ShapeDtypeStruct((heads, rows, padded), f32)] * len(strands)
    if batches[0][0][1] == 0:
        outs = outs + [jax.ShapeDtypeStruct((rows, heads * lookup), bf16)]
        if batches[0][0][0]:
            outs = outs + [jax.ShapeDtypeStruct((mp, part, width), bf16)]
    scratch = []
    for batch in batches:
        scratch += [pltpu.VMEM((len(batch), part, width), bf16), pltpu.VMEM((len(batch), part, 128), f32)]
    return pl.pallas_call(
        functools.partial(chunk_kernel, dims, batches, where, last, (len(x_parts), len(loc_parts))),
        out_shape=outs,
        in_specs=[SMEM] + specs,
        out_specs=[VMEM] * len(outs),
        scratch_shapes=scratch,
        compiler_params=pltpu.CompilerParams(vmem_limit_bytes=24 * 2**20),
        cost_estimate=pl.CostEstimate(flops=COST, bytes_accessed=COST, transcendentals=0),
        name=name,
    )(scal, *args)


def mix_kernel(n, x_ref, loc_ref, back_ref, att0, att1, wo0, wo1, out_ref):
    rows = out_ref.shape[1]
    lo = n * rows
    mixed = dot(att0[...].reshape(2 * rows, -1), wo0[...]) + dot(att1[n].reshape(2 * rows, -1), wo1[...])
    x_f = x_ref[lo : lo + rows].astype(f32)
    for t, loc in enumerate((loc_ref, back_ref)):
        out_ref[t] = x_f + loc[lo : lo + rows].astype(f32) + mixed[t * rows : (t + 1) * rows]


def mix_call(n, x, loc, back, att, wo):
    rows, width = att[0].shape[1], x.shape[1]
    return pl.pallas_call(
        functools.partial(mix_kernel, n),
        out_shape=jax.ShapeDtypeStruct((2, rows, width), f32),
        in_specs=[VMEM] * 7,
        out_specs=VMEM,
        compiler_params=pltpu.CompilerParams(vmem_limit_bytes=24 * 2**20),
        cost_estimate=pl.CostEstimate(
            flops=8 * rows * width * wo[0].shape[0], bytes_accessed=8 * 2**20, transcendentals=0
        ),
        name="mix",
    )(x, loc, back, *att, *wo)


def mid_kernel(groups, scal, *refs):
    partial, gain_ref, w1_ref, w2_ref, *refs = refs
    even_out, odd_out, middle_out, summed, mixed = refs[-5:]
    refs = refs[:-5]
    att, wo = refs[: len(refs) // (1 + groups)], refs[len(refs) // (1 + groups) :]
    here_m, here_g = scal[0], scal[1]
    rows = partial.shape[1]
    half = partial.shape[2] // groups
    blocks = [a_ref[...].reshape(2 * rows, -1) for a_ref in att]
    for h in range(groups):
        columns = pl.ds(pl.multiple_of((h ^ here_g) * half, half), half)
        part = partial[:, :, columns].reshape(2 * rows, half)
        mixed[:, columns] = part + sum(dot(a, w[...]) for a, w in zip(blocks, wo[h * len(att) : (h + 1) * len(att)]))
    middle = mixed[...]
    normed = (unit(middle) * gain_ref[...]).astype(bf16)
    expanded = jax.nn.gelu(dot(normed, w1_ref[...]), approximate=True).astype(bf16)
    out = dot(expanded, w2_ref[...])
    out = out[:rows] + out[rows:]
    both = middle[:rows] + middle[rows:]
    mp, _, share = summed.shape
    for j in range(mp):
        summed[j] = out[:, j * share : (j + 1) * share].astype(bf16)
    for k in range(mp):
        (odd_out if k & 1 else even_out)[k >> 1] = summed[here_m ^ k]
    for j in range(mp):
        block = both[:, j * share : (j + 1) * share]

        @pl.when(here_m == j)
        def _():
            middle_out[...] = block


def mid_call(groups, mp, scal, partial, gain, w1, w2, att, wo):
    _, rows, width = partial.shape
    share = width // mp
    args = [partial, gain, w1, w2, *att, *wo]
    return pl.pallas_call(
        functools.partial(mid_kernel, groups),
        out_shape=[jax.ShapeDtypeStruct((mp // 2, rows, share), bf16)] * 2 + [jax.ShapeDtypeStruct((rows, share), f32)],
        in_specs=[SMEM] + [VMEM] * len(args),
        out_specs=[VMEM] * 3,
        scratch_shapes=[pltpu.VMEM((mp, rows, share), bf16), pltpu.VMEM((2 * rows, width), f32)],
        compiler_params=pltpu.CompilerParams(vmem_limit_bytes=24 * 2**20),
        cost_estimate=pl.CostEstimate(
            flops=4 * rows * width * (width // 2 + 2 * w1.shape[1]),
            bytes_accessed=14 * 2**20,
            transcendentals=2 * rows * w1.shape[1],
        ),
        name="middle",
    )(scal, *args)


def stack_kernel(*refs):
    for i, ref in enumerate(refs[:-1]):
        refs[-1][i] = ref[...]


def stack_call(arrays):
    shape = (len(arrays),) + arrays[0].shape
    return pl.pallas_call(
        stack_kernel,
        out_shape=jax.ShapeDtypeStruct(shape, arrays[0].dtype),
        in_specs=[VMEM] * len(arrays),
        out_specs=VMEM,
        compiler_params=pltpu.CompilerParams(vmem_limit_bytes=24 * 2**20),
        cost_estimate=pl.CostEstimate(flops=COST, bytes_accessed=COST, transcendentals=0),
        name="stack",
    )(*arrays)


def together(*arrays):
    return lax.optimization_barrier(arrays)


def shards(
    nucleotide_features,
    location_table,
    premix_rescaler,
    probe_lookup_matrices,
    payload_projector,
    logit_sharpness,
    mixing_projector,
    premlp_rescaler,
    widening_matrix,
    narrowing_matrix,
):
    rows, width = nucleotide_features.shape
    heads = logit_sharpness.shape[0]
    lookup = probe_lookup_matrices.shape[2] // heads
    value_size = payload_projector.shape[1] // heads
    padded = (value_size // 128 + 1) * 128
    groups, seq, mp = (lax.axis_size(name) for name in AXES)
    here_g, here_m = lax.axis_index("groups"), lax.axis_index("mp")
    nx = mp // 2
    part, half = rows // mp, width // groups
    dims = (groups, seq, mp, heads, lookup, value_size, padded)
    scal = jnp.stack([here_m, here_g]).astype(jnp.int32)
    x_own = nucleotide_features.reshape(mp, part, width)
    loc_own = location_table.reshape(mp, part, width)

    place = lax.broadcasted_iota(jnp.int32, (2 * part, 2 * part), 0) + lax.broadcasted_iota(jnp.int32, (2 * part, 2 * part), 1)
    flip = (place == 2 * part - 1).astype(bf16)
    gain = premix_rescaler.reshape(width, 1)
    wq, wk = [(gain * w.astype(f32)).astype(bf16) for w in (probe_lookup_matrices[0], probe_lookup_matrices[1])]
    wv = (gain * payload_projector.astype(f32)).astype(bf16)
    wv = jnp.pad(wv, ((0, 0), (0, -wv.shape[1] % 128)))

    have = {}

    def hold(array, names):
        have.update({name: (array, i) for i, name in enumerate(names)})

    def chunk(name, batches, last, loc_parts, q=(), numer=()):
        flip, wq, wk, wv = prepared
        weights = (wk, wv, wq) if batches[0][0][1] == 0 else (wk, wv)
        x_parts = {}
        for r, k in sorted({item[1:] for batch in batches for item in batch}):
            array, i = have[r, k]
            x_parts.setdefault(id(array), (array, {}))[1][r, k] = i
        return chunk_call(
            name, dims, batches, last, scal, list(x_parts.values()), loc_own, loc_parts,
            flip, logit_sharpness, weights, q, numer,
        )

    direct = range(3, seq, 2)
    loc_part = lax.dynamic_slice(location_table, (here_m * part, here_g * half), (part, half))
    loc_part, mix_first, x_first = together(loc_part, mixing_projector, x_own)
    mix_part = lax.dynamic_slice_in_dim(mix_first, here_g * half, half, 1)
    mix_x = [swap(mix_part, m=2 * kx) for kx in range(1, nx)]
    loc_z = [swap(loc_part, s=r) for r in range(1, seq)]
    x_mine = lax.dynamic_slice_in_dim(x_first, here_m, 1, 0)
    x_direct = [swap(x_mine, s=r) for r in direct]

    x_mine, flip, wq, wk, wv, loc_z = together(x_mine, flip, wq, wk, wv, loc_z)
    prepared = (flip, wq, wk, wv)
    loc_far = stack_call(loc_z)
    x_near = swap(x_mine, s=1)
    loc_xy = [loc_far] + [swap(loc_far, m=2 * kx) for kx in range(1, nx)]
    loc_y = [swap(loc_far, g=h) for h in range(1, groups)]
    x_direct, x_near, mix_x, loc_y = together(x_direct, x_near, mix_x, loc_y)
    loc_xy = loc_xy + [a for h in range(1, groups) for a in (loc_y[h - 1], *(swap(a, g=h) for a in loc_xy[1:]))]
    mix_far = [swap(a, g=h) if h else a for h in range(groups) for a in mix_x]
    x_relayed = [swap(a, s=1) for a in x_direct]
    x_across = [swap(a, m=2 * kx) for a in x_direct for kx in range(1, nx)]
    hold(x_own, [(0, k) for k in range(mp)])
    numer0, q0 = chunk("own_forward", [[(0, 0, k) for k in range(mp)]], False, [])

    x_near_across = [swap(x_near, m=2 * kx) for kx in range(1, nx)]
    numer0, loc_xy, *held = together(numer0, loc_xy, *x_relayed, x_near, *x_direct, *x_near_across)
    loc_even = stack_call(loc_xy)
    loc_odd = swap(loc_even, m=1)
    names = [[(r - 1, 0)] for r in direct] + [[(1, 0)]] + [[(r, 0)] for r in direct]
    names += [[(1, 2 * kx)] for kx in range(1, nx)]
    odd_names = lambda names: [(r, k + 1) for r, k in names]
    both = lambda names: [(t, r, k) for t in range(2) for r, k in names]
    hold(stack_call([a[0] for a in held]), [name for some in names for name in some])
    hold(swap(have[names[0][0]][0], m=1), odd_names([name for some in names for name in some]))
    early = [name for some in names for name in some]
    early = [early[i : i + 4] for i in range(0, len(early), 4)]
    x_late = [swap(a, m=2 * kx) for a in held[: len(direct)] for kx in range(1, nx)] + x_across
    late_names = [(r, 2 * kx) for r in [*(r - 1 for r in direct), *direct] for kx in range(1, nx)]
    loc_parts = [loc_even, loc_odd]
    numer1, q1, back = chunk("own_back", [[(1, 0, k) for k in range(mp)]], False, loc_parts)
    q, numer = [q0, q1], [numer0, numer1]
    for some in early:
        numer = chunk("first", [both(some), both(odd_names(some))], False, loc_parts, q, numer)
    numer, mix_far, *x_late = together(numer, mix_far, *x_late)
    x_late = stack_call([a[0] for a in x_late])
    hold(x_late, late_names)
    x_late_odd = swap(x_late, m=1)
    late = [late_names[i : i + 2] for i in range(0, len(late_names), 2)]
    for some in late:
        numer = chunk("second", [both(some)], False, loc_parts, q, numer)
    numer, x_late_odd = together(numer, x_late_odd)
    hold(x_late_odd, odd_names(late_names))
    for some in late[:-1]:
        numer = chunk("third", [both(odd_names(some))], False, loc_parts, q, numer)
    a0, a1, blocks = chunk("last", [both(odd_names(late[-1]))], True, loc_parts, q, numer)

    mixing, blocks = together(mixing_projector, blocks)
    wo_own = [mixing, swap(mixing, m=1)]
    w_mid = (premlp_rescaler.reshape(1, width), widening_matrix, narrowing_matrix)
    stream = (nucleotide_features, location_table, back.reshape(rows, width))

    def over_x(block):
        return [swap(block, m=2 * kx) for kx in range(1, nx)]

    def cores(blocks):
        return list(blocks) + [swap(a, m=1) for a in blocks]

    far0 = over_x(a0)
    blocks_odd = swap(blocks, m=1)
    part0 = mix_call(0, *stream, [a0, blocks_odd], wo_own)
    far1 = over_x(a1)
    part1 = mix_call(1, *stream, [a1, blocks_odd], wo_own)
    part0, part1, mix_far = together(part0, part1, mix_far)
    wo_far = []
    for h in range(groups):
        some = mix_far[h * (nx - 1) : (h + 1) * (nx - 1)]
        wo_far += [*(a if h else stack_call([a])[0] for a in some), *(swap(a, m=1) for a in some)]
    part0, part1, *far0 = together(part0, part1, *far0)
    even0, odd0, share0 = mid_call(groups, mp, scal, part0, *w_mid, cores(far0), wo_far)
    even0, odd0, share0, *far1 = together(even0, odd0, share0, *far1)
    paired0 = even0.astype(f32) + swap(odd0, m=1).astype(f32)
    part1, paired0 = together(part1, paired0)
    across0 = [swap(paired0[kx].astype(bf16), m=2 * kx) for kx in range(1, nx)]
    even1, odd1, share1 = mid_call(groups, mp, scal, part1, *w_mid, cores(far1), wo_far)
    even1, odd1, share1, *across0 = together(even1, odd1, share1, *across0)
    paired1 = even1.astype(f32) + swap(odd1, m=1).astype(f32)
    across1 = [swap(paired1[kx].astype(bf16), m=2 * kx) for kx in range(1, nx)]
    blocks = [
        0.5 * (share + paired[0] + sum(a.astype(f32) for a in arrived))
        for share, paired, arrived in ((share0, paired0, across0), (share1, paired1, across1))
    ]
    return jnp.concatenate(blocks, axis=0)


def solution(mesh):
    return jax.shard_map(
        shards,
        mesh=mesh,
        in_specs=(
            P(("groups", "seq"), None),
            P("seq", None),
            P(),
            P(None, None, "mp"),
            P(None, "mp"),
            P("mp"),
            P("mp", None),
            P(),
            P(None, "mp"),
            P("mp", None),
        ),
        out_specs=P(("groups", "seq"), "mp"),
        check_vma=False,
    )
```

```python
import functools

import jax
import jax.numpy as jnp
from jax import lax
from jax.experimental import pallas as pl
from jax.experimental.pallas import tpu as pltpu
from jax.sharding import PartitionSpec as P

epsilon = 1e-06
LOG2E = 1.4426950408889634
COST = 2**20
f32, bf16 = jnp.float32, jnp.bfloat16
AXES = ("groups", "seq", "mp")


def swap(block, g=0, s=0, m=0):
    groups, seq, mp = (lax.axis_size(name) for name in AXES)
    code = (g * seq + s) * mp + m
    return lax.ppermute(block, AXES, [(i, i ^ code) for i in range(groups * seq * mp)])


def unit(block):
    return block * lax.rsqrt(jnp.mean(block * block, axis=-1, keepdims=True) + epsilon)


def scaled_unit(block, scale, gain=None):
    mean = jnp.mean(block * block, axis=-1, keepdims=True)
    factor = scale * lax.rsqrt(scale * scale * mean + epsilon)
    return (block * (factor if gain is None else factor * gain)).astype(bf16)


def window(head, size):
    low = head * size // 128 * 128
    return low, (0 if head * size > low else size)


def dot(a, b):
    return jnp.dot(a, b, preferred_element_type=f32)


def chunk_kernel(dims, batches, where, last, counts, scal, *refs):
    groups, seq, mp, heads, lookup, value_size, padded = dims
    nx = mp // 2
    strands = sorted({t for batch in batches for t, r, k in batch})
    refs = list(refs)
    take = lambda n: [refs.pop(0) for _ in range(n)]
    x_refs = take(counts[0])
    (own_loc,) = take(1)
    loc_refs = take(counts[1])
    flip_ref, sharp_ref, wk_ref, wv_ref = take(4)
    own = batches[0][0][0] if batches[0][0][1] == 0 else None
    wq_ref = None if own is None else take(1)[0]
    q_refs = {t: take(1)[0] for t in strands if t != own}
    numer_in = {t: take(1)[0] for t in strands if t != own}
    out_refs = take(3 if last else len(strands))
    if own is not None:
        q_refs[own] = take(1)[0]
        back_out = take(1)[0] if own else None
    scratch = list(zip(refs[::2], refs[1::2]))
    here_m, here_g = scal[0], scal[1]
    part, width = own_loc.shape[1:]
    half = width // groups
    columns = [pl.ds(pl.multiple_of((h ^ here_g) * half, half), half) for h in range(groups)]

    def loc_piece(r, k, h):
        if r == 0:
            return own_loc[here_m ^ k, :, columns[h]]
        return loc_refs[k & 1][h * nx + (k >> 1), r - 1]

    products = []
    for batch, (streams, scales) in zip(batches, scratch):
        group = flip_ref.shape[0] // part
        backs = {}
        mirrored = [(r, k) for t, r, k in batch if t == 1]
        for n in range(0, len(mirrored), group):
            some = mirrored[n : n + group]
            for h in range(groups):
                pieces = [loc_piece(r ^ (seq - 1), k ^ (mp - 1), h) for r, k in reversed(some)]
                size = len(some) * part
                exchange = flip_ref[:size, group * part - size :]
                flipped = dot(exchange, jnp.concatenate(pieces, axis=0)).astype(bf16)
                for i, (r, k) in enumerate(some):
                    backs[r, k, h] = flipped[i * part : (i + 1) * part]
        for i, (t, r, k) in enumerate(batch):
            ref, at = x_refs[where[r, k][0]], where[r, k][1] if r else here_m ^ k
            place = i if r else here_m ^ k
            square = 0.0
            for h in range(groups):
                loc = backs[r, k, h] if t else loc_piece(r, k, h)
                if t and r == 0:
                    back_out[place, :, columns[h]] = loc
                stream = ref[at, :, columns[h]] + loc
                streams[place, :, columns[h]] = stream
                square = square + jnp.sum(jnp.square(stream.astype(f32)), axis=-1, keepdims=True)
            scales[place] = jnp.broadcast_to(lax.rsqrt(square / width + epsilon), (part, 128))
        rows = streams[...].reshape(-1, width)
        scale = scales[...].reshape(-1, 128)
        if batch[0][1] == 0:
            query = dot(rows, wq_ref[...])
            for h in range(heads):
                cols = slice(h * lookup, (h + 1) * lookup)
                q_refs[own][:, cols] = scaled_unit(query[:, cols], scale, sharp_ref[h] * (LOG2E / lookup))
        products.append((scale, dot(rows, wk_ref[...]), dot(rows, wv_ref[...])))
    for p, t in enumerate(strands):
        mine = []
        for batch, product in zip(batches, products):
            places = [i for i, item in enumerate(batch) if item[0] == t]
            if places:
                rows = slice(places[0] * part, (places[-1] + 1) * part)
                mine.append([a[rows] for a in product])
        attended = []
        for h in range(heads):
            cols = slice(h * lookup, (h + 1) * lookup)
            key_n = jnp.concatenate([scaled_unit(k[:, cols], scale) for scale, k, v in mine], axis=0)
            low, spare = window(h, value_size)
            value_h = []
            for c in range(padded // 128):
                block = slice(low + c * 128, low + (c + 1) * 128)
                column = jnp.concatenate([v[:, block] * scale for scale, k, v in mine], axis=0)
                if c == spare // 128:
                    lane = lax.broadcasted_iota(jnp.int32, column.shape, 1)
                    column = jnp.where(lane == spare % 128, 1.0, column)
                value_h.append(column.astype(bf16))
            value_h = jnp.concatenate(value_h, axis=1)
            scores = lax.dot_general(
                q_refs[t][:, cols], key_n, (((1,), (1,)), ((), ())), preferred_element_type=f32
            )
            weight = jnp.exp2(scores).astype(bf16)
            numer = dot(weight, value_h)
            if t != own:
                numer = numer + numer_in[t][h]
            if last:
                first = h * value_size - low
                attended.append(numer[:, first : first + value_size] / numer[:, spare : spare + 1])
            else:
                out_refs[p][h] = numer
        if last:
            attended = jnp.concatenate(attended, axis=1).astype(bf16)
            block = attended.shape[0] // 2
            for i in range(2):
                out_refs[i][p] = attended[i * block : (i + 1) * block]
                out_refs[2][i, p] = attended[i * block : (i + 1) * block]


VMEM = pl.BlockSpec(memory_space=pltpu.VMEM)
SMEM = pl.BlockSpec(memory_space=pltpu.SMEM)


def chunk_call(name, dims, batches, last, scal, x_parts, own_loc, loc_parts, flip, sharp, weights, q, numer):
    groups, seq, mp, heads, lookup, value_size, padded = dims
    _, part, width = own_loc.shape
    rows = part * mp
    batches = tuple(tuple(sorted(batch)) for batch in batches)
    strands = sorted({t for batch in batches for t, r, k in batch})
    where = {name: (n, i) for n, (_, names) in enumerate(x_parts) for name, i in names.items()}
    args = [a for a, _ in x_parts] + [own_loc] + list(loc_parts) + [flip, sharp] + list(weights) + list(q) + list(numer)
    specs = [SMEM if a is sharp else VMEM for a in args]
    if last:
        outs = [jax.ShapeDtypeStruct((2, rows // 2, heads * value_size), bf16)] * 2
        outs = outs + [jax.ShapeDtypeStruct((2, 2, rows // 2, heads * value_size), bf16)]
    else:
        outs = [jax.ShapeDtypeStruct((heads, rows, padded), f32)] * len(strands)
    if batches[0][0][1] == 0:
        outs = outs + [jax.ShapeDtypeStruct((rows, heads * lookup), bf16)]
        if batches[0][0][0]:
            outs = outs + [jax.ShapeDtypeStruct((mp, part, width), bf16)]
    scratch = []
    for batch in batches:
        scratch += [pltpu.VMEM((len(batch), part, width), bf16), pltpu.VMEM((len(batch), part, 128), f32)]
    return pl.pallas_call(
        functools.partial(chunk_kernel, dims, batches, where, last, (len(x_parts), len(loc_parts))),
        out_shape=outs,
        in_specs=[SMEM] + specs,
        out_specs=[VMEM] * len(outs),
        scratch_shapes=scratch,
        compiler_params=pltpu.CompilerParams(vmem_limit_bytes=24 * 2**20),
        cost_estimate=pl.CostEstimate(flops=COST, bytes_accessed=COST, transcendentals=0),
        name=name,
    )(scal, *args)


def mix_kernel(n, x_ref, loc_ref, back_ref, att0, att1, wo0, wo1, *refs):
    count = len(refs) // 2
    out_ref = refs[count]
    for i in range(count):
        refs[count + 1 + i][...] = refs[i][...]
    rows = out_ref.shape[1]
    lo = n * rows
    mixed = dot(att0[...].reshape(2 * rows, -1), wo0[...]) + dot(att1[n].reshape(2 * rows, -1), wo1[...])
    x_f = x_ref[lo : lo + rows].astype(f32)
    for t, loc in enumerate((loc_ref, back_ref)):
        out_ref[t] = x_f + loc[lo : lo + rows].astype(f32) + mixed[t * rows : (t + 1) * rows]


def mix_call(n, x, loc, back, att, wo, copied=()):
    rows, width = att[0].shape[1], x.shape[1]
    return pl.pallas_call(
        functools.partial(mix_kernel, n),
        out_shape=[jax.ShapeDtypeStruct((2, rows, width), f32)] + [jax.ShapeDtypeStruct(a.shape, a.dtype) for a in copied],
        in_specs=[VMEM] * (7 + len(copied)),
        out_specs=[VMEM] * (1 + len(copied)),
        compiler_params=pltpu.CompilerParams(vmem_limit_bytes=24 * 2**20),
        cost_estimate=pl.CostEstimate(
            flops=8 * rows * width * wo[0].shape[0], bytes_accessed=8 * 2**20, transcendentals=0
        ),
        name="mix",
    )(x, loc, back, *att, *wo, *copied)


def mid_kernel(groups, scal, *refs):
    partial, gain_ref, w1_ref, w2_ref, *refs = refs
    even_out, odd_out, middle_out, summed, mixed = refs[-5:]
    refs = refs[:-5]
    att, wo = refs[: len(refs) // (1 + groups)], refs[len(refs) // (1 + groups) :]
    here_m, here_g = scal[0], scal[1]
    rows = partial.shape[1]
    half = partial.shape[2] // groups
    blocks = [a_ref[...].reshape(2 * rows, -1) for a_ref in att]
    for h in range(groups):
        columns = pl.ds(pl.multiple_of((h ^ here_g) * half, half), half)
        part = partial[:, :, columns].reshape(2 * rows, half)
        mixed[:, columns] = part + sum(dot(a, w[...]) for a, w in zip(blocks, wo[h * len(att) : (h + 1) * len(att)]))
    middle = mixed[...]
    normed = (unit(middle) * gain_ref[...]).astype(bf16)
    expanded = jax.nn.gelu(dot(normed, w1_ref[...]), approximate=True).astype(bf16)
    out = dot(expanded, w2_ref[...])
    out = out[:rows] + out[rows:]
    both = middle[:rows] + middle[rows:]
    mp, _, share = summed.shape
    for j in range(mp):
        summed[j] = out[:, j * share : (j + 1) * share].astype(bf16)
    for k in range(mp):
        (odd_out if k & 1 else even_out)[k >> 1] = summed[here_m ^ k]
    for j in range(mp):
        block = both[:, j * share : (j + 1) * share]

        @pl.when(here_m == j)
        def _():
            middle_out[...] = block


def mid_call(groups, mp, scal, partial, gain, w1, w2, att, wo):
    _, rows, width = partial.shape
    share = width // mp
    args = [partial, gain, w1, w2, *att, *wo]
    return pl.pallas_call(
        functools.partial(mid_kernel, groups),
        out_shape=[jax.ShapeDtypeStruct((mp // 2, rows, share), bf16)] * 2 + [jax.ShapeDtypeStruct((rows, share), f32)],
        in_specs=[SMEM] + [VMEM] * len(args),
        out_specs=[VMEM] * 3,
        scratch_shapes=[pltpu.VMEM((mp, rows, share), bf16), pltpu.VMEM((2 * rows, width), f32)],
        compiler_params=pltpu.CompilerParams(vmem_limit_bytes=24 * 2**20),
        cost_estimate=pl.CostEstimate(
            flops=4 * rows * width * (width // 2 + 2 * w1.shape[1]),
            bytes_accessed=14 * 2**20,
            transcendentals=2 * rows * w1.shape[1],
        ),
        name="middle",
    )(scal, *args)


def stack_kernel(*refs):
    for i, ref in enumerate(refs[:-1]):
        refs[-1][i] = ref[...]


def stack_call(arrays):
    shape = (len(arrays),) + arrays[0].shape
    return pl.pallas_call(
        stack_kernel,
        out_shape=jax.ShapeDtypeStruct(shape, arrays[0].dtype),
        in_specs=[VMEM] * len(arrays),
        out_specs=VMEM,
        compiler_params=pltpu.CompilerParams(vmem_limit_bytes=24 * 2**20),
        cost_estimate=pl.CostEstimate(flops=COST, bytes_accessed=COST, transcendentals=0),
        name="stack",
    )(*arrays)


def together(*arrays):
    return lax.optimization_barrier(arrays)


def shards(
    nucleotide_features,
    location_table,
    premix_rescaler,
    probe_lookup_matrices,
    payload_projector,
    logit_sharpness,
    mixing_projector,
    premlp_rescaler,
    widening_matrix,
    narrowing_matrix,
):
    rows, width = nucleotide_features.shape
    heads = logit_sharpness.shape[0]
    lookup = probe_lookup_matrices.shape[2] // heads
    value_size = payload_projector.shape[1] // heads
    padded = (value_size // 128 + 1) * 128
    groups, seq, mp = (lax.axis_size(name) for name in AXES)
    here_g, here_m = lax.axis_index("groups"), lax.axis_index("mp")
    nx = mp // 2
    part, half = rows // mp, width // groups
    dims = (groups, seq, mp, heads, lookup, value_size, padded)
    scal = jnp.stack([here_m, here_g]).astype(jnp.int32)
    x_own = nucleotide_features.reshape(mp, part, width)
    loc_own = location_table.reshape(mp, part, width)

    place = lax.broadcasted_iota(jnp.int32, (2 * part, 2 * part), 0) + lax.broadcasted_iota(jnp.int32, (2 * part, 2 * part), 1)
    flip = (place == 2 * part - 1).astype(bf16)
    gain = premix_rescaler.reshape(width, 1)
    wq, wk = [(gain * w.astype(f32)).astype(bf16) for w in (probe_lookup_matrices[0], probe_lookup_matrices[1])]
    wv = (gain * payload_projector.astype(f32)).astype(bf16)
    wv = jnp.pad(wv, ((0, 0), (0, -wv.shape[1] % 128)))

    have = {}

    def hold(array, names):
        have.update({name: (array, i) for i, name in enumerate(names)})

    def chunk(name, batches, last, loc_parts, q=(), numer=()):
        flip, wq, wk, wv = prepared
        weights = (wk, wv, wq) if batches[0][0][1] == 0 else (wk, wv)
        x_parts = {}
        for r, k in sorted({item[1:] for batch in batches for item in batch}):
            array, i = have[r, k]
            x_parts.setdefault(id(array), (array, {}))[1][r, k] = i
        return chunk_call(
            name, dims, batches, last, scal, list(x_parts.values()), loc_own, loc_parts,
            flip, logit_sharpness, weights, q, numer,
        )

    direct = range(3, seq, 2)
    loc_part = lax.dynamic_slice(location_table, (here_m * part, here_g * half), (part, half))
    loc_part, mix_first, x_first = together(loc_part, mixing_projector, x_own)
    mix_part = lax.dynamic_slice_in_dim(mix_first, here_g * half, half, 1)
    mix_x = [swap(mix_part, m=2 * kx) for kx in range(1, nx)]
    loc_z = [swap(loc_part, s=r) for r in range(1, seq)]
    x_mine = lax.dynamic_slice_in_dim(x_first, here_m, 1, 0)
    x_direct = [swap(x_mine, s=r) for r in direct]

    x_mine, flip, wq, wk, wv, loc_z = together(x_mine, flip, wq, wk, wv, loc_z)
    prepared = (flip, wq, wk, wv)
    loc_far = stack_call(loc_z)
    x_near = swap(x_mine, s=1)
    loc_xy = [loc_far] + [swap(loc_far, m=2 * kx) for kx in range(1, nx)]
    loc_y = [swap(loc_far, g=h) for h in range(1, groups)]
    x_direct, x_near, mix_x, loc_y = together(x_direct, x_near, mix_x, loc_y)
    loc_xy = loc_xy + [a for h in range(1, groups) for a in (loc_y[h - 1], *(swap(a, g=h) for a in loc_xy[1:]))]
    mix_far = [swap(a, g=h) if h else a for h in range(groups) for a in mix_x]
    x_relayed = [swap(a, s=1) for a in x_direct]
    x_across = [swap(a, m=2 * kx) for a in x_direct for kx in range(1, nx)]
    hold(x_own, [(0, k) for k in range(mp)])
    numer0, q0 = chunk("own_forward", [[(0, 0, k) for k in range(mp)]], False, [])

    x_near_across = [swap(x_near, m=2 * kx) for kx in range(1, nx)]
    numer0, loc_xy, *held = together(numer0, loc_xy, *x_relayed, x_near, *x_direct, *x_near_across)
    loc_even = stack_call(loc_xy)
    loc_odd = swap(loc_even, m=1)
    names = [[(r - 1, 0)] for r in direct] + [[(1, 0)]] + [[(r, 0)] for r in direct]
    names += [[(1, 2 * kx)] for kx in range(1, nx)]
    odd_names = lambda names: [(r, k + 1) for r, k in names]
    both = lambda names: [(t, r, k) for t in range(2) for r, k in names]
    hold(stack_call([a[0] for a in held]), [name for some in names for name in some])
    hold(swap(have[names[0][0]][0], m=1), odd_names([name for some in names for name in some]))
    early = [name for some in names for name in some]
    early = [early[i : i + 4] for i in range(0, len(early), 4)]
    x_late = [swap(a, m=2 * kx) for a in held[: len(direct)] for kx in range(1, nx)] + x_across
    late_names = [(r, 2 * kx) for r in [*(r - 1 for r in direct), *direct] for kx in range(1, nx)]
    loc_parts = [loc_even, loc_odd]
    numer1, q1, back = chunk("own_back", [[(1, 0, k) for k in range(mp)]], False, loc_parts)
    q, numer = [q0, q1], [numer0, numer1]
    for some in early:
        numer = chunk("first", [both(some), both(odd_names(some))], False, loc_parts, q, numer)
    numer, mix_far, *x_late = together(numer, mix_far, *x_late)
    x_late = stack_call([a[0] for a in x_late])
    hold(x_late, late_names)
    x_late_odd = swap(x_late, m=1)
    late = [late_names[i : i + 2] for i in range(0, len(late_names), 2)]
    for some in late:
        numer = chunk("second", [both(some)], False, loc_parts, q, numer)
    numer, x_late_odd = together(numer, x_late_odd)
    hold(x_late_odd, odd_names(late_names))
    for some in late[:-1]:
        numer = chunk("third", [both(odd_names(some))], False, loc_parts, q, numer)
    a0, a1, blocks = chunk("last", [both(odd_names(late[-1]))], True, loc_parts, q, numer)

    mixing, blocks = together(mixing_projector, blocks)
    wo_own = [mixing, swap(mixing, m=1)]
    w_mid = (premlp_rescaler.reshape(1, width), widening_matrix, narrowing_matrix)
    stream = (nucleotide_features, location_table, back.reshape(rows, width))

    def over_x(block):
        return [swap(block, m=2 * kx) for kx in range(1, nx)]

    def cores(blocks):
        return list(blocks) + [swap(a, m=1) for a in blocks]

    far0 = over_x(a0)
    blocks_odd = swap(blocks, m=1)
    (part0,) = mix_call(0, *stream, [a0, blocks_odd], wo_own)
    far1 = over_x(a1)
    part1, *copies = mix_call(1, *stream, [a1, blocks_odd], wo_own, mix_far[: nx - 1])
    part0, part1, mix_far = together(part0, part1, mix_far)
    wo_far = []
    for h in range(groups):
        some = mix_far[h * (nx - 1) : (h + 1) * (nx - 1)]
        wo_far += [*(some if h else copies), *(swap(a, m=1) for a in some)]
    part0, part1, *far0 = together(part0, part1, *far0)
    even0, odd0, share0 = mid_call(groups, mp, scal, part0, *w_mid, cores(far0), wo_far)
    even0, odd0, share0, *far1 = together(even0, odd0, share0, *far1)
    paired0 = even0.astype(f32) + swap(odd0, m=1).astype(f32)
    part1, paired0 = together(part1, paired0)
    across0 = [swap(paired0[kx].astype(bf16), m=2 * kx) for kx in range(1, nx)]
    even1, odd1, share1 = mid_call(groups, mp, scal, part1, *w_mid, cores(far1), wo_far)
    even1, odd1, share1, *across0 = together(even1, odd1, share1, *across0)
    paired1 = even1.astype(f32) + swap(odd1, m=1).astype(f32)
    across1 = [swap(paired1[kx].astype(bf16), m=2 * kx) for kx in range(1, nx)]
    blocks = [
        0.5 * (share + paired[0] + sum(a.astype(f32) for a in arrived))
        for share, paired, arrived in ((share0, paired0, across0), (share1, paired1, across1))
    ]
    return jnp.concatenate(blocks, axis=0)


def solution(mesh):
    return jax.shard_map(
        shards,
        mesh=mesh,
        in_specs=(
            P(("groups", "seq"), None),
            P("seq", None),
            P(),
            P(None, None, "mp"),
            P(None, "mp"),
            P("mp"),
            P("mp", None),
            P(),
            P(None, "mp"),
            P("mp", None),
        ),
        out_specs=P(("groups", "seq"), "mp"),
        check_vma=False,
    )
```

```python
import functools

import jax
import jax.numpy as jnp
from jax import lax
from jax.experimental import pallas as pl
from jax.experimental.pallas import tpu as pltpu
from jax.sharding import PartitionSpec as P

epsilon = 1e-06
LOG2E = 1.4426950408889634
COST = 2**20
f32, bf16 = jnp.float32, jnp.bfloat16
AXES = ("groups", "seq", "mp")


def swap(block, g=0, s=0, m=0):
    groups, seq, mp = (lax.axis_size(name) for name in AXES)
    code = (g * seq + s) * mp + m
    return lax.ppermute(block, AXES, [(i, i ^ code) for i in range(groups * seq * mp)])


def unit(block):
    return block * lax.rsqrt(jnp.mean(block * block, axis=-1, keepdims=True) + epsilon)


def scaled_unit(block, scale, gain=None):
    mean = jnp.mean(block * block, axis=-1, keepdims=True)
    factor = scale * lax.rsqrt(scale * scale * mean + epsilon)
    return (block * (factor if gain is None else factor * gain)).astype(bf16)


def window(head, size):
    low = head * size // 128 * 128
    return low, (0 if head * size > low else size)


def dot(a, b):
    return jnp.dot(a, b, preferred_element_type=f32)


def chunk_kernel(dims, batches, where, last, counts, scal, *refs):
    groups, seq, mp, heads, lookup, value_size, padded = dims
    nx = mp // 2
    strands = sorted({t for batch in batches for t, r, k in batch})
    refs = list(refs)
    take = lambda n: [refs.pop(0) for _ in range(n)]
    x_refs = take(counts[0])
    (own_loc,) = take(1)
    loc_refs = take(counts[1])
    flip_ref, sharp_ref, wk_ref, wv_ref = take(4)
    own = batches[0][0][0] if batches[0][0][1] == 0 else None
    wq_ref = None if own is None else take(1)[0]
    q_refs = {t: take(1)[0] for t in strands if t != own}
    numer_in = {t: take(1)[0] for t in strands if t != own}
    out_refs = take(3 if last else len(strands))
    if own is not None:
        q_refs[own] = take(1)[0]
        back_out = take(1)[0] if own else None
    scratch = list(zip(refs[::2], refs[1::2]))
    here_m, here_g = scal[0], scal[1]
    part, width = own_loc.shape[1:]
    half = width // groups
    columns = [pl.ds(pl.multiple_of((h ^ here_g) * half, half), half) for h in range(groups)]

    def loc_piece(r, k, h):
        if r == 0:
            return own_loc[here_m ^ k, :, columns[h]]
        return loc_refs[k & 1][h * nx + (k >> 1), r - 1]

    products = []
    for batch, (streams, scales) in zip(batches, scratch):
        group = flip_ref.shape[0] // part
        backs = {}
        mirrored = [(r, k) for t, r, k in batch if t == 1]
        for n in range(0, len(mirrored), group):
            some = mirrored[n : n + group]
            for h in range(groups):
                pieces = [loc_piece(r ^ (seq - 1), k ^ (mp - 1), h) for r, k in reversed(some)]
                size = len(some) * part
                exchange = flip_ref[:size, group * part - size :]
                flipped = dot(exchange, jnp.concatenate(pieces, axis=0)).astype(bf16)
                for i, (r, k) in enumerate(some):
                    backs[r, k, h] = flipped[i * part : (i + 1) * part]
        for i, (t, r, k) in enumerate(batch):
            ref, at = x_refs[where[r, k][0]], where[r, k][1] if r else here_m ^ k
            place = i if r else here_m ^ k
            square = 0.0
            for h in range(groups):
                loc = backs[r, k, h] if t else loc_piece(r, k, h)
                if t and r == 0:
                    back_out[place, :, columns[h]] = loc
                stream = ref[at, :, columns[h]] + loc
                streams[place, :, columns[h]] = stream
                square = square + jnp.sum(jnp.square(stream.astype(f32)), axis=-1, keepdims=True)
            scales[place] = jnp.broadcast_to(lax.rsqrt(square / width + epsilon), (part, 128))
        rows = streams[...].reshape(-1, width)
        scale = scales[...].reshape(-1, 128)
        if batch[0][1] == 0:
            query = dot(rows, wq_ref[...])
            for h in range(heads):
                cols = slice(h * lookup, (h + 1) * lookup)
                q_refs[own][:, cols] = scaled_unit(query[:, cols], scale, sharp_ref[h] * (LOG2E / lookup))
        products.append((scale, dot(rows, wk_ref[...]), dot(rows, wv_ref[...])))
    for p, t in enumerate(strands):
        mine = []
        for batch, product in zip(batches, products):
            places = [i for i, item in enumerate(batch) if item[0] == t]
            if places:
                rows = slice(places[0] * part, (places[-1] + 1) * part)
                mine.append([a[rows] for a in product])
        attended = []
        for h in range(heads):
            cols = slice(h * lookup, (h + 1) * lookup)
            key_n = jnp.concatenate([scaled_unit(k[:, cols], scale) for scale, k, v in mine], axis=0)
            low, spare = window(h, value_size)
            value_h = []
            for c in range(padded // 128):
                block = slice(low + c * 128, low + (c + 1) * 128)
                column = jnp.concatenate([v[:, block] * scale for scale, k, v in mine], axis=0)
                if c == spare // 128:
                    lane = lax.broadcasted_iota(jnp.int32, column.shape, 1)
                    column = jnp.where(lane == spare % 128, 1.0, column)
                value_h.append(column.astype(bf16))
            value_h = jnp.concatenate(value_h, axis=1)
            scores = lax.dot_general(
                q_refs[t][:, cols], key_n, (((1,), (1,)), ((), ())), preferred_element_type=f32
            )
            weight = jnp.exp2(scores).astype(bf16)
            numer = dot(weight, value_h)
            if t != own:
                numer = numer + numer_in[t][h]
            if last:
                first = h * value_size - low
                attended.append(numer[:, first : first + value_size] / numer[:, spare : spare + 1])
            else:
                out_refs[p][h] = numer
        if last:
            attended = jnp.concatenate(attended, axis=1).astype(bf16)
            block = attended.shape[0] // 2
            for i in range(2):
                out_refs[i][p] = attended[i * block : (i + 1) * block]
                out_refs[2][i, p] = attended[i * block : (i + 1) * block]


VMEM = pl.BlockSpec(memory_space=pltpu.VMEM)
SMEM = pl.BlockSpec(memory_space=pltpu.SMEM)


def chunk_call(name, dims, batches, last, scal, x_parts, own_loc, loc_parts, flip, sharp, weights, q, numer):
    groups, seq, mp, heads, lookup, value_size, padded = dims
    _, part, width = own_loc.shape
    rows = part * mp
    batches = tuple(tuple(sorted(batch)) for batch in batches)
    strands = sorted({t for batch in batches for t, r, k in batch})
    where = {name: (n, i) for n, (_, names) in enumerate(x_parts) for name, i in names.items()}
    args = [a for a, _ in x_parts] + [own_loc] + list(loc_parts) + [flip, sharp] + list(weights) + list(q) + list(numer)
    specs = [SMEM if a is sharp else VMEM for a in args]
    if last:
        outs = [jax.ShapeDtypeStruct((2, rows // 2, heads * value_size), bf16)] * 2
        outs = outs + [jax.ShapeDtypeStruct((2, 2, rows // 2, heads * value_size), bf16)]
    else:
        outs = [jax.ShapeDtypeStruct((heads, rows, padded), f32)] * len(strands)
    if batches[0][0][1] == 0:
        outs = outs + [jax.ShapeDtypeStruct((rows, heads * lookup), bf16)]
        if batches[0][0][0]:
            outs = outs + [jax.ShapeDtypeStruct((mp, part, width), bf16)]
    scratch = []
    for batch in batches:
        scratch += [pltpu.VMEM((len(batch), part, width), bf16), pltpu.VMEM((len(batch), part, 128), f32)]
    return pl.pallas_call(
        functools.partial(chunk_kernel, dims, batches, where, last, (len(x_parts), len(loc_parts))),
        out_shape=outs,
        in_specs=[SMEM] + specs,
        out_specs=[VMEM] * len(outs),
        scratch_shapes=scratch,
        compiler_params=pltpu.CompilerParams(vmem_limit_bytes=24 * 2**20),
        cost_estimate=pl.CostEstimate(flops=COST, bytes_accessed=COST, transcendentals=0),
        name=name,
    )(scal, *args)


def mix_kernel(n, x_ref, loc_ref, back_ref, att0, att1, wo0, wo1, *refs):
    count = len(refs) // 2
    out_ref = refs[count]
    for i in range(count):
        refs[count + 1 + i][...] = refs[i][...]
    rows = out_ref.shape[1]
    lo = n * rows
    mixed = dot(att0[...].reshape(2 * rows, -1), wo0[...]) + dot(att1[n].reshape(2 * rows, -1), wo1[...])
    x_f = x_ref[lo : lo + rows].astype(f32)
    for t, loc in enumerate((loc_ref, back_ref)):
        out_ref[t] = x_f + loc[lo : lo + rows].astype(f32) + mixed[t * rows : (t + 1) * rows]


def mix_call(n, x, loc, back, att, wo, copied=()):
    rows, width = att[0].shape[1], x.shape[1]
    return pl.pallas_call(
        functools.partial(mix_kernel, n),
        out_shape=[jax.ShapeDtypeStruct((2, rows, width), f32)] + [jax.ShapeDtypeStruct(a.shape, a.dtype) for a in copied],
        in_specs=[VMEM] * (7 + len(copied)),
        out_specs=[VMEM] * (1 + len(copied)),
        compiler_params=pltpu.CompilerParams(vmem_limit_bytes=24 * 2**20),
        cost_estimate=pl.CostEstimate(
            flops=8 * rows * width * wo[0].shape[0], bytes_accessed=8 * 2**20, transcendentals=0
        ),
        name="mix",
    )(x, loc, back, *att, *wo, *copied)


def mid_kernel(groups, scal, *refs):
    partial, gain_ref, w1_ref, w2_ref, *refs = refs
    even_out, odd_out, middle_out, summed, mixed = refs[-5:]
    refs = refs[:-5]
    att, wo = refs[: len(refs) // (1 + groups)], refs[len(refs) // (1 + groups) :]
    here_m, here_g = scal[0], scal[1]
    rows = partial.shape[1]
    half = partial.shape[2] // groups
    blocks = [a_ref[...].reshape(2 * rows, -1) for a_ref in att]
    for h in range(groups):
        columns = pl.ds(pl.multiple_of((h ^ here_g) * half, half), half)
        part = partial[:, :, columns].reshape(2 * rows, half)
        mixed[:, columns] = part + sum(dot(a, w[...]) for a, w in zip(blocks, wo[h * len(att) : (h + 1) * len(att)]))
    middle = mixed[...]
    normed = (unit(middle) * gain_ref[...]).astype(bf16)
    expanded = jax.nn.gelu(dot(normed, w1_ref[...]), approximate=True).astype(bf16)
    out = dot(expanded, w2_ref[...])
    out = out[:rows] + out[rows:]
    both = middle[:rows] + middle[rows:]
    mp, _, share = summed.shape
    for j in range(mp):
        summed[j] = out[:, j * share : (j + 1) * share].astype(bf16)
    for k in range(mp):
        (odd_out if k & 1 else even_out)[k >> 1] = summed[here_m ^ k]
    for j in range(mp):
        block = both[:, j * share : (j + 1) * share]

        @pl.when(here_m == j)
        def _():
            middle_out[...] = block


def mid_call(groups, mp, scal, partial, gain, w1, w2, att, wo):
    _, rows, width = partial.shape
    share = width // mp
    args = [partial, gain, w1, w2, *att, *wo]
    return pl.pallas_call(
        functools.partial(mid_kernel, groups),
        out_shape=[jax.ShapeDtypeStruct((mp // 2, rows, share), bf16)] * 2 + [jax.ShapeDtypeStruct((rows, share), f32)],
        in_specs=[SMEM] + [VMEM] * len(args),
        out_specs=[VMEM] * 3,
        scratch_shapes=[pltpu.VMEM((mp, rows, share), bf16), pltpu.VMEM((2 * rows, width), f32)],
        compiler_params=pltpu.CompilerParams(vmem_limit_bytes=24 * 2**20),
        cost_estimate=pl.CostEstimate(
            flops=4 * rows * width * (width // 2 + 2 * w1.shape[1]),
            bytes_accessed=14 * 2**20,
            transcendentals=2 * rows * w1.shape[1],
        ),
        name="middle",
    )(scal, *args)


def stack_kernel(*refs):
    for i, ref in enumerate(refs[:-1]):
        refs[-1][i] = ref[...]


def stack_call(arrays):
    shape = (len(arrays),) + arrays[0].shape
    return pl.pallas_call(
        stack_kernel,
        out_shape=jax.ShapeDtypeStruct(shape, arrays[0].dtype),
        in_specs=[VMEM] * len(arrays),
        out_specs=VMEM,
        compiler_params=pltpu.CompilerParams(vmem_limit_bytes=24 * 2**20),
        cost_estimate=pl.CostEstimate(flops=COST, bytes_accessed=COST, transcendentals=0),
        name="stack",
    )(*arrays)


def together(*arrays):
    return lax.optimization_barrier(arrays)


def shards(
    nucleotide_features,
    location_table,
    premix_rescaler,
    probe_lookup_matrices,
    payload_projector,
    logit_sharpness,
    mixing_projector,
    premlp_rescaler,
    widening_matrix,
    narrowing_matrix,
):
    rows, width = nucleotide_features.shape
    heads = logit_sharpness.shape[0]
    lookup = probe_lookup_matrices.shape[2] // heads
    value_size = payload_projector.shape[1] // heads
    padded = (value_size // 128 + 1) * 128
    groups, seq, mp = (lax.axis_size(name) for name in AXES)
    here_g, here_m = lax.axis_index("groups"), lax.axis_index("mp")
    nx = mp // 2
    part, half = rows // mp, width // groups
    dims = (groups, seq, mp, heads, lookup, value_size, padded)
    scal = jnp.stack([here_m, here_g]).astype(jnp.int32)
    x_own = nucleotide_features.reshape(mp, part, width)
    loc_own = location_table.reshape(mp, part, width)

    place = lax.broadcasted_iota(jnp.int32, (2 * part, 2 * part), 0) + lax.broadcasted_iota(jnp.int32, (2 * part, 2 * part), 1)
    flip = (place == 2 * part - 1).astype(bf16)
    gain = premix_rescaler.reshape(width, 1)
    wq, wk = [(gain * w.astype(f32)).astype(bf16) for w in (probe_lookup_matrices[0], probe_lookup_matrices[1])]
    wv = (gain * payload_projector.astype(f32)).astype(bf16)
    wv = jnp.pad(wv, ((0, 0), (0, -wv.shape[1] % 128)))

    have = {}

    def hold(array, names):
        have.update({name: (array, i) for i, name in enumerate(names)})

    def chunk(name, batches, last, loc_parts, q=(), numer=()):
        flip, wq, wk, wv = prepared
        weights = (wk, wv, wq) if batches[0][0][1] == 0 else (wk, wv)
        x_parts = {}
        for r, k in sorted({item[1:] for batch in batches for item in batch}):
            array, i = have[r, k]
            x_parts.setdefault(id(array), (array, {}))[1][r, k] = i
        return chunk_call(
            name, dims, batches, last, scal, list(x_parts.values()), loc_own, loc_parts,
            flip, logit_sharpness, weights, q, numer,
        )

    direct = range(3, seq, 2)
    loc_part = lax.dynamic_slice(location_table, (here_m * part, here_g * half), (part, half))
    loc_part, mix_first, x_first = together(loc_part, mixing_projector, x_own)
    mix_part = lax.dynamic_slice_in_dim(mix_first, here_g * half, half, 1)
    mix_x = [swap(mix_part, m=2 * kx) for kx in range(1, nx)]
    loc_z = [swap(loc_part, s=r) for r in range(1, seq)]
    x_mine = lax.dynamic_slice_in_dim(x_first, here_m, 1, 0)
    x_direct = [swap(x_mine, s=r) for r in direct]

    x_mine, flip, wq, wk, wv, loc_z = together(x_mine, flip, wq, wk, wv, loc_z)
    prepared = (flip, wq, wk, wv)
    loc_far = stack_call(loc_z)
    x_near = swap(x_mine, s=1)
    loc_xy = [loc_far] + [swap(loc_far, m=2 * kx) for kx in range(1, nx)]
    loc_y = [swap(loc_far, g=h) for h in range(1, groups)]
    x_direct, x_near, mix_x, loc_y = together(x_direct, x_near, mix_x, loc_y)
    loc_xy = loc_xy + [a for h in range(1, groups) for a in (loc_y[h - 1], *(swap(a, g=h) for a in loc_xy[1:]))]
    mix_far = [swap(a, g=h) if h else a for h in range(groups) for a in mix_x]
    x_relayed = [swap(a, s=1) for a in x_direct]
    x_across = [swap(a, m=2 * kx) for a in x_direct for kx in range(1, nx)]
    hold(x_own, [(0, k) for k in range(mp)])
    numer0, q0 = chunk("own_forward", [[(0, 0, k) for k in range(mp)]], False, [])

    x_near_across = [swap(x_near, m=2 * kx) for kx in range(1, nx)]
    numer0, loc_xy, *held = together(numer0, loc_xy, *x_relayed, x_near, *x_direct, *x_near_across)
    loc_even = stack_call(loc_xy)
    loc_odd = swap(loc_even, m=1)
    names = [[(r - 1, 0)] for r in direct] + [[(1, 0)]] + [[(r, 0)] for r in direct]
    names += [[(1, 2 * kx)] for kx in range(1, nx)]
    odd_names = lambda names: [(r, k + 1) for r, k in names]
    both = lambda names: [(t, r, k) for t in range(2) for r, k in names]
    apart = lambda names: [[(t, r, k) for r, k in names] for t in range(2)]
    hold(stack_call([a[0] for a in held]), [name for some in names for name in some])
    hold(swap(have[names[0][0]][0], m=1), odd_names([name for some in names for name in some]))
    early = [name for some in names for name in some]
    early = [early[i : i + 4] for i in range(0, len(early), 4)]
    x_late = [swap(a, m=2 * kx) for a in held[: len(direct)] for kx in range(1, nx)] + x_across
    late_names = [(r, 2 * kx) for r in [*(r - 1 for r in direct), *direct] for kx in range(1, nx)]
    loc_parts = [loc_even, loc_odd]
    numer1, q1, back = chunk("own_back", [[(1, 0, k) for k in range(mp)]], False, loc_parts)
    q, numer = [q0, q1], [numer0, numer1]
    for some in early:
        numer = chunk("first", [both(some), both(odd_names(some))], False, loc_parts, q, numer)
    numer, mix_far, *x_late = together(numer, mix_far, *x_late)
    x_late = stack_call([a[0] for a in x_late])
    hold(x_late, late_names)
    x_late_odd = swap(x_late, m=1)
    late = [late_names[i : i + 2] for i in range(0, len(late_names), 2)]
    for some in late:
        numer = chunk("second", apart(some), False, loc_parts, q, numer)
    numer, x_late_odd = together(numer, x_late_odd)
    hold(x_late_odd, odd_names(late_names))
    for some in late[:-1]:
        numer = chunk("third", [both(odd_names(some))], False, loc_parts, q, numer)
    a0, a1, blocks = chunk("last", apart(odd_names(late[-1])), True, loc_parts, q, numer)

    mixing, blocks = together(mixing_projector, blocks)
    wo_own = [mixing, swap(mixing, m=1)]
    w_mid = (premlp_rescaler.reshape(1, width), widening_matrix, narrowing_matrix)
    stream = (nucleotide_features, location_table, back.reshape(rows, width))

    def over_x(block):
        return [swap(block, m=2 * kx) for kx in range(1, nx)]

    def cores(blocks):
        return list(blocks) + [swap(a, m=1) for a in blocks]

    far0 = over_x(a0)
    blocks_odd = swap(blocks, m=1)
    (part0,) = mix_call(0, *stream, [a0, blocks_odd], wo_own)
    far1 = over_x(a1)
    part1, *copies = mix_call(1, *stream, [a1, blocks_odd], wo_own, mix_far[: nx - 1])
    part0, part1, mix_far = together(part0, part1, mix_far)
    wo_far = []
    for h in range(groups):
        some = mix_far[h * (nx - 1) : (h + 1) * (nx - 1)]
        wo_far += [*(some if h else copies), *(swap(a, m=1) for a in some)]
    part0, part1, *far0 = together(part0, part1, *far0)
    even0, odd0, share0 = mid_call(groups, mp, scal, part0, *w_mid, cores(far0), wo_far)
    even0, odd0, share0, *far1 = together(even0, odd0, share0, *far1)
    paired0 = even0.astype(f32) + swap(odd0, m=1).astype(f32)
    part1, paired0 = together(part1, paired0)
    across0 = [swap(paired0[kx].astype(bf16), m=2 * kx) for kx in range(1, nx)]
    even1, odd1, share1 = mid_call(groups, mp, scal, part1, *w_mid, cores(far1), wo_far)
    even1, odd1, share1, *across0 = together(even1, odd1, share1, *across0)
    paired1 = even1.astype(f32) + swap(odd1, m=1).astype(f32)
    across1 = [swap(paired1[kx].astype(bf16), m=2 * kx) for kx in range(1, nx)]
    blocks = [
        0.5 * (share + paired[0] + sum(a.astype(f32) for a in arrived))
        for share, paired, arrived in ((share0, paired0, across0), (share1, paired1, across1))
    ]
    return jnp.concatenate(blocks, axis=0)


def solution(mesh):
    return jax.shard_map(
        shards,
        mesh=mesh,
        in_specs=(
            P(("groups", "seq"), None),
            P("seq", None),
            P(),
            P(None, None, "mp"),
            P(None, "mp"),
            P("mp"),
            P("mp", None),
            P(),
            P(None, "mp"),
            P("mp", None),
        ),
        out_specs=P(("groups", "seq"), "mp"),
        check_vma=False,
    )
```
